512 devices in a mesh: row: 32 (over y, z_lo, core), col: 16 (over x, z_hi).
Axes of the slice: x: 4, y: 8, z: 8 (z_hi: 4, z_lo: 2; z = z_hi * 2 + z_lo), core: 2. Of those that a mesh axis runs over, the one named last changes fastest.
Arguments:
- pair_rep: bfloat16 [448, 448, 128], P('row', 'col'), may hold values from -6 to 6
- chain_lengths: int32 [4], replicated, may hold values from 1 to 112, 336 in all
- in_gain: float32 [2, 128], replicated, may hold values from 0.1 to 1.9
- in_bias: float32 [2, 128], replicated, may hold values from -3 to 3
- weight_in: bfloat16 [2, 128, 640], replicated, may hold values from -0.5 to 0.5
- out_gain: float32 [2, 128], replicated, may hold values from 0.1 to 1.9
- out_bias: float32 [2, 128], replicated, may hold values from -3 to 3
- weight_out: bfloat16 [2, 128, 128], replicated, may hold values from -0.5 to 0.5
Outputs:
- updated: bfloat16 [448, 448, 128], P('row', 'col')
The draws below stay inside these ranges and needn't reach their ends.
Inputs may be any that keep to these rules, and one draw needn't show every extreme that they name: Chain c occupies token positions c * 112 to (c + 1) * 112 - 1 of both pair dimensions; its first chain_lengths[c] positions are real, the rest padding; the lengths sum to 336.
All inputs are finite; a program needn't handle non-finite values.
Results may differ from the reference program's by a relative error of at most 0.012.
Values may be sent and summed in bfloat16 or wider, within the bound.
No kernel may reach another device: no remote copies, remote signals or barrier semaphores. Data moves between devices by JAX's collectives and lax.ppermute only.
A program may use at most 64 MiB of HBM per device.

```python
import math
import jax
import jax.numpy as jnp
import numpy as np
from jax import lax

C = 128
H = 128
CHAINS = 4
TOKENS = 448
SLOT = 112
VALID = 336


def levels(own_key, shape, shards, smallest, largest):
    loudness = 1.0
    for axis_at, parts in shards:
        draws = jax.random.uniform(jax.random.fold_in(jax.random.fold_in(own_key, 6), axis_at), (parts,), jnp.float32, smallest / len(shards), largest / len(shards))
        loudness = loudness * jnp.repeat(jnp.exp(draws), shape[axis_at] // parts).reshape((-1,) + (1,) * (len(shape) - 1 - axis_at))
    return loudness


def split_up(amount, total, reach, lean):
    loads = [(1 << 20) // math.isqrt(rank ** lean) + 1 for rank in range(2, amount + 1)]
    rest, given = total - reach - (amount - 1), [1] * (amount - 1)
    while rest > 0:
        movable = [i for i in range(amount - 1) if given[i] < reach]
        whole, remaining = sum([loads[i] for i in movable]), rest
        for i in movable:
            addition = min(reach - given[i], max(1, remaining * loads[i] // whole), rest)
            given[i] = given[i] + addition
            rest = rest - addition
    return np.array([reach] + given)


def uneven(key, amount, total, reach, slope):
    if amount == 2:
        one = jax.random.randint(key, (), max(1, total - reach), min(reach, total - 1) + 1)
        return jnp.stack([one, total - one])
    tallies = jnp.asarray(split_up(amount, total, reach, slope), jnp.int32)
    twos = (amount - 1) // 2
    source_of, receiver = tallies[1:1 + 2 * twos:2], tallies[2:2 + 2 * twos:2]
    margin = jnp.minimum(source_of - 1, reach - receiver)
    moved = jax.random.randint(jax.random.fold_in(key, 1), (twos,), 0, 1 << 20) % (margin + 1)
    tallies = tallies.at[1:1 + 2 * twos:2].set(source_of - moved).at[2:2 + 2 * twos:2].set(receiver + moved)
    return tallies[jax.random.permutation(jax.random.fold_in(key, 2), amount)]


def centred(rng, dims, deviation, bound, shards=(), held_as=jnp.bfloat16):
    array = jax.random.normal(rng, dims, jnp.float32) * deviation
    if len(shards) > 0:
        array = levels(rng, dims, shards, -0.22, 0.18) * array
    return jnp.clip(array, min=-bound, max=bound).astype(held_as)


def setup_inputs(seed: int = 0) -> dict:
    arg_keys = jax.random.split(jax.random.key(seed), 9)
    return {
        "pair_rep": centred(arg_keys[0], (TOKENS, TOKENS, C), 1.0, 6.0, ((0, 32), (1, 16))),
        "chain_lengths": uneven(arg_keys[1], CHAINS, VALID, SLOT, 1).astype(jnp.int32),
        "in_gain": jnp.clip(1.0 + 0.18 * jax.random.normal(arg_keys[2], (2, C), jnp.float32), 0.1, 1.9),
        "in_bias": centred(arg_keys[3], (2, C), 0.5, 3.0, (), jnp.float32),
        "weight_in": centred(arg_keys[4], (2, C, 4 * H + C), C ** -0.5, 0.5),
        "out_gain": jnp.clip(1.0 + 0.18 * jax.random.normal(arg_keys[5], (2, H), jnp.float32), 0.1, 1.9),
        "out_bias": centred(arg_keys[6], (2, H), 0.5, 3.0, (), jnp.float32),
        "weight_out": centred(arg_keys[7], (2, H, C), H ** -0.5, 0.5),
    }


EPSILON = 1e-05

def layer_norm(values, gain, bias):
    average = lax.optimization_barrier(jnp.mean(values, axis=-1, keepdims=True))
    centered = values - average
    variance = lax.optimization_barrier(jnp.mean(centered * centered, axis=-1, keepdims=True))
    return centered * lax.rsqrt(variance + EPSILON) * gain + bias

def token_valid(chain_lengths, token_count):
    chain_count = chain_lengths.shape[0]
    slot_size = token_count // chain_count
    position = jnp.arange(token_count, dtype=jnp.int32)
    chain_index = position // slot_size
    chain_ids = jnp.arange(chain_count, dtype=jnp.int32)
    limits = lax.optimization_barrier(jnp.sum(jnp.where(chain_index[:, None] == chain_ids[None, :], chain_lengths[None, :], 0), axis=1))
    return (position - chain_index * slot_size < limits).astype(jnp.float32)

def project_row(pair_row, mask_row, gain, bias, weight_in):
    channels = pair_row.shape[1]
    hidden = (weight_in.shape[1] - channels) // 4
    normed = layer_norm(pair_row.astype(jnp.float32), gain, bias).astype(jnp.bfloat16)
    projected = jnp.dot(normed, weight_in, preferred_element_type=jnp.float32)
    weighting = mask_row[:, None]
    left_proj = (weighting * jax.nn.sigmoid(projected[:, hidden:2 * hidden]) * projected[:, :hidden]).astype(jnp.bfloat16)
    right_proj = (weighting * jax.nn.sigmoid(projected[:, 3 * hidden:4 * hidden]) * projected[:, 2 * hidden:3 * hidden]).astype(jnp.bfloat16)
    gating = jax.nn.sigmoid(projected[:, 4 * hidden:])
    return (left_proj, right_proj, gating)

def project_pair(pair_rep, pair_mask, gain, bias, weight_in):

    def one_row(items):
        return project_row(items[0], items[1], gain, bias, weight_in)
    return lax.map(one_row, (pair_rep, pair_mask))

def finish_update(pair_rep, triangle, gating, gain, bias, weight_out):
    normed = layer_norm(triangle, gain, bias).astype(jnp.bfloat16)
    hidden = normed.shape[2]
    update = jnp.dot(normed.reshape(-1, hidden), weight_out, preferred_element_type=jnp.float32)
    update = update.reshape(pair_rep.shape)
    return (pair_rep.astype(jnp.float32) + gating * update).astype(jnp.bfloat16)

def reference(pair_rep, chain_lengths, in_gain, in_bias, weight_in, out_gain, out_bias, weight_out):
    token_count = pair_rep.shape[0]
    valid_mask = token_valid(chain_lengths, token_count)
    pair_mask = valid_mask[:, None] * valid_mask[None, :]
    left_proj, right_proj, gating = project_pair(pair_rep, pair_mask, in_gain[0], in_bias[0], weight_in[0])
    triangle = jnp.einsum('ikh,jkh->ijh', left_proj.astype(jnp.float32), right_proj.astype(jnp.float32), precision=lax.Precision.HIGHEST)
    middle = finish_update(pair_rep, triangle, gating, out_gain[0], out_bias[0], weight_out[0])
    left_proj, right_proj, gating = project_pair(middle, pair_mask, in_gain[1], in_bias[1], weight_in[1])
    triangle = jnp.einsum('kih,kjh->ijh', left_proj.astype(jnp.float32), right_proj.astype(jnp.float32), precision=lax.Precision.HIGHEST)
    return finish_update(middle, triangle, gating, out_gain[1], out_bias[1], weight_out[1])
```

```python
import jax
import jax.numpy as jnp
from jax import lax
from jax.experimental import pallas as pl
from jax.experimental.pallas import tpu as pltpu
from jax.sharding import Mesh, PartitionSpec as P

EPSILON = 1e-05
F32 = jnp.float32
BF16 = jnp.bfloat16

ROWS = 14
COLS = 28
WIDE = 32
CELLS = 512
GROUPS = 4
LANES = 128
SLOT = 112
CHAINS = 4

ROW_AXES = ("y", "zl", "core")
COL_AXES = ("x", "zh")
GROUP1 = ("x", "zh", "y")
GROUP2 = ("zh",) + ROW_AXES


def nt_dot(left, right):
    return lax.dot_general(left, right, (((1,), (1,)), ((), ())), preferred_element_type=F32)


def tn_dot(left, right):
    return lax.dot_general(left, right, (((0,), (0,)), ((), ())), preferred_element_type=F32)


def nn_dot(left, right):
    return jnp.dot(left, right, preferred_element_type=F32)


def norm_rows(values, gain, bias):
    average = jnp.mean(values, axis=0, keepdims=True)
    centered = values - average
    variance = jnp.mean(centered * centered, axis=0, keepdims=True)
    return (centered * lax.rsqrt(variance + EPSILON) * gain + bias).astype(BF16)


def one_hot(row_code, col_code):
    return (row_code == col_code).astype(F32).astype(BF16)


def swap_matrix():
    row = lax.broadcasted_iota(jnp.int32, (CELLS, 1), 0)
    col = lax.broadcasted_iota(jnp.int32, (1, CELLS), 1)
    swapped = ((col >> 5) & 3) * 128 + (col >> 7) * 32 + (col & 31)
    return one_hot(row, swapped)


def fields(code, *widths):
    out = []
    for width in reversed(widths):
        out.append(code & (width - 1))
        code = code >> (width.bit_length() - 1)
    return out[::-1]


def token_of_row(row, a, skip):
    return jnp.where(a < ROWS, row * ROWS + a, skip)


def token_of_col(x, zh, b, skip):
    return jnp.where(b < COLS, x * SLOT + zh * COLS + b, skip)


def valid_token(token, lengths_ref):
    valid = jnp.zeros(token.shape, jnp.bool_)
    for chain in range(CHAINS):
        start = chain * SLOT
        valid = valid | ((token >= start) & (token < start + lengths_ref[chain]))
    return valid


def cell_mask(place_ref, lengths_ref):
    lane = lax.broadcasted_iota(jnp.int32, (1, CELLS), 1)
    a, b = lane >> 5, lane & 31
    row = valid_token(place_ref[0] * ROWS + a, lengths_ref)
    col = valid_token(place_ref[1] * COLS + b, lengths_ref)
    inside = (a < ROWS) & (b < COLS)
    return jnp.where(row & col & inside, 1.0, 0.0).astype(F32)


def project(columns, mask, gain, bias, weight, send, send_ref, gate_ref):
    for m in range(GROUPS):
        lanes = slice(m * LANES, (m + 1) * LANES)
        normed = norm_rows(columns[:, lanes], gain, bias)
        projected = tn_dot(weight, normed)
        weighting = mask[:, lanes]
        left = weighting * jax.nn.sigmoid(projected[128:256]) * projected[0:128]
        right = weighting * jax.nn.sigmoid(projected[384:512]) * projected[256:384]
        send[pl.ds(m, 128, stride=8), :] = left
        send[pl.ds(4 + m, 128, stride=8), :] = right
        gate_ref[:, lanes] = jax.nn.sigmoid(projected[512:640])
    send_ref[...] = send[...].astype(BF16)


def turn_vectors(in_gain, in_bias, out_gain, out_bias):
    rows = jnp.concatenate([in_gain[...], in_bias[...], out_gain[...], out_bias[...]], axis=0)
    return rows.T


def first_kernel(
    place, lengths, pair, in_gain, in_bias, weight, out_gain, out_bias,
    send_ref, gate_ref, columns_ref, cells, send,
):
    vectors = turn_vectors(in_gain, in_bias, out_gain, out_bias)
    cells[...] = jnp.zeros_like(cells)
    for a in range(ROWS):
        cells[pl.ds(a * WIDE, COLS), :] = pair[a].astype(F32)
    columns = cells[...].T
    columns_ref[...] = columns
    mask = cell_mask(place, lengths)
    project(columns, mask, vectors[:, 0:1], vectors[:, 2:3], weight[0], send, send_ref, gate_ref)


def finish(back, update, gate, columns, vectors, weight_out, got):
    got[...] = back[...].astype(F32)
    parts = []
    for m in range(GROUPS):
        lanes = slice(m * LANES, (m + 1) * LANES)
        triangle = got[pl.ds(m, 128, stride=4), :]
        normed = norm_rows(triangle, vectors[:, 4 + update : 5 + update], vectors[:, 6 + update : 7 + update])
        change = tn_dot(weight_out, normed)
        parts.append(columns[:, lanes] + gate[:, lanes] * change)
    return jnp.concatenate(parts, axis=1).astype(BF16)


def middle_kernel(
    place, lengths, back, gate, columns, in_gain, in_bias, weight, out_gain, out_bias, weight_out,
    send_ref, gate_ref, columns_ref, got, send,
):
    vectors = turn_vectors(in_gain, in_bias, out_gain, out_bias)
    middle = finish(back, 0, gate, columns, vectors, weight_out[0], got).astype(F32)
    columns_ref[...] = middle
    mask = cell_mask(place, lengths)
    project(middle, mask, vectors[:, 1:2], vectors[:, 3:4], weight[1], send, send_ref, gate_ref)


def last_kernel(
    back, gate, columns, in_gain, in_bias, out_gain, out_bias, weight_out, out_ref, got, cells
):
    vectors = turn_vectors(in_gain, in_bias, out_gain, out_bias)
    updated = finish(back, 1, gate, columns, vectors, weight_out[1], got).astype(F32)
    cells[...] = updated.T
    for a in range(ROWS):
        out_ref[a] = cells[pl.ds(a * WIDE, COLS), :].astype(BF16)


def outgoing_kernel(mine, gathered, out_ref, mine_f, right_f, out_f):
    swap = swap_matrix()
    mine_f[...] = mine[...].astype(F32)
    right_f[...] = gathered[...].astype(F32)

    def matrix(source, base, stride):
        rows = []
        for m in range(GROUPS):
            for x in range(4):
                rows.append(jnp.concatenate([
                    source[pl.ds(base + (x * 4 + zh) * 8 * stride + m, 8, stride=stride), :] for zh in range(4)
                ], axis=1))
        turned = nn_dot(jnp.concatenate(rows, axis=0).astype(BF16), swap)
        rows = []
        for q in range(4):
            for m in range(GROUPS):
                rows.append(jnp.concatenate([
                    turned[(m * 4 + x) * 8 : (m * 4 + x) * 8 + 8, q * 128 : q * 128 + 128] for x in range(4)
                ], axis=1))
        return jnp.concatenate(rows, axis=0).astype(BF16)

    left = matrix(mine_f, 0, 8)
    right = jnp.concatenate([matrix(right_f, g * 512, 4) for g in range(4)], axis=0)
    triangle = nt_dot(left, right).astype(BF16)
    code = lax.broadcasted_iota(jnp.int32, (CELLS, 1), 0)
    g, q, m, y = fields(code, 4, 4, 4, 8)
    from_token = token_of_row(y * 4 + g, m * 4 + q, -1)
    code = lax.broadcasted_iota(jnp.int32, (1, CELLS), 1)
    x, zh, b = fields(code, 4, 4, 32)
    to_token = token_of_col(x, zh, b, -2)
    triangle = nn_dot(triangle, one_hot(from_token, to_token))
    rows = []
    for m in range(GROUPS):
        for x in range(4):
            rows.append(jnp.concatenate([
                triangle[(q * 4 + m) * 8 : (q * 4 + m) * 8 + 8, x * 128 : x * 128 + 128] for q in range(4)
            ], axis=1))
    turned = nn_dot(jnp.concatenate(rows, axis=0).astype(BF16), swap)
    for m in range(GROUPS):
        for x in range(4):
            for zh in range(4):
                out_f[pl.ds((x * 4 + zh) * 32 + m, 8, stride=4), :] = turned[
                    (m * 4 + x) * 8 : (m * 4 + x) * 8 + 8, zh * 128 : zh * 128 + 128
                ]
    out_ref[...] = out_f[...].astype(BF16)


def incoming_kernel(mine, gathered, out_ref, mine_f, left_f, out_f):
    swap = swap_matrix()
    mine_f[...] = mine[...].astype(F32)
    left_f[...] = gathered[...].astype(F32)

    def stacked(source, base, stride):
        return jnp.concatenate([
            jnp.concatenate([
                source[pl.ds(base + zh * 32 * stride + m, 32, stride=stride), :] for zh in range(4)
            ], axis=1)
            for m in range(GROUPS)
        ], axis=0).astype(BF16)

    def tall(source, base, stride):
        turned = nn_dot(stacked(source, base, stride), swap)
        return jnp.concatenate([turned[:, q * 128 : q * 128 + 128] for q in range(4)], axis=0).astype(BF16)

    turned = nt_dot(swap, stacked(mine_f, 4, 8))
    right = jnp.concatenate([turned[q * 128 : q * 128 + 128] for q in range(4)], axis=1).astype(BF16)
    left = jnp.concatenate([tall(left_f, x * 512, 4) for x in range(4)], axis=1)
    triangle = nn_dot(right, left).astype(BF16)
    code = lax.broadcasted_iota(jnp.int32, (CELLS, 1), 0)
    q, m, row = fields(code, 4, 4, 32)
    to_token = token_of_row(row, m * 4 + q, -1)
    code = lax.broadcasted_iota(jnp.int32, (1, CELLS), 1)
    x, zh, b = fields(code, 4, 4, 32)
    from_token = token_of_col(x, zh, b, -2)
    triangle = nt_dot(one_hot(to_token, from_token), triangle)
    wide = jnp.concatenate([triangle[q * 128 : q * 128 + 128] for q in range(4)], axis=1).astype(BF16)
    turned = nn_dot(wide, swap)
    for m in range(GROUPS):
        for zh in range(4):
            out_f[pl.ds(zh * 128 + m, 32, stride=4), :] = turned[m * 32 : m * 32 + 32, zh * 128 : zh * 128 + 128]
    out_ref[...] = out_f[...].astype(BF16)


def call(kernel, outs, scratch, name, scalars=0):
    specs = [pl.BlockSpec(memory_space=pltpu.SMEM)] * scalars

    def run(*args):
        return pl.pallas_call(
            kernel,
            out_shape=outs,
            in_specs=specs + [pl.BlockSpec(memory_space=pltpu.VMEM)] * (len(args) - scalars),
            out_specs=jax.tree.map(lambda _: pl.BlockSpec(memory_space=pltpu.VMEM), outs),
            scratch_shapes=[pltpu.VMEM(shape, F32) for shape in scratch],
            compiler_params=pltpu.CompilerParams(vmem_limit_bytes=32 * 1024 * 1024),
            name=name,
        )(*args)

    return run


def exchange(array, axes):
    return lax.all_to_all(array, axes, 0, 0, tiled=True)


def on_device(pair_rep, chain_lengths, in_gain, in_bias, weight_in, out_gain, out_bias, weight_out):
    place = jnp.stack([lax.axis_index(ROW_AXES), lax.axis_index(COL_AXES)]).astype(jnp.int32)
    tile = jax.ShapeDtypeStruct((LANES, CELLS), F32)
    sent = jax.ShapeDtypeStruct((1024, LANES), BF16)
    returned = jax.ShapeDtypeStruct((512, LANES), BF16)
    norms = (in_gain, in_bias)
    ends = (out_gain, out_bias)

    send, gate, columns = call(
        first_kernel, (sent, tile, tile), [(CELLS, LANES), (1024, LANES)], "first", 2
    )(place, chain_lengths, pair_rep, *norms, weight_in, *ends)
    mine = exchange(send.reshape(128, 8, LANES), GROUP1)
    gathered = lax.all_gather(mine[:, 4:], ("zl", "core"), axis=0, tiled=True)
    back = call(
        outgoing_kernel, returned, [(1024, LANES), (2048, LANES), (512, LANES)], "outgoing"
    )(mine.reshape(1024, LANES), gathered.reshape(2048, LANES))
    back = exchange(back.reshape(128, 4, LANES), GROUP1)

    send, gate, columns = call(
        middle_kernel, (sent, tile, tile), [(512, LANES), (1024, LANES)], "middle", 2
    )(place, chain_lengths, back.reshape(512, LANES), gate, columns, *norms, weight_in, *ends, weight_out)
    mine = exchange(send.reshape(128, 8, LANES), GROUP2)
    own = mine[:, :4].reshape(1, 512, LANES)
    gathered = exchange(jnp.broadcast_to(own, (4, 512, LANES)), "x")
    back = call(
        incoming_kernel, returned, [(1024, LANES), (2048, LANES), (512, LANES)], "incoming"
    )(mine.reshape(1024, LANES), gathered.reshape(2048, LANES))
    back = exchange(back.reshape(128, 4, LANES), GROUP2)

    out = jax.ShapeDtypeStruct(pair_rep.shape, BF16)
    return call(last_kernel, out, [(512, LANES), (CELLS, LANES)], "last")(
        back.reshape(512, LANES), gate, columns, *norms, *ends, weight_out
    )


def solution(mesh):
    fine = Mesh(mesh.devices.reshape(8, 2, 2, 4, 4), ROW_AXES + COL_AXES)
    placed = P(ROW_AXES, COL_AXES, None)
    return jax.shard_map(
        on_device, mesh=fine, in_specs=(placed,) + (P(),) * 7, out_specs=placed, check_vma=False
    )
```

```python
import jax
import jax.numpy as jnp
from jax import lax
from jax.experimental import pallas as pl
from jax.experimental.pallas import tpu as pltpu
from jax.sharding import Mesh, PartitionSpec as P

EPSILON = 1e-05
F32 = jnp.float32
BF16 = jnp.bfloat16

ROWS = 14
COLS = 28
WIDE = 32
CELLS = 512
GROUPS = 4
LANES = 128
SLOT = 112
CHAINS = 4

ROW_AXES = ("y", "zl", "core")
COL_AXES = ("x", "zh")
GROUP1 = ("x", "y", "zh")
GROUP2 = ("zl", "core", "zh", "y")


def nt_dot(left, right):
    return lax.dot_general(left, right, (((1,), (1,)), ((), ())), preferred_element_type=F32)


def tn_dot(left, right):
    return lax.dot_general(left, right, (((0,), (0,)), ((), ())), preferred_element_type=F32)


def nn_dot(left, right):
    return jnp.dot(left, right, preferred_element_type=F32)


def norm_rows(values, gain, bias):
    average = jnp.mean(values, axis=0, keepdims=True)
    centered = values - average
    variance = jnp.mean(centered * centered, axis=0, keepdims=True)
    return (centered * lax.rsqrt(variance + EPSILON) * gain + bias).astype(BF16)


def one_hot(row_code, col_code):
    return (row_code == col_code).astype(F32).astype(BF16)


def swap_matrix():
    row = lax.broadcasted_iota(jnp.int32, (CELLS, 1), 0)
    col = lax.broadcasted_iota(jnp.int32, (1, CELLS), 1)
    swapped = ((col >> 5) & 3) * 128 + (col >> 7) * 32 + (col & 31)
    return one_hot(row, swapped)


def fields(code, *widths):
    out = []
    for width in reversed(widths):
        out.append(code & (width - 1))
        code = code >> (width.bit_length() - 1)
    return out[::-1]


def token_of_row(row, a, skip):
    return jnp.where(a < ROWS, row * ROWS + a, skip)


def token_of_col(x, zh, b, skip):
    return jnp.where(b < COLS, x * SLOT + zh * COLS + b, skip)


def valid_token(token, lengths_ref):
    valid = jnp.zeros(token.shape, jnp.bool_)
    for chain in range(CHAINS):
        start = chain * SLOT
        valid = valid | ((token >= start) & (token < start + lengths_ref[chain]))
    return valid


def cell_mask(place_ref, lengths_ref):
    lane = lax.broadcasted_iota(jnp.int32, (1, CELLS), 1)
    a, b = lane >> 5, lane & 31
    row = valid_token(place_ref[0] * ROWS + a, lengths_ref)
    col = valid_token(place_ref[1] * COLS + b, lengths_ref)
    inside = (a < ROWS) & (b < COLS)
    return jnp.where(row & col & inside, 1.0, 0.0).astype(F32)


def project(columns, mask, gain, bias, weight, send, send_ref, gate_ref):
    for m in range(GROUPS):
        lanes = slice(m * LANES, (m + 1) * LANES)
        normed = norm_rows(columns[:, lanes], gain, bias)
        projected = tn_dot(weight, normed)
        weighting = mask[:, lanes]
        left = weighting * jax.nn.sigmoid(projected[128:256]) * projected[0:128]
        right = weighting * jax.nn.sigmoid(projected[384:512]) * projected[256:384]
        send[pl.ds(m, 128, stride=8), :] = left
        send[pl.ds(4 + m, 128, stride=8), :] = right
        gate_ref[:, lanes] = jax.nn.sigmoid(projected[512:640])
    send_ref[...] = send[...].astype(BF16)


def turn_vectors(in_gain, in_bias, out_gain, out_bias):
    rows = jnp.concatenate([in_gain[...], in_bias[...], out_gain[...], out_bias[...]], axis=0)
    return rows.T


def first_kernel(
    place, lengths_hbm, pair_hbm, gain_hbm, bias_hbm, weight_hbm,
    send_ref, gate_ref, columns_ref, cells, send, lengths, pair, gain, bias, weight, sems,
):
    copies = [
        pltpu.make_async_copy(source, target, sems.at[at])
        for at, (source, target) in enumerate((
            (pair_hbm, pair), (weight_hbm.at[0], weight), (gain_hbm, gain), (bias_hbm, bias), (lengths_hbm, lengths),
        ))
    ]
    for copy in copies:
        copy.start()
    cells[...] = jnp.zeros_like(cells)
    for copy in copies:
        copy.wait()
    mask = cell_mask(place, lengths)
    vectors = jnp.concatenate([gain[...], bias[...], gain[...], bias[...]], axis=0).T
    for a in range(ROWS):
        cells[pl.ds(a * WIDE, COLS), :] = pair[a].astype(F32)
    columns = cells[...].T
    columns_ref[...] = columns
    project(columns, mask, vectors[:, 0:1], vectors[:, 2:3], weight[...], send, send_ref, gate_ref)


def finish(back, update, gate, columns, vectors, weight_out, got):
    got[...] = back[...].astype(F32)
    parts = []
    for m in range(GROUPS):
        lanes = slice(m * LANES, (m + 1) * LANES)
        triangle = got[pl.ds(m, 128, stride=4), :]
        normed = norm_rows(triangle, vectors[:, 4 + update : 5 + update], vectors[:, 6 + update : 7 + update])
        change = tn_dot(weight_out, normed)
        parts.append(columns[:, lanes] + gate[:, lanes] * change)
    return jnp.concatenate(parts, axis=1).astype(BF16)


def middle_kernel(
    place, lengths, back, gate, columns, in_gain, in_bias, weight, out_gain, out_bias, weight_out,
    send_ref, gate_ref, columns_ref, got, send,
):
    vectors = turn_vectors(in_gain, in_bias, out_gain, out_bias)
    middle = finish(back, 0, gate, columns, vectors, weight_out[0], got).astype(F32)
    columns_ref[...] = middle
    mask = cell_mask(place, lengths)
    project(middle, mask, vectors[:, 1:2], vectors[:, 3:4], weight[1], send, send_ref, gate_ref)


def last_kernel(
    back, gate, columns, in_gain, in_bias, out_gain, out_bias, weight_out, out_ref, got, cells
):
    vectors = turn_vectors(in_gain, in_bias, out_gain, out_bias)
    updated = finish(back, 1, gate, columns, vectors, weight_out[1], got).astype(F32)
    cells[...] = updated.T
    for a in range(ROWS):
        out_ref[a] = cells[pl.ds(a * WIDE, COLS), :].astype(BF16)


def outgoing_kernel(mine, gathered, out_ref, mine_f, right_f, out_f):
    swap = swap_matrix()
    mine_f[...] = mine[...].astype(F32)
    right_f[...] = gathered[...].astype(F32)

    def matrix(source, base, stride):
        rows = []
        for m in range(GROUPS):
            for x in range(4):
                rows.append(jnp.concatenate([
                    source[pl.ds(base + (x * 32 + zh) * stride + m, 8, stride=4 * stride), :] for zh in range(4)
                ], axis=1))
        turned = nn_dot(jnp.concatenate(rows, axis=0).astype(BF16), swap)
        rows = []
        for q in range(4):
            for m in range(GROUPS):
                rows.append(jnp.concatenate([
                    turned[(m * 4 + x) * 8 : (m * 4 + x) * 8 + 8, q * 128 : q * 128 + 128] for x in range(4)
                ], axis=1))
        return jnp.concatenate(rows, axis=0).astype(BF16)

    left = matrix(mine_f, 0, 8)
    right = jnp.concatenate([matrix(right_f, g * 512, 4) for g in range(4)], axis=0)
    triangle = nt_dot(left, right).astype(BF16)
    code = lax.broadcasted_iota(jnp.int32, (CELLS, 1), 0)
    g, q, m, y = fields(code, 4, 4, 4, 8)
    from_token = token_of_row(y * 4 + g, m * 4 + q, -1)
    code = lax.broadcasted_iota(jnp.int32, (1, CELLS), 1)
    x, zh, b = fields(code, 4, 4, 32)
    to_token = token_of_col(x, zh, b, -2)
    triangle = nn_dot(triangle, one_hot(from_token, to_token))
    rows = []
    for m in range(GROUPS):
        for x in range(4):
            rows.append(jnp.concatenate([
                triangle[(q * 4 + m) * 8 : (q * 4 + m) * 8 + 8, x * 128 : x * 128 + 128] for q in range(4)
            ], axis=1))
    turned = nn_dot(jnp.concatenate(rows, axis=0).astype(BF16), swap)
    for m in range(GROUPS):
        for x in range(4):
            for zh in range(4):
                out_f[pl.ds((x * 32 + zh) * 4 + m, 8, stride=16), :] = turned[
                    (m * 4 + x) * 8 : (m * 4 + x) * 8 + 8, zh * 128 : zh * 128 + 128
                ]
    out_ref[...] = out_f[...].astype(BF16)


def incoming_kernel(mine, gathered, out_ref, mine_f, left_f, out_f):
    swap = swap_matrix()
    mine_f[...] = mine[...].astype(F32)
    left_f[...] = gathered[...].astype(F32)

    def stacked(source, base, stride):
        return jnp.concatenate([
            jnp.concatenate([
                source[pl.ds(base + (g * 32 + zh * 8) * stride + m, 8, stride=stride), :] for zh in range(4)
            ], axis=1)
            for m in range(GROUPS) for g in range(4)
        ], axis=0).astype(BF16)

    def tall(source, base, stride):
        turned = nn_dot(stacked(source, base, stride), swap)
        return jnp.concatenate([turned[:, q * 128 : q * 128 + 128] for q in range(4)], axis=0).astype(BF16)

    turned = nt_dot(swap, stacked(mine_f, 4, 8))
    right = jnp.concatenate([turned[q * 128 : q * 128 + 128] for q in range(4)], axis=1).astype(BF16)
    left = jnp.concatenate([tall(left_f, x * 512, 4) for x in range(4)], axis=1)
    triangle = nn_dot(right, left).astype(BF16)
    code = lax.broadcasted_iota(jnp.int32, (CELLS, 1), 0)
    q, m, g, y = fields(code, 4, 4, 4, 8)
    to_token = token_of_row(y * 4 + g, m * 4 + q, -1)
    code = lax.broadcasted_iota(jnp.int32, (1, CELLS), 1)
    x, zh, b = fields(code, 4, 4, 32)
    from_token = token_of_col(x, zh, b, -2)
    triangle = nt_dot(one_hot(to_token, from_token), triangle)
    wide = jnp.concatenate([triangle[q * 128 : q * 128 + 128] for q in range(4)], axis=1).astype(BF16)
    turned = nn_dot(wide, swap)
    for m in range(GROUPS):
        for g in range(4):
            for zh in range(4):
                out_f[pl.ds((g * 32 + zh * 8) * 4 + m, 8, stride=4), :] = turned[
                    (m * 4 + g) * 8 : (m * 4 + g) * 8 + 8, zh * 128 : zh * 128 + 128
                ]
    out_ref[...] = out_f[...].astype(BF16)


def call(kernel, outs, scratch, name, scalars=0, space=pltpu.VMEM, more=()):
    specs = [pl.BlockSpec(memory_space=pltpu.SMEM)] * scalars

    def run(*args):
        return pl.pallas_call(
            kernel,
            out_shape=outs,
            in_specs=specs + [pl.BlockSpec(memory_space=space)] * (len(args) - scalars),
            out_specs=jax.tree.map(lambda _: pl.BlockSpec(memory_space=pltpu.VMEM), outs),
            scratch_shapes=[pltpu.VMEM(shape, F32) for shape in scratch] + list(more),
            compiler_params=pltpu.CompilerParams(vmem_limit_bytes=32 * 1024 * 1024),
            name=name,
        )(*args)

    return run


def in_hbm(array):
    return pltpu.with_memory_space_constraint(array, pltpu.HBM)


def exchange(array, axes):
    return lax.all_to_all(array, axes, 0, 0, tiled=True)


def on_device(pair_rep, chain_lengths, in_gain, in_bias, weight_in, out_gain, out_bias, weight_out):
    place = jnp.stack([lax.axis_index(ROW_AXES), lax.axis_index(COL_AXES)]).astype(jnp.int32)
    tile = jax.ShapeDtypeStruct((LANES, CELLS), F32)
    sent = jax.ShapeDtypeStruct((1024, LANES), BF16)
    returned = jax.ShapeDtypeStruct((512, LANES), BF16)
    norms = (in_gain, in_bias)
    ends = (out_gain, out_bias)

    send, gate, columns = call(
        first_kernel, (sent, tile, tile), [(CELLS, LANES), (1024, LANES)], "first", 1, pltpu.HBM,
        [
            pltpu.SMEM(chain_lengths.shape, jnp.int32),
            pltpu.VMEM(pair_rep.shape, BF16), pltpu.VMEM(in_gain.shape, F32), pltpu.VMEM(in_bias.shape, F32),
            pltpu.VMEM(weight_in.shape[1:], BF16), pltpu.SemaphoreType.DMA((5,)),
        ],
    )(place, *(in_hbm(array) for array in (chain_lengths, pair_rep, *norms, weight_in)))
    mine = exchange(send.reshape(128, 8, LANES), GROUP1)
    gathered = lax.all_gather(mine[:, 4:], ("zl", "core"), axis=0, tiled=True)
    back = call(
        outgoing_kernel, returned, [(1024, LANES), (2048, LANES), (512, LANES)], "outgoing"
    )(mine.reshape(1024, LANES), gathered.reshape(2048, LANES))
    back = exchange(back.reshape(128, 4, LANES), GROUP1)

    send, gate, columns = call(
        middle_kernel, (sent, tile, tile), [(512, LANES), (1024, LANES)], "middle", 2
    )(place, chain_lengths, back.reshape(512, LANES), gate, columns, *norms, weight_in, *ends, weight_out)
    mine = exchange(send.reshape(128, 8, LANES), GROUP2)
    own = mine[:, :4].reshape(1, 512, LANES)
    gathered = exchange(jnp.broadcast_to(own, (4, 512, LANES)), "x")
    back = call(
        incoming_kernel, returned, [(1024, LANES), (2048, LANES), (512, LANES)], "incoming"
    )(mine.reshape(1024, LANES), gathered.reshape(2048, LANES))
    back = exchange(back.reshape(128, 4, LANES), GROUP2)

    out = jax.ShapeDtypeStruct(pair_rep.shape, BF16)
    return call(last_kernel, out, [(512, LANES), (CELLS, LANES)], "last")(
        back.reshape(512, LANES), gate, columns, *norms, *ends, weight_out
    )


def solution(mesh):
    fine = Mesh(mesh.devices.reshape(8, 2, 2, 4, 4), ROW_AXES + COL_AXES)
    placed = P(ROW_AXES, COL_AXES, None)
    return jax.shard_map(
        on_device, mesh=fine, in_specs=(placed,) + (P(),) * 7, out_specs=placed, check_vma=False
    )
```

```python
import jax
import jax.numpy as jnp
from jax import lax
from jax.experimental import pallas as pl
from jax.experimental.pallas import tpu as pltpu
from jax.sharding import Mesh, PartitionSpec as P

EPSILON = 1e-05
F32 = jnp.float32
BF16 = jnp.bfloat16

ROWS = 14
COLS = 28
WIDE = 32
CELLS = 512
GROUPS = 4
LANES = 128
SLOT = 112
CHAINS = 4

ROW_AXES = ("y", "zl", "core")
COL_AXES = ("xh", "xl", "zh")
GROUP1 = ("zl", "xl", "zh", "y")
GROUP2 = ("xh", "xl", "zh", "y")
BACK = ("zl", "zh", "y", "xh", "xl")


def nt_dot(left, right):
    return lax.dot_general(left, right, (((1,), (1,)), ((), ())), preferred_element_type=F32)


def tn_dot(left, right):
    return lax.dot_general(left, right, (((0,), (0,)), ((), ())), preferred_element_type=F32)


def nn_dot(left, right):
    return jnp.dot(left, right, preferred_element_type=F32)


def norm_rows(values, gain, bias):
    average = jnp.mean(values, axis=0, keepdims=True)
    centered = values - average
    variance = jnp.mean(centered * centered, axis=0, keepdims=True)
    return (centered * lax.rsqrt(variance + EPSILON) * gain + bias).astype(BF16)


def one_hot(row_code, col_code):
    return (row_code == col_code).astype(F32).astype(BF16)


def swap_matrix():
    row = lax.broadcasted_iota(jnp.int32, (CELLS, 1), 0)
    col = lax.broadcasted_iota(jnp.int32, (1, CELLS), 1)
    swapped = ((col >> 5) & 3) * 128 + (col >> 7) * 32 + (col & 31)
    return one_hot(row, swapped)


def fields(code, *widths):
    out = []
    for width in reversed(widths):
        out.append(code & (width - 1))
        code = code >> (width.bit_length() - 1)
    return out[::-1]


def token_of_row(row, a, skip):
    return jnp.where(a < ROWS, row * ROWS + a, skip)


def token_of_col(x, zh, b, skip):
    return jnp.where(b < COLS, x * SLOT + zh * COLS + b, skip)


def valid_token(token, lengths_ref):
    valid = jnp.zeros(token.shape, jnp.bool_)
    for chain in range(CHAINS):
        start = chain * SLOT
        valid = valid | ((token >= start) & (token < start + lengths_ref[chain]))
    return valid


def cell_mask(place_ref, lengths_ref):
    lane = lax.broadcasted_iota(jnp.int32, (1, CELLS), 1)
    a, b = lane >> 5, lane & 31
    row = valid_token(place_ref[0] * ROWS + a, lengths_ref)
    col = valid_token(place_ref[1] * COLS + b, lengths_ref)
    inside = (a < ROWS) & (b < COLS)
    return jnp.where(row & col & inside, 1.0, 0.0).astype(F32)


def project(columns, mask, gain, bias, weight, send, send_ref, gate_ref):
    for m in range(GROUPS):
        lanes = slice(m * LANES, (m + 1) * LANES)
        normed = norm_rows(columns[:, lanes], gain, bias)
        projected = tn_dot(weight, normed)
        weighting = mask[:, lanes]
        left = weighting * jax.nn.sigmoid(projected[128:256]) * projected[0:128]
        right = weighting * jax.nn.sigmoid(projected[384:512]) * projected[256:384]
        send[pl.ds(m, 128, stride=8), :] = left
        send[pl.ds(4 + m, 128, stride=8), :] = right
        gate_ref[:, lanes] = jax.nn.sigmoid(projected[512:640])
    send_ref[...] = send[...].astype(BF16)


def first_kernel(
    place, lengths_hbm, pair_hbm, in_gain_hbm, in_bias_hbm, weight_hbm, out_gain_hbm, out_bias_hbm,
    send_ref, gate_ref, columns_ref, vectors_ref, cells, send, norms, lengths, pair, in_gain, in_bias, out_gain, out_bias, weight, sems,
):
    copies = [
        pltpu.make_async_copy(source, target, sems.at[at])
        for at, (source, target) in enumerate((
            (pair_hbm, pair), (weight_hbm.at[0], weight), (in_gain_hbm, in_gain), (in_bias_hbm, in_bias),
            (out_gain_hbm, out_gain), (out_bias_hbm, out_bias), (lengths_hbm, lengths),
        ))
    ]
    for copy in copies:
        copy.start()
    cells[...] = jnp.zeros_like(cells)
    norms[...] = jnp.zeros_like(norms)
    for copy in copies:
        copy.wait()
    mask = cell_mask(place, lengths)
    for at, pair_of in enumerate((in_gain, in_bias, out_gain, out_bias)):
        norms[pl.ds(2 * at, 2), :] = pair_of[...]
    vectors = norms[...].T
    vectors_ref[...] = vectors
    for a in range(ROWS):
        cells[pl.ds(a * WIDE, COLS), :] = pair[a].astype(F32)
    columns = cells[...].T
    columns_ref[...] = columns
    project(columns, mask, vectors[:, 0:1], vectors[:, 2:3], weight[...], send, send_ref, gate_ref)


def finish(home, source_rows, gain, bias, gate, columns, weight_out, got):
    got[...] = home[...].astype(F32)
    parts = []
    for m in range(GROUPS):
        lanes = slice(m * LANES, (m + 1) * LANES)
        triangle = source_rows(got, 0, m) + source_rows(got, 1, m)
        change = tn_dot(weight_out, norm_rows(triangle, gain, bias))
        parts.append(columns[:, lanes] + gate[:, lanes] * change)
    return jnp.concatenate(parts, axis=1).astype(BF16)


def rows_after_first(got, xh, m):
    return jnp.concatenate([
        got[pl.ds(zl * 512 + xh * 8 + xl * 4 + m, 32, stride=16), :] for zl in range(2) for xl in range(2)
    ], axis=0)


def rows_after_second(got, zl, m):
    return jnp.concatenate([got[pl.ds(zl * 512 + x * 4 + m, 32, stride=16), :] for x in range(4)], axis=0)


def middle_kernel(
    place, lengths, home, gate, columns, vectors, weight, weight_out, send_ref, gate_ref, columns_ref, got, send
):
    middle = finish(
        home, rows_after_first, vectors[:, 4:5], vectors[:, 6:7], gate, columns, weight_out[0], got
    ).astype(F32)
    columns_ref[...] = middle
    mask = cell_mask(place, lengths)
    project(middle, mask, vectors[:, 1:2], vectors[:, 3:4], weight[1], send, send_ref, gate_ref)


def last_kernel(home, gate, columns, vectors, weight_out, out_ref, got, cells):
    updated = finish(
        home, rows_after_second, vectors[:, 5:6], vectors[:, 7:8], gate, columns, weight_out[1], got
    ).astype(F32)
    cells[...] = updated.T
    for a in range(ROWS):
        out_ref[a] = cells[pl.ds(a * WIDE, COLS), :].astype(BF16)


def group_lanes(rows, swap):
    return nn_dot(jnp.concatenate(rows, axis=0).astype(BF16), swap)


def send_home(triangle, swap, out_ref, out_f):
    rows = []
    for m in range(GROUPS):
        for zl in range(2):
            for x in range(4):
                rows.append(jnp.concatenate([
                    triangle[((q * 4 + m) * 2 + zl) * 8 : ((q * 4 + m) * 2 + zl) * 8 + 8, x * 128 : x * 128 + 128]
                    for q in range(4)
                ], axis=1))
    turned = group_lanes(rows, swap)
    for m in range(GROUPS):
        for zl in range(2):
            for x in range(4):
                at = ((m * 2 + zl) * 4 + x) * 8
                for zh in range(4):
                    out_f[pl.ds((zl * 4 + zh) * 128 + x * 4 + m, 8, stride=16), :] = turned[
                        at : at + 8, zh * 128 : zh * 128 + 128
                    ]
    out_ref[...] = out_f[...].astype(BF16)


def outgoing_kernel(mine, both, out_ref, mine_f, both_f, out_f):
    swap = swap_matrix()
    mine_f[...] = mine[...].astype(F32)
    both_f[...] = both[...].astype(F32)

    def matrix(source, base):
        turned = group_lanes([
            jnp.concatenate([
                source[pl.ds(base + ((zl * 2 + xl) * 4 + zh) * 64 + m, 8, stride=8), :] for zh in range(4)
            ], axis=1)
            for m in range(GROUPS) for zl in range(2) for xl in range(2)
        ], swap)
        rows = []
        for q in range(4):
            for m in range(GROUPS):
                for zl in range(2):
                    rows.append(jnp.concatenate([
                        turned[((m * 2 + zl) * 2 + xl) * 8 : ((m * 2 + zl) * 2 + xl) * 8 + 8, q * 128 : q * 128 + 128]
                        for xl in range(2)
                    ], axis=1))
        return jnp.concatenate(rows, axis=0).astype(BF16)

    left = matrix(mine_f, 0)
    right = jnp.concatenate([matrix(both_f, core * 1024 + 4) for core in range(2)], axis=0)
    triangle = nt_dot(left, right).astype(BF16)
    code = lax.broadcasted_iota(jnp.int32, (CELLS, 1), 0)
    core, q, m, zl, y = fields(code, 2, 4, 4, 2, 8)
    from_token = token_of_row(y * 4 + zl * 2 + core, m * 4 + q, -1)
    code = lax.broadcasted_iota(jnp.int32, (1, CELLS), 1)
    x, zh, b = fields(code, 4, 4, 32)
    to_token = token_of_col(x, zh, b, -2)
    send_home(nn_dot(triangle, one_hot(from_token, to_token)), swap, out_ref, out_f)


def incoming_kernel(place, both, out_ref, both_f, out_f):
    swap = swap_matrix()
    both_f[...] = both[...].astype(F32)

    def matrix(base):
        turned = group_lanes([
            jnp.concatenate([
                both_f[pl.ds(base + core * 1024 + (x * 4 + zh) * 64 + m, 8, stride=8), :] for zh in range(4)
            ], axis=1)
            for m in range(GROUPS) for core in range(2) for x in range(4)
        ], swap)
        rows = []
        for q in range(4):
            for m in range(GROUPS):
                for core in range(2):
                    rows.append(jnp.concatenate([
                        turned[((m * 2 + core) * 4 + x) * 8 : ((m * 2 + core) * 4 + x) * 8 + 8, q * 128 : q * 128 + 128]
                        for x in range(4)
                    ], axis=1))
        return jnp.concatenate(rows, axis=0).astype(BF16)

    code = lax.broadcasted_iota(jnp.int32, (CELLS // 2, 1), 0)
    q, m, zl, y = fields(code, 4, 4, 2, 8)
    to_token = token_of_row(y * 4 + zl * 2 + (place[0] & 1), m * 4 + q, -1)
    code = lax.broadcasted_iota(jnp.int32, (1, CELLS), 1)
    x, zh, b = fields(code, 4, 4, 32)
    from_token = token_of_col(x, zh, b, -2)
    left = nt_dot(one_hot(to_token, from_token), matrix(0)).astype(BF16)
    send_home(nn_dot(left, matrix(4)).astype(BF16).astype(F32), swap, out_ref, out_f)


def call(kernel, outs, scratch, name, scalars=0, space=pltpu.VMEM, more=()):
    specs = [pl.BlockSpec(memory_space=pltpu.SMEM)] * scalars

    def run(*args):
        return pl.pallas_call(
            kernel,
            out_shape=outs,
            in_specs=specs + [pl.BlockSpec(memory_space=space)] * (len(args) - scalars),
            out_specs=jax.tree.map(lambda _: pl.BlockSpec(memory_space=pltpu.VMEM), outs),
            scratch_shapes=[pltpu.VMEM(shape, F32) for shape in scratch] + list(more),
            compiler_params=pltpu.CompilerParams(vmem_limit_bytes=32 * 1024 * 1024),
            name=name,
        )(*args)

    return run


def in_hbm(array):
    return pltpu.with_memory_space_constraint(array, pltpu.HBM)


def exchange(array, axes):
    return lax.all_to_all(array, axes, 0, 0, tiled=True)


def on_device(pair_rep, chain_lengths, in_gain, in_bias, weight_in, out_gain, out_bias, weight_out):
    place = jnp.stack([lax.axis_index(ROW_AXES), lax.axis_index(COL_AXES)]).astype(jnp.int32)
    tile = jax.ShapeDtypeStruct((LANES, CELLS), F32)
    sent = jax.ShapeDtypeStruct((1024, LANES), BF16)

    send, gate, columns, vectors = call(
        first_kernel, (sent, tile, tile, jax.ShapeDtypeStruct((LANES, 8), F32)),
        [(CELLS, LANES), (1024, LANES), (8, LANES)], "first", 1, pltpu.HBM,
        [
            pltpu.SMEM(chain_lengths.shape, jnp.int32), pltpu.VMEM(pair_rep.shape, BF16),
            pltpu.VMEM(in_gain.shape, F32), pltpu.VMEM(in_bias.shape, F32),
            pltpu.VMEM(out_gain.shape, F32), pltpu.VMEM(out_bias.shape, F32),
            pltpu.VMEM(weight_in.shape[1:], BF16), pltpu.SemaphoreType.DMA((7,)),
        ],
    )(place, *map(in_hbm, (chain_lengths, pair_rep, in_gain, in_bias, weight_in, out_gain, out_bias)))
    mine = exchange(send.reshape(128, 8, LANES), GROUP1).reshape(1024, LANES)
    both = lax.all_gather(mine, "core", axis=0, tiled=True)
    home = call(
        outgoing_kernel, sent, [(1024, LANES), (2048, LANES), (1024, LANES)], "outgoing"
    )(mine, both)
    home = exchange(home.reshape(256, 4, LANES), BACK).reshape(1024, LANES)

    send, gate, columns = call(
        middle_kernel, (sent, tile, tile), [(1024, LANES), (1024, LANES)], "middle", 2
    )(place, chain_lengths, home, gate, columns, vectors, weight_in, weight_out)
    mine = exchange(send.reshape(128, 8, LANES), GROUP2).reshape(1024, LANES)
    both = lax.all_gather(mine, "core", axis=0, tiled=True)
    home = call(
        incoming_kernel, sent, [(2048, LANES), (1024, LANES)], "incoming", 1
    )(place, both)
    home = exchange(home.reshape(256, 4, LANES), BACK).reshape(1024, LANES)

    out = jax.ShapeDtypeStruct(pair_rep.shape, BF16)
    return call(last_kernel, out, [(1024, LANES), (CELLS, LANES)], "last")(home, gate, columns, vectors, weight_out)


def solution(mesh):
    fine = Mesh(mesh.devices.reshape(8, 2, 2, 2, 2, 4), ROW_AXES + COL_AXES)
    placed = P(ROW_AXES, COL_AXES, None)
    return jax.shard_map(
        on_device, mesh=fine, in_specs=(placed,) + (P(),) * 7, out_specs=placed, check_vma=False
    )
```

```python
import jax
import jax.numpy as jnp
from jax import lax
from jax.experimental import pallas as pl
from jax.experimental.pallas import tpu as pltpu
from jax.sharding import Mesh, PartitionSpec as P

EPSILON = 1e-05
F32 = jnp.float32
BF16 = jnp.bfloat16

ROWS = 14
COLS = 28
WIDE = 32
CELLS = 512
GROUPS = 4
LANES = 128
SLOT = 112
CHAINS = 4

ROW_AXES = ("y", "zl", "core")
COL_AXES = ("xh", "xl", "zh")
GROUP1 = ("zl", "xl", "zh", "y")
GROUP2 = ("xh", "xl", "zh", "y")
BACK = ("zl", "zh", "y", "xh", "xl")


def nt_dot(left, right):
    return lax.dot_general(left, right, (((1,), (1,)), ((), ())), preferred_element_type=F32)


def tn_dot(left, right):
    return lax.dot_general(left, right, (((0,), (0,)), ((), ())), preferred_element_type=F32)


def nn_dot(left, right):
    return jnp.dot(left, right, preferred_element_type=F32)


def norm_rows(values, gain, bias):
    average = jnp.mean(values, axis=0, keepdims=True)
    centered = values - average
    variance = jnp.mean(centered * centered, axis=0, keepdims=True)
    return (centered * lax.rsqrt(variance + EPSILON) * gain + bias).astype(BF16)


def swap_groups(tiles):
    group = lax.broadcasted_iota(jnp.int32, tiles[0].shape, 1) >> 5
    for bit in (1, 2):
        keep = (group & bit) == 0
        out = list(tiles)
        for p in range(4):
            if p & bit == 0:
                low, high = tiles[p], tiles[p + bit]
                out[p] = jnp.where(keep, low, pltpu.roll(high, 32 * bit, 1))
                out[p + bit] = jnp.where(keep, pltpu.roll(low, LANES - 32 * bit, 1), high)
        tiles = out
    return tiles


def token_matrix(cores):
    code = lax.broadcasted_iota(jnp.int32, (8, CELLS), 1)
    b = code & 31
    token = jnp.where(b < COLS, (code >> 5) * COLS + b, -4096)
    token = token - 4 * ROWS * lax.broadcasted_iota(jnp.int32, (8, CELLS), 0)
    none = jnp.zeros((8, CELLS), F32)
    rows = []
    for core in cores:
        for q in range(4):
            for m in range(GROUPS):
                for zl in range(2):
                    a = 4 * m + q
                    first = (zl * 2 + core) * ROWS + a
                    rows.append(jnp.where(token == first, 1.0, 0.0).astype(F32) if a < ROWS else none)
    return jnp.concatenate(rows, axis=0).astype(BF16)


def fields(code, *widths):
    out = []
    for width in reversed(widths):
        out.append(code & (width - 1))
        code = code >> (width.bit_length() - 1)
    return out[::-1]


def own_matrix(core):
    q, m, zl, y = fields(lax.broadcasted_iota(jnp.int32, (8, CELLS // 2), 1), 4, 4, 2, 8)
    a = 4 * m + q
    sub = lax.broadcasted_iota(jnp.int32, (8, CELLS // 2), 0)
    token = jnp.where(a < ROWS, ((y * 2 + zl) * 2 + core) * ROWS + a, -4096) - sub
    last = jnp.where(sub < COLS - 24, token, -4096)
    return jnp.concatenate([
        jnp.where((last if b == 24 else token) == c * COLS + b, 1.0, 0.0).astype(F32)
        for c in range(16) for b in range(0, WIDE, 8)
    ], axis=0).astype(BF16)


def valid_token(token, lengths_ref):
    valid = jnp.zeros(token.shape, jnp.bool_)
    for chain in range(CHAINS):
        start = chain * SLOT
        valid = valid | ((token >= start) & (token < start + lengths_ref[chain]))
    return valid


def cell_mask(place, lengths_ref):
    lane = lax.broadcasted_iota(jnp.int32, (1, CELLS), 1)
    a, b = lane >> 5, lane & 31
    row = valid_token(place[0:1, 0:1] * ROWS + a, lengths_ref)
    col = valid_token(place[8:9, 0:1] * COLS + b, lengths_ref)
    inside = (a < ROWS) & (b < COLS)
    return jnp.where(row & col & inside, 1.0, 0.0).astype(F32)


def project(columns, mask, gain, bias, weight, send, send_ref, gate_ref):
    for m in range(GROUPS):
        lanes = slice(m * LANES, (m + 1) * LANES)
        normed = norm_rows(columns[:, lanes], gain, bias)
        projected = tn_dot(weight, normed)
        weighting = mask[:, lanes]
        left = weighting * jax.nn.sigmoid(projected[128:256]) * projected[0:128]
        right = weighting * jax.nn.sigmoid(projected[384:512]) * projected[256:384]
        send[pl.ds(m, 128, stride=8), :] = left
        send[pl.ds(4 + m, 128, stride=8), :] = right
        gate_ref[:, lanes] = jax.nn.sigmoid(projected[512:640])
    send_ref[...] = send[...].astype(BF16)


def first_kernel(
    place, lengths_hbm, pair_hbm, in_gain_hbm, in_bias_hbm, weight_hbm, out_gain_hbm, out_bias_hbm,
    send_ref, gate_ref, columns_ref, vectors_ref, mask_ref, cells, send, norms, lengths, pair, in_gain, in_bias, out_gain, out_bias, weight, sems,
):
    copies = [
        pltpu.make_async_copy(source, target, sems.at[at])
        for at, (source, target) in enumerate((
            (pair_hbm, pair), (weight_hbm.at[0], weight), (in_gain_hbm, in_gain), (in_bias_hbm, in_bias),
            (out_gain_hbm, out_gain), (out_bias_hbm, out_bias), (lengths_hbm, lengths),
        ))
    ]
    for copy in copies:
        copy.start()
    cells[...] = jnp.zeros_like(cells)
    norms[...] = jnp.zeros_like(norms)
    for copy in copies:
        copy.wait()
    mask = cell_mask(place, lengths)
    mask_ref[...] = mask
    for at, pair_of in enumerate((in_gain, in_bias, out_gain, out_bias)):
        norms[pl.ds(2 * at, 2), :] = pair_of[...]
    vectors = norms[...].T
    vectors_ref[...] = vectors
    for a in range(ROWS):
        cells[pl.ds(a * WIDE, COLS), :] = pair[a].astype(F32)
    columns = cells[...].T
    columns_ref[...] = columns
    project(columns, mask, vectors[:, 0:1], vectors[:, 2:3], weight[...], send, send_ref, gate_ref)


def finish(home, source_rows, gain, bias, gate, columns, weight_out, got):
    got[...] = home[...].astype(F32)
    parts = []
    for m in range(GROUPS):
        lanes = slice(m * LANES, (m + 1) * LANES)
        triangle = source_rows(got, 0, m) + source_rows(got, 1, m)
        change = tn_dot(weight_out, norm_rows(triangle, gain, bias))
        parts.append(columns[:, lanes] + gate[:, lanes] * change)
    return jnp.concatenate(parts, axis=1).astype(BF16)


def rows_after_first(got, xh, m):
    return jnp.concatenate([
        got[pl.ds(zl * 512 + xh * 8 + xl * 4 + m, 32, stride=16), :] for zl in range(2) for xl in range(2)
    ], axis=0)


def rows_after_second(got, zl, m):
    return jnp.concatenate([got[pl.ds(zl * 512 + x * 4 + m, 32, stride=16), :] for x in range(4)], axis=0)


def middle_kernel(
    home, gate, columns, vectors, mask, weight, weight_out, send_ref, gate_ref, columns_ref, got, send
):
    middle = finish(
        home, rows_after_first, vectors[:, 4:5], vectors[:, 6:7], gate, columns, weight_out[0], got
    ).astype(F32)
    columns_ref[...] = middle
    project(middle, mask, vectors[:, 1:2], vectors[:, 3:4], weight[1], send, send_ref, gate_ref)


def last_kernel(home, gate, columns, vectors, weight_out, out_ref, got, cells):
    updated = finish(
        home, rows_after_second, vectors[:, 5:6], vectors[:, 7:8], gate, columns, weight_out[1], got
    ).astype(F32)
    cells[...] = updated.T
    for a in range(ROWS):
        out_ref[a] = cells[pl.ds(a * WIDE, COLS), :].astype(BF16)


def stack(pieces):
    return jnp.concatenate(list(pieces), axis=0)


def send_home(triangle, out_ref, out_f):
    tiles = swap_groups([
        stack(
            triangle[((q * 4 + m) * 2 + zl) * 8 : ((q * 4 + m) * 2 + zl) * 8 + 8, x * 128 : x * 128 + 128]
            for m in range(GROUPS) for zl in range(2) for x in range(4)
        )
        for q in range(4)
    ])
    for m in range(GROUPS):
        for zl in range(2):
            for x in range(4):
                at = ((m * 2 + zl) * 4 + x) * 8
                for zh in range(4):
                    out_f[pl.ds((zl * 4 + zh) * 128 + x * 4 + m, 8, stride=16), :] = tiles[zh][at : at + 8]
    out_ref[...] = out_f[...].astype(BF16)


def outgoing_kernel(mine, both, out_ref, mine_f, both_f, out_f):
    mine_f[...] = mine[...].astype(F32)
    both_f[...] = both[...].astype(F32)

    def matrix(source, base):
        tiles = swap_groups([
            stack(
                source[pl.ds(base + ((zl * 2 + xl) * 4 + zh) * 64 + m, 8, stride=8), :]
                for xl in range(2) for m in range(GROUPS) for zl in range(2)
            )
            for zh in range(4)
        ])
        half = tiles[0].shape[0] // 2
        return stack(jnp.concatenate([tile[:half], tile[half:]], axis=1) for tile in tiles).astype(BF16)

    left = matrix(mine_f, 0)
    right = stack(matrix(both_f, core * 1024 + 4) for core in range(2))
    triangle = nt_dot(left, right).astype(BF16)
    send_home(nn_dot(triangle, token_matrix(range(2))), out_ref, out_f)


def incoming_kernel(place, both, out_ref, both_f, out_f):
    both_f[...] = both[...].astype(F32)

    def matrix(base):
        tiles = swap_groups([
            stack(
                both_f[pl.ds(base + core * 1024 + (x * 4 + zh) * 64 + m, 8, stride=8), :]
                for x in range(4) for m in range(GROUPS) for core in range(2)
            )
            for zh in range(4)
        ])
        return stack(
            jnp.concatenate([tile[x * 64 : x * 64 + 64] for x in range(4)], axis=1) for tile in tiles
        ).astype(BF16)

    left = nn_dot(matrix(0), own_matrix(place[0:1, 0:1] & 1)).astype(BF16)
    send_home(tn_dot(left, matrix(4)), out_ref, out_f)


def call(kernel, outs, scratch, name, held=()):
    def run(*args):
        return pl.pallas_call(
            kernel,
            out_shape=outs,
            in_specs=[pl.BlockSpec(memory_space=pltpu.HBM if at in held else pltpu.VMEM) for at in range(len(args))],
            out_specs=jax.tree.map(lambda _: pl.BlockSpec(memory_space=pltpu.VMEM), outs),
            scratch_shapes=[pltpu.VMEM(entry, F32) if isinstance(entry, tuple) else entry for entry in scratch],
            compiler_params=pltpu.CompilerParams(vmem_limit_bytes=32 * 1024 * 1024),
            name=name,
        )(*args)

    return run


def in_hbm(array):
    return pltpu.with_memory_space_constraint(array, pltpu.HBM)


def exchange(array, axes):
    return lax.all_to_all(array, axes, 0, 0, tiled=True)


def on_device(pair_rep, chain_lengths, in_gain, in_bias, weight_in, out_gain, out_bias, weight_out):
    place = jnp.concatenate([
        jnp.full((8, LANES), lax.axis_index(axes), jnp.int32) for axes in (ROW_AXES, COL_AXES)
    ])
    tile = jax.ShapeDtypeStruct((LANES, CELLS), F32)
    sent = jax.ShapeDtypeStruct((1024, LANES), BF16)

    small = (jax.ShapeDtypeStruct((LANES, 8), F32), jax.ShapeDtypeStruct((1, CELLS), F32))
    send, gate, columns, vectors, mask = call(
        first_kernel, (sent, tile, tile) + small, [
            (CELLS, LANES), (1024, LANES), (8, LANES), pltpu.SMEM(chain_lengths.shape, jnp.int32),
            pltpu.VMEM(pair_rep.shape, BF16), in_gain.shape, in_bias.shape, out_gain.shape, out_bias.shape,
            pltpu.VMEM(weight_in.shape[1:], BF16), pltpu.SemaphoreType.DMA((7,)),
        ], "first", range(1, 8),
    )(place, *map(in_hbm, (chain_lengths, pair_rep, in_gain, in_bias, weight_in, out_gain, out_bias)))
    mine = exchange(send.reshape(128, 8, LANES), GROUP1).reshape(1024, LANES)
    both = lax.all_gather(mine, "core", axis=0, tiled=True)
    home = call(
        outgoing_kernel, sent, [(1024, LANES), (2048, LANES), (1024, LANES)], "outgoing"
    )(mine, both)
    home = exchange(home.reshape(256, 4, LANES), BACK).reshape(1024, LANES)

    send, gate, columns = call(
        middle_kernel, (sent, tile, tile), [(1024, LANES), (1024, LANES)], "middle"
    )(home, gate, columns, vectors, mask, weight_in, weight_out)
    mine = exchange(send.reshape(128, 8, LANES), GROUP2).reshape(1024, LANES)
    both = lax.all_gather(mine, "core", axis=0, tiled=True)
    home = call(
        incoming_kernel, sent, [(2048, LANES), (1024, LANES)], "incoming"
    )(place, both)
    home = exchange(home.reshape(256, 4, LANES), BACK).reshape(1024, LANES)

    out = jax.ShapeDtypeStruct(pair_rep.shape, BF16)
    return call(last_kernel, out, [(1024, LANES), (CELLS, LANES)], "last")(home, gate, columns, vectors, weight_out)


def solution(mesh):
    fine = Mesh(mesh.devices.reshape(8, 2, 2, 2, 2, 4), ROW_AXES + COL_AXES)
    placed = P(ROW_AXES, COL_AXES, None)
    return jax.shard_map(
        on_device, mesh=fine, in_specs=(placed,) + (P(),) * 7, out_specs=placed, check_vma=False
    )
```

```python
import jax
import jax.numpy as jnp
from jax import lax
from jax.experimental import pallas as pl
from jax.experimental.pallas import tpu as pltpu
from jax.sharding import Mesh, PartitionSpec as P

EPSILON = 1e-05
F32 = jnp.float32
BF16 = jnp.bfloat16

ROWS = 14
COLS = 28
WIDE = 32
CELLS = 512
GROUPS = 4
LANES = 128
SLOT = 112
CHAINS = 4

ROW_AXES = ("yh", "yl", "zl", "core")
COL_AXES = ("xh", "xl", "zh")
GROUP1 = ("xl", "zh", "yh", "yl", "zl")
GROUP2 = ("zh", "xh", "xl", "yl", "zl")
BACK = ("zh", "yh", "yl", "zl", "xh", "xl")


def nt_dot(left, right):
    return lax.dot_general(left, right, (((1,), (1,)), ((), ())), preferred_element_type=F32)


def tn_dot(left, right):
    return lax.dot_general(left, right, (((0,), (0,)), ((), ())), preferred_element_type=F32)


def nn_dot(left, right):
    return jnp.dot(left, right, preferred_element_type=F32)


def stack(pieces):
    return jnp.concatenate(list(pieces), axis=0)


def norm_rows(values, gain, bias):
    average = jnp.mean(values, axis=0, keepdims=True)
    centered = values - average
    variance = jnp.mean(centered * centered, axis=0, keepdims=True)
    return (centered * lax.rsqrt(variance + EPSILON) * gain + bias).astype(BF16)


def swap_groups(tiles):
    group = lax.broadcasted_iota(jnp.int32, tiles[0].shape, 1) >> 5
    for bit in (1, 2):
        keep = (group & bit) == 0
        out = list(tiles)
        for p in range(4):
            if p & bit == 0:
                low, high = tiles[p], tiles[p + bit]
                out[p] = jnp.where(keep, low, pltpu.roll(high, 32 * bit, 1))
                out[p + bit] = jnp.where(keep, pltpu.roll(low, LANES - 32 * bit, 1), high)
        tiles = out
    return tiles


def token_matrix():
    code = lax.broadcasted_iota(jnp.int32, (8, CELLS), 1)
    token = jnp.where(code & 31 < COLS, (code >> 5) * COLS + (code & 31), -4096)
    token = token - COLS * lax.broadcasted_iota(jnp.int32, (8, CELLS), 0)
    none = jnp.zeros((8, CELLS), F32)
    rows = []
    for core in range(2):
        for q in range(4):
            for m in range(GROUPS):
                for yh in range(2):
                    a = 4 * m + q
                    first = yh * 8 * COLS + core * ROWS + a
                    rows.append(jnp.where(token == first, 1.0, 0.0).astype(F32) if a < ROWS else none)
    return jnp.concatenate(rows, axis=0).astype(BF16)


def fields(code, *widths):
    out = []
    for width in reversed(widths):
        out.append(code & (width - 1))
        code = code >> (width.bit_length() - 1)
    return out[::-1]


def own_matrix(core):
    q, m, yh, s = fields(lax.broadcasted_iota(jnp.int32, (8, CELLS // 2), 1), 4, 4, 2, 8)
    a = 4 * m + q
    sub = lax.broadcasted_iota(jnp.int32, (8, CELLS // 2), 0)
    token = jnp.where(a < ROWS, ((yh * 8 + s) * 2 + core) * ROWS + a, -4096) - sub
    last = jnp.where(sub < COLS - 24, token, -4096)
    return jnp.concatenate([
        jnp.where((last if b == 24 else token) == c * COLS + b, 1.0, 0.0).astype(F32)
        for c in range(16) for b in range(0, WIDE, 8)
    ], axis=0).astype(BF16)


def valid_token(token, lengths_ref):
    valid = jnp.zeros(token.shape, jnp.bool_)
    for chain in range(CHAINS):
        start = chain * SLOT
        valid = valid | ((token >= start) & (token < start + lengths_ref[chain]))
    return valid


def cell_mask(place, lengths_ref):
    lane = lax.broadcasted_iota(jnp.int32, (1, CELLS), 1)
    a, b = lane >> 5, lane & 31
    row = valid_token(place[0:1, 0:1] * ROWS + a, lengths_ref)
    col = valid_token(place[8:9, 0:1] * COLS + b, lengths_ref)
    inside = (a < ROWS) & (b < COLS)
    return jnp.where(row & col & inside, 1.0, 0.0).astype(F32)


def project(columns, mask, gain, bias, weight, send, send_ref, gate_ref):
    for m in range(GROUPS):
        lanes = slice(m * LANES, (m + 1) * LANES)
        normed = norm_rows(columns[:, lanes], gain, bias)
        projected = tn_dot(weight, normed)
        weighting = mask[:, lanes]
        left = weighting * jax.nn.sigmoid(projected[128:256]) * projected[0:128]
        right = weighting * jax.nn.sigmoid(projected[384:512]) * projected[256:384]
        send[pl.ds(m, 128, stride=8), :] = left
        send[pl.ds(4 + m, 128, stride=8), :] = right
        gate_ref[:, lanes] = jax.nn.sigmoid(projected[512:640])
    send_ref[...] = send[...].astype(BF16)


def first_kernel(
    place, lengths_hbm, pair_hbm, in_gain_hbm, in_bias_hbm, weight_hbm, out_gain_hbm, out_bias_hbm,
    send_ref, gate_ref, columns_ref, vectors_ref, mask_ref, cells, send, norms, lengths, pair, in_gain, in_bias, out_gain, out_bias, weight, sems,
):
    copies = [
        pltpu.make_async_copy(source, target, sems.at[at])
        for at, (source, target) in enumerate((
            (pair_hbm, pair), (weight_hbm.at[0], weight), (in_gain_hbm, in_gain), (in_bias_hbm, in_bias),
            (out_gain_hbm, out_gain), (out_bias_hbm, out_bias), (lengths_hbm, lengths),
        ))
    ]
    for copy in copies:
        copy.start()
    cells[...] = jnp.zeros_like(cells)
    norms[...] = jnp.zeros_like(norms)
    for copy in copies:
        copy.wait()
    mask = cell_mask(place, lengths)
    mask_ref[...] = mask
    for at, pair_of in enumerate((in_gain, in_bias, out_gain, out_bias)):
        norms[pl.ds(2 * at, 2), :] = pair_of[...]
    vectors = norms[...].T
    vectors_ref[...] = vectors
    for a in range(ROWS):
        cells[pl.ds(a * WIDE, COLS), :] = pair[a].astype(F32)
    columns = cells[...].T
    columns_ref[...] = columns
    project(columns, mask, vectors[:, 0:1], vectors[:, 2:3], weight[...], send, send_ref, gate_ref)


def finish(home, source_rows, gain, bias, gate, columns, weight_out, got):
    got[...] = home[...].astype(F32)
    parts = []
    for m in range(GROUPS):
        lanes = slice(m * LANES, (m + 1) * LANES)
        triangle = source_rows(got, 0, m) + source_rows(got, 1, m)
        change = tn_dot(weight_out, norm_rows(triangle, gain, bias))
        parts.append(columns[:, lanes] + gate[:, lanes] * change)
    return jnp.concatenate(parts, axis=1).astype(BF16)


def rows_after_first(got, xh, m):
    return stack(got[pl.ds(xh * 8 + xl * 4 + m, 64, stride=16), :] for xl in range(2))


def rows_after_second(got, yh, m):
    return stack(
        got[pl.ds((zh * 2 + yh) * 128 + x * 4 + m, 8, stride=16), :] for zh in range(4) for x in range(4)
    )


def middle_kernel(
    home, gate, columns, vectors, mask, weight, weight_out, send_ref, gate_ref, columns_ref, got, send
):
    middle = finish(
        home, rows_after_first, vectors[:, 4:5], vectors[:, 6:7], gate, columns, weight_out[0], got
    ).astype(F32)
    columns_ref[...] = middle
    project(middle, mask, vectors[:, 1:2], vectors[:, 3:4], weight[1], send, send_ref, gate_ref)


def last_kernel(home, gate, columns, vectors, weight_out, out_ref, got, cells):
    updated = finish(
        home, rows_after_second, vectors[:, 5:6], vectors[:, 7:8], gate, columns, weight_out[1], got
    ).astype(F32)
    cells[...] = updated.T
    for a in range(ROWS):
        out_ref[a] = cells[pl.ds(a * WIDE, COLS), :].astype(BF16)


def send_home(triangle, out_ref, out_f):
    tiles = swap_groups([
        stack(
            triangle[((q * 4 + m) * 2 + yh) * 8 : ((q * 4 + m) * 2 + yh) * 8 + 8, x * 128 : x * 128 + 128]
            for m in range(GROUPS) for yh in range(2) for x in range(4)
        )
        for q in range(4)
    ])
    for m in range(GROUPS):
        for yh in range(2):
            for x in range(4):
                at = ((m * 2 + yh) * 4 + x) * 8
                for zh in range(4):
                    out_f[pl.ds((zh * 2 + yh) * 128 + x * 4 + m, 8, stride=16), :] = tiles[zh][at : at + 8]
    out_ref[...] = out_f[...].astype(BF16)


def outgoing_kernel(mine, both, out_ref, mine_f, both_f, out_f):
    mine_f[...] = mine[...].astype(F32)
    both_f[...] = both[...].astype(F32)

    def matrix(source, base):
        tiles = swap_groups([
            stack(
                source[pl.ds(base + ((xl * 4 + zh) * 2 + yh) * 64 + m, 8, stride=8), :]
                for xl in range(2) for m in range(GROUPS) for yh in range(2)
            )
            for zh in range(4)
        ])
        half = tiles[0].shape[0] // 2
        return stack(jnp.concatenate([tile[:half], tile[half:]], axis=1) for tile in tiles).astype(BF16)

    left = matrix(mine_f, 0)
    right = stack(matrix(both_f, core * 1024 + 4) for core in range(2))
    triangle = nt_dot(left, right).astype(BF16)
    send_home(nn_dot(triangle, token_matrix()), out_ref, out_f)


def incoming_kernel(place, both, out_ref, both_f, out_f):
    both_f[...] = both[...].astype(F32)

    def matrix(base):
        tiles = swap_groups([
            stack(
                both_f[pl.ds(base + core * 1024 + (zh * 4 + x) * 64 + m, 8, stride=8), :]
                for x in range(4) for m in range(GROUPS) for core in range(2)
            )
            for zh in range(4)
        ])
        return stack(
            jnp.concatenate([tile[x * 64 : x * 64 + 64] for x in range(4)], axis=1) for tile in tiles
        ).astype(BF16)

    left = nn_dot(matrix(0), own_matrix(place[0:1, 0:1] & 1)).astype(BF16)
    send_home(tn_dot(left, matrix(4)), out_ref, out_f)


def call(kernel, outs, scratch, name, held=()):
    def run(*args):
        return pl.pallas_call(
            kernel,
            out_shape=outs,
            in_specs=[pl.BlockSpec(memory_space=pltpu.HBM if at in held else pltpu.VMEM) for at in range(len(args))],
            out_specs=jax.tree.map(lambda _: pl.BlockSpec(memory_space=pltpu.VMEM), outs),
            scratch_shapes=[pltpu.VMEM(entry, F32) if isinstance(entry, tuple) else entry for entry in scratch],
            compiler_params=pltpu.CompilerParams(vmem_limit_bytes=32 * 1024 * 1024),
            name=name,
        )(*args)

    return run


def in_hbm(array):
    return pltpu.with_memory_space_constraint(array, pltpu.HBM)


def exchange(array, axes):
    return lax.all_to_all(array, axes, 0, 0, tiled=True)


def on_device(pair_rep, chain_lengths, in_gain, in_bias, weight_in, out_gain, out_bias, weight_out):
    place = jnp.concatenate([
        jnp.full((8, LANES), lax.axis_index(axes), jnp.int32) for axes in (ROW_AXES, COL_AXES)
    ])
    tile = jax.ShapeDtypeStruct((LANES, CELLS), F32)
    sent = jax.ShapeDtypeStruct((1024, LANES), BF16)

    small = (jax.ShapeDtypeStruct((LANES, 8), F32), jax.ShapeDtypeStruct((1, CELLS), F32))
    send, gate, columns, vectors, mask = call(
        first_kernel, (sent, tile, tile) + small, [
            (CELLS, LANES), (1024, LANES), (8, LANES), pltpu.SMEM(chain_lengths.shape, jnp.int32),
            pltpu.VMEM(pair_rep.shape, BF16), in_gain.shape, in_bias.shape, out_gain.shape, out_bias.shape,
            pltpu.VMEM(weight_in.shape[1:], BF16), pltpu.SemaphoreType.DMA((7,)),
        ], "first", range(1, 8),
    )(place, *map(in_hbm, (chain_lengths, pair_rep, in_gain, in_bias, weight_in, out_gain, out_bias)))
    mine = exchange(send.reshape(128, 8, LANES), GROUP1).reshape(1024, LANES)
    both = lax.all_gather(mine, "core", axis=0, tiled=True)
    home = call(
        outgoing_kernel, sent, [(1024, LANES), (2048, LANES), (1024, LANES)], "outgoing"
    )(mine, both)
    home = exchange(home.reshape(256, 4, LANES), BACK).reshape(1024, LANES)

    send, gate, columns = call(
        middle_kernel, (sent, tile, tile), [(1024, LANES), (1024, LANES)], "middle"
    )(home, gate, columns, vectors, mask, weight_in, weight_out)
    mine = exchange(send.reshape(128, 8, LANES), GROUP2).reshape(1024, LANES)
    both = lax.all_gather(mine, "core", axis=0, tiled=True)
    home = call(
        incoming_kernel, sent, [(2048, LANES), (1024, LANES)], "incoming"
    )(place, both)
    home = exchange(home.reshape(256, 4, LANES), BACK).reshape(1024, LANES)

    out = jax.ShapeDtypeStruct(pair_rep.shape, BF16)
    return call(last_kernel, out, [(1024, LANES), (CELLS, LANES)], "last")(home, gate, columns, vectors, weight_out)


def solution(mesh):
    fine = Mesh(mesh.devices.reshape(2, 4, 2, 2, 2, 2, 4), ROW_AXES + COL_AXES)
    placed = P(ROW_AXES, COL_AXES, None)
    return jax.shard_map(
        on_device, mesh=fine, in_specs=(placed,) + (P(),) * 7, out_specs=placed, check_vma=False
    )
```

```python
import jax
import jax.numpy as jnp
from jax import lax
from jax.experimental import pallas as pl
from jax.experimental.pallas import tpu as pltpu
from jax.sharding import Mesh, PartitionSpec as P

EPSILON = 1e-05
F32 = jnp.float32
BF16 = jnp.bfloat16

ROWS = 14
COLS = 28
WIDE = 32
CELLS = 512
GROUPS = 4
LANES = 128
SLOT = 112
CHAINS = 4

ROW_AXES = ("yh", "yl", "zl", "core")
COL_AXES = ("xh", "xl", "zh")
GROUP1 = ("zh", "xl", "yh", "yl", "zl")
GROUP2 = ("zh", "xh", "xl", "yl", "zl")
BACK = ("zh", "yh", "yl", "zl", "xh", "xl")


def nt_dot(left, right):
    return lax.dot_general(left, right, (((1,), (1,)), ((), ())), preferred_element_type=F32)


def tn_dot(left, right):
    return lax.dot_general(left, right, (((0,), (0,)), ((), ())), preferred_element_type=F32)


def nn_dot(left, right):
    return jnp.dot(left, right, preferred_element_type=F32)


def stack(pieces):
    return jnp.concatenate(list(pieces), axis=0)


def norm_rows(values, gain, bias):
    average = jnp.mean(values, axis=0, keepdims=True)
    centered = values - average
    variance = jnp.mean(centered * centered, axis=0, keepdims=True)
    return (centered * lax.rsqrt(variance + EPSILON) * gain + bias).astype(BF16)


def swap_groups(tiles):
    group = lax.broadcasted_iota(jnp.int32, tiles[0].shape, 1) >> 5
    for bit in (1, 2):
        keep = (group & bit) == 0
        out = list(tiles)
        for p in range(4):
            if p & bit == 0:
                low, high = tiles[p], tiles[p + bit]
                out[p] = jnp.where(keep, low, pltpu.roll(high, 32 * bit, 1))
                out[p + bit] = jnp.where(keep, pltpu.roll(low, LANES - 32 * bit, 1), high)
        tiles = out
    return tiles


def token_matrix():
    code = lax.broadcasted_iota(jnp.int32, (8, CELLS), 1)
    token = jnp.where(code & 31 < COLS, (code >> 5) * COLS + (code & 31), -4096)
    token = token - COLS * lax.broadcasted_iota(jnp.int32, (8, CELLS), 0)
    none = jnp.zeros((8, CELLS), F32)
    rows = []
    for core in range(2):
        for q in range(4):
            for m in range(GROUPS):
                for yh in range(2):
                    a = 4 * m + q
                    first = yh * 8 * COLS + core * ROWS + a
                    rows.append(jnp.where(token == first, 1.0, 0.0).astype(F32) if a < ROWS else none)
    return jnp.concatenate(rows, axis=0).astype(BF16)


def fields(code, *widths):
    out = []
    for width in reversed(widths):
        out.append(code & (width - 1))
        code = code >> (width.bit_length() - 1)
    return out[::-1]


def own_matrix(core):
    q, m, yh, s = fields(lax.broadcasted_iota(jnp.int32, (8, CELLS // 2), 1), 4, 4, 2, 8)
    a = 4 * m + q
    sub = lax.broadcasted_iota(jnp.int32, (8, CELLS // 2), 0)
    token = jnp.where(a < ROWS, ((yh * 8 + s) * 2 + core) * ROWS + a, -4096) - sub
    last = jnp.where(sub < COLS - 24, token, -4096)
    return jnp.concatenate([
        jnp.where((last if b == 24 else token) == c * COLS + b, 1.0, 0.0).astype(F32)
        for c in range(16) for b in range(0, WIDE, 8)
    ], axis=0).astype(BF16)


def valid_token(token, lengths_ref):
    valid = jnp.zeros(token.shape, jnp.bool_)
    for chain in range(CHAINS):
        start = chain * SLOT
        valid = valid | ((token >= start) & (token < start + lengths_ref[chain]))
    return valid


def cell_mask(place, lengths_ref):
    lane = lax.broadcasted_iota(jnp.int32, (1, CELLS), 1)
    a, b = lane >> 5, lane & 31
    row = valid_token(place[0:1, 0:1] * ROWS + a, lengths_ref)
    col = valid_token(place[8:9, 0:1] * COLS + b, lengths_ref)
    inside = (a < ROWS) & (b < COLS)
    return jnp.where(row & col & inside, 1.0, 0.0).astype(F32)


def project(columns, mask, gain, bias, weight, send, send_ref, gate_ref):
    for m in range(GROUPS):
        lanes = slice(m * LANES, (m + 1) * LANES)
        normed = norm_rows(columns[:, lanes], gain, bias)
        projected = tn_dot(weight, normed)
        weighting = mask[:, lanes]
        left = weighting * jax.nn.sigmoid(projected[128:256]) * projected[0:128]
        right = weighting * jax.nn.sigmoid(projected[384:512]) * projected[256:384]
        send[pl.ds(m, 128, stride=8), :] = left
        send[pl.ds(4 + m, 128, stride=8), :] = right
        gate_ref[:, lanes] = jax.nn.sigmoid(projected[512:640])
    send_ref[...] = send[...].astype(BF16)


def first_kernel(
    place, lengths_hbm, pair_hbm, in_gain_hbm, in_bias_hbm, weight_hbm, out_gain_hbm, out_bias_hbm,
    send_ref, gate_ref, columns_ref, vectors_ref, mask_ref, cells, send, norms, lengths, pair, in_gain, in_bias, out_gain, out_bias, weight, sems,
):
    copies = [
        pltpu.make_async_copy(source, target, sems.at[at])
        for at, (source, target) in enumerate((
            (pair_hbm, pair), (weight_hbm.at[0], weight), (in_gain_hbm, in_gain), (in_bias_hbm, in_bias),
            (out_gain_hbm, out_gain), (out_bias_hbm, out_bias), (lengths_hbm, lengths),
        ))
    ]
    for copy in copies:
        copy.start()
    cells[...] = jnp.zeros_like(cells)
    norms[...] = jnp.zeros_like(norms)
    for copy in copies:
        copy.wait()
    mask = cell_mask(place, lengths)
    mask_ref[...] = mask
    for at, pair_of in enumerate((in_gain, in_bias, out_gain, out_bias)):
        norms[pl.ds(2 * at, 2), :] = pair_of[...]
    vectors = norms[...].T
    vectors_ref[...] = vectors
    for a in range(ROWS):
        cells[pl.ds(a * WIDE, COLS), :] = pair[a].astype(F32)
    columns = cells[...].T
    columns_ref[...] = columns
    project(columns, mask, vectors[:, 0:1], vectors[:, 2:3], weight[...], send, send_ref, gate_ref)


def finish(home, source_rows, gain, bias, gate, columns, weight_out, got):
    got[...] = home[...].astype(F32)
    parts = []
    for m in range(GROUPS):
        lanes = slice(m * LANES, (m + 1) * LANES)
        triangle = source_rows(got, 0, m) + source_rows(got, 1, m)
        change = tn_dot(weight_out, norm_rows(triangle, gain, bias))
        parts.append(columns[:, lanes] + gate[:, lanes] * change)
    return jnp.concatenate(parts, axis=1).astype(BF16)


def rows_after_first(got, xh, m):
    return stack(
        got[pl.ds(zh * 256 + xh * 8 + xl * 4 + m, 16, stride=16), :] for zh in range(4) for xl in range(2)
    )


def rows_after_second(got, yh, m):
    return stack(
        got[pl.ds((zh * 2 + yh) * 128 + x * 4 + m, 8, stride=16), :] for zh in range(4) for x in range(4)
    )


def middle_kernel(
    home, gate, columns, vectors, mask, weight, weight_out, send_ref, gate_ref, columns_ref, got, send
):
    middle = finish(
        home, rows_after_first, vectors[:, 4:5], vectors[:, 6:7], gate, columns, weight_out[0], got
    ).astype(F32)
    columns_ref[...] = middle
    project(middle, mask, vectors[:, 1:2], vectors[:, 3:4], weight[1], send, send_ref, gate_ref)


def last_kernel(home, gate, columns, vectors, weight_out, out_ref, got, cells):
    updated = finish(
        home, rows_after_second, vectors[:, 5:6], vectors[:, 7:8], gate, columns, weight_out[1], got
    ).astype(F32)
    cells[...] = updated.T
    for a in range(ROWS):
        out_ref[a] = cells[pl.ds(a * WIDE, COLS), :].astype(BF16)


def send_home(triangle, out_ref, out_f):
    tiles = swap_groups([
        stack(
            triangle[((q * 4 + m) * 2 + yh) * 8 : ((q * 4 + m) * 2 + yh) * 8 + 8, x * 128 : x * 128 + 128]
            for m in range(GROUPS) for yh in range(2) for x in range(4)
        )
        for q in range(4)
    ])
    for m in range(GROUPS):
        for yh in range(2):
            for x in range(4):
                at = ((m * 2 + yh) * 4 + x) * 8
                for zh in range(4):
                    out_f[pl.ds((zh * 2 + yh) * 128 + x * 4 + m, 8, stride=16), :] = tiles[zh][at : at + 8]
    out_ref[...] = out_f[...].astype(BF16)


def outgoing_kernel(mine, both, out_ref, mine_f, both_f, out_f):
    mine_f[...] = mine[...].astype(F32)
    both_f[...] = both[...].astype(F32)

    def matrix(source, base):
        tiles = swap_groups([
            stack(
                source[pl.ds(base + ((zh * 2 + xl) * 2 + yh) * 64 + m, 8, stride=8), :]
                for xl in range(2) for m in range(GROUPS) for yh in range(2)
            )
            for zh in range(4)
        ])
        half = tiles[0].shape[0] // 2
        return stack(jnp.concatenate([tile[:half], tile[half:]], axis=1) for tile in tiles).astype(BF16)

    left = matrix(mine_f, 0)
    right = stack(matrix(both_f, core * 1024 + 4) for core in range(2))
    triangle = nt_dot(left, right).astype(BF16)
    send_home(nn_dot(triangle, token_matrix()), out_ref, out_f)


def incoming_kernel(place, both, out_ref, both_f, out_f):
    both_f[...] = both[...].astype(F32)

    def matrix(base):
        tiles = swap_groups([
            stack(
                both_f[pl.ds(base + core * 1024 + (zh * 4 + x) * 64 + m, 8, stride=8), :]
                for x in range(4) for m in range(GROUPS) for core in range(2)
            )
            for zh in range(4)
        ])
        return stack(
            jnp.concatenate([tile[x * 64 : x * 64 + 64] for x in range(4)], axis=1) for tile in tiles
        ).astype(BF16)

    left = nn_dot(matrix(0), own_matrix(place[0:1, 0:1] & 1)).astype(BF16)
    send_home(tn_dot(left, matrix(4)), out_ref, out_f)


def call(kernel, outs, scratch, name, held=()):
    def run(*args):
        return pl.pallas_call(
            kernel,
            out_shape=outs,
            in_specs=[pl.BlockSpec(memory_space=pltpu.HBM if at in held else pltpu.VMEM) for at in range(len(args))],
            out_specs=jax.tree.map(lambda _: pl.BlockSpec(memory_space=pltpu.VMEM), outs),
            scratch_shapes=[pltpu.VMEM(entry, F32) if isinstance(entry, tuple) else entry for entry in scratch],
            compiler_params=pltpu.CompilerParams(vmem_limit_bytes=32 * 1024 * 1024),
            name=name,
        )(*args)

    return run


def in_hbm(array):
    return pltpu.with_memory_space_constraint(array, pltpu.HBM)


def exchange(array, axes):
    return lax.all_to_all(array, axes, 0, 0, tiled=True)


def on_device(pair_rep, chain_lengths, in_gain, in_bias, weight_in, out_gain, out_bias, weight_out):
    place = jnp.concatenate([
        jnp.full((8, LANES), lax.axis_index(axes), jnp.int32) for axes in (ROW_AXES, COL_AXES)
    ])
    tile = jax.ShapeDtypeStruct((LANES, CELLS), F32)
    sent = jax.ShapeDtypeStruct((1024, LANES), BF16)

    small = (jax.ShapeDtypeStruct((LANES, 8), F32), jax.ShapeDtypeStruct((1, CELLS), F32))
    send, gate, columns, vectors, mask = call(
        first_kernel, (sent, tile, tile) + small, [
            (CELLS, LANES), (1024, LANES), (8, LANES), pltpu.SMEM(chain_lengths.shape, jnp.int32),
            pltpu.VMEM(pair_rep.shape, BF16), in_gain.shape, in_bias.shape, out_gain.shape, out_bias.shape,
            pltpu.VMEM(weight_in.shape[1:], BF16), pltpu.SemaphoreType.DMA((7,)),
        ], "first", range(1, 8),
    )(place, *map(in_hbm, (chain_lengths, pair_rep, in_gain, in_bias, weight_in, out_gain, out_bias)))
    mine = exchange(send.reshape(128, 8, LANES), GROUP1).reshape(1024, LANES)
    both = lax.all_gather(mine, "core", axis=0, tiled=True)
    home = call(
        outgoing_kernel, sent, [(1024, LANES), (2048, LANES), (1024, LANES)], "outgoing"
    )(mine, both)
    home = exchange(home.reshape(256, 4, LANES), BACK).reshape(1024, LANES)

    send, gate, columns = call(
        middle_kernel, (sent, tile, tile), [(1024, LANES), (1024, LANES)], "middle"
    )(home, gate, columns, vectors, mask, weight_in, weight_out)
    mine = exchange(send.reshape(128, 8, LANES), GROUP2).reshape(1024, LANES)
    both = lax.all_gather(mine, "core", axis=0, tiled=True)
    home = call(
        incoming_kernel, sent, [(2048, LANES), (1024, LANES)], "incoming"
    )(place, both)
    home = exchange(home.reshape(256, 4, LANES), BACK).reshape(1024, LANES)

    out = jax.ShapeDtypeStruct(pair_rep.shape, BF16)
    return call(last_kernel, out, [(1024, LANES), (CELLS, LANES)], "last")(home, gate, columns, vectors, weight_out)


def solution(mesh):
    fine = Mesh(mesh.devices.reshape(2, 4, 2, 2, 2, 2, 4), ROW_AXES + COL_AXES)
    placed = P(ROW_AXES, COL_AXES, None)
    return jax.shard_map(
        on_device, mesh=fine, in_specs=(placed,) + (P(),) * 7, out_specs=placed, check_vma=False
    )
```

```python
import jax
import jax.numpy as jnp
from jax import lax
from jax.experimental import pallas as pl
from jax.experimental.pallas import tpu as pltpu
from jax.sharding import Mesh, PartitionSpec as P

EPSILON = 1e-05
F32 = jnp.float32
BF16 = jnp.bfloat16

SPARE = 16

ROWS = 14
COLS = 28
WIDE = 32
CELLS = 512
GROUPS = 4
LANES = 128
SLOT = 112
CHAINS = 4

ROW_AXES = ("yh", "yl", "zl", "core")
COL_AXES = ("xh", "xl", "zh")
GROUP1 = ("zh", "xl", "yh", "yl", "zl")
GROUP2 = ("zh", "xh", "xl", "yl", "zl")
BACK = ("zh", "yh", "yl", "zl", "xh", "xl")


def nt_dot(left, right):
    return lax.dot_general(left, right, (((1,), (1,)), ((), ())), preferred_element_type=F32)


def tn_dot(left, right):
    return lax.dot_general(left, right, (((0,), (0,)), ((), ())), preferred_element_type=F32)


def nn_dot(left, right):
    return jnp.dot(left, right, preferred_element_type=F32)


def stack(pieces):
    return jnp.concatenate(list(pieces), axis=0)


def norm_rows(values, gain, bias):
    average = jnp.mean(values, axis=0, keepdims=True)
    centered = values - average
    variance = jnp.mean(centered * centered, axis=0, keepdims=True)
    return (centered * lax.rsqrt(variance + EPSILON) * gain + bias).astype(BF16)


def swap_groups(tiles):
    group = lax.broadcasted_iota(jnp.int32, tiles[0].shape, 1) >> 5
    for bit in (1, 2):
        keep = (group & bit) == 0
        out = list(tiles)
        for p in range(4):
            if p & bit == 0:
                low, high = tiles[p], tiles[p + bit]
                out[p] = jnp.where(keep, low, pltpu.roll(high, 32 * bit, 1))
                out[p + bit] = jnp.where(keep, pltpu.roll(low, LANES - 32 * bit, 1), high)
        tiles = out
    return tiles


def token_matrix():
    code = lax.broadcasted_iota(jnp.int32, (8, CELLS), 1)
    token = jnp.where(code & 31 < COLS, (code >> 5) * COLS + (code & 31), -4096)
    token = token - COLS * lax.broadcasted_iota(jnp.int32, (8, CELLS), 0)
    none = jnp.zeros((8, CELLS), F32)
    rows = []
    for core in range(2):
        for q in range(4):
            for m in range(GROUPS):
                for yh in range(2):
                    a = 4 * m + q
                    first = yh * 8 * COLS + core * ROWS + a
                    rows.append(jnp.where(token == first, 1.0, 0.0).astype(F32) if a < ROWS else none)
    return jnp.concatenate(rows, axis=0).astype(BF16)


def fields(code, *widths):
    out = []
    for width in reversed(widths):
        out.append(code & (width - 1))
        code = code >> (width.bit_length() - 1)
    return out[::-1]


def own_matrix(core):
    q, m, yh, s = fields(lax.broadcasted_iota(jnp.int32, (8, CELLS // 2), 1), 4, 4, 2, 8)
    a = 4 * m + q
    sub = lax.broadcasted_iota(jnp.int32, (8, CELLS // 2), 0)
    token = jnp.where(a < ROWS, ((yh * 8 + s) * 2 + core) * ROWS + a, -4096) - sub
    last = jnp.where(sub < COLS - 24, token, -4096)
    return jnp.concatenate([
        jnp.where((last if b == 24 else token) == c * COLS + b, 1.0, 0.0).astype(F32)
        for c in range(16) for b in range(0, WIDE, 8)
    ], axis=0).astype(BF16)


def valid_token(token, lengths_ref):
    valid = jnp.zeros(token.shape, jnp.bool_)
    for chain in range(CHAINS):
        start = chain * SLOT
        valid = valid | ((token >= start) & (token < start + lengths_ref[chain]))
    return valid


def cell_mask(place, lengths_ref):
    lane = lax.broadcasted_iota(jnp.int32, (1, CELLS), 1)
    a, b = lane >> 5, lane & 31
    row = valid_token(place[0:1, 0:1] * ROWS + a, lengths_ref)
    col = valid_token(place[8:9, 0:1] * COLS + b, lengths_ref)
    inside = (a < ROWS) & (b < COLS)
    return jnp.where(row & col & inside, 1.0, 0.0).astype(F32)


def project(columns, mask, gain, bias, weight, send, send_ref, gate_ref):
    for m in range(GROUPS):
        lanes = slice(m * LANES, (m + 1) * LANES)
        normed = norm_rows(columns[:, lanes], gain, bias)
        projected = tn_dot(weight, normed)
        weighting = mask[:, lanes]
        left = weighting * jax.nn.sigmoid(projected[128:256]) * projected[0:128]
        right = weighting * jax.nn.sigmoid(projected[384:512]) * projected[256:384]
        send[pl.ds(m, 128, stride=8), :] = left
        send[pl.ds(4 + m, 128, stride=8), :] = right
        gate_ref[:, lanes] = jax.nn.sigmoid(projected[512:640])
    send_ref[...] = send[pl.ds(0, 1024), :].astype(BF16)


def first_kernel(
    place, lengths_hbm, pair_hbm, in_gain_hbm, in_bias_hbm, weight_hbm, out_gain_hbm, out_bias_hbm,
    send_ref, gate_ref, columns_ref, vectors_ref, mask_ref, cells, send, norms, lengths, pair, in_gain, in_bias, out_gain, out_bias, weight, sems,
):
    copies = [
        pltpu.make_async_copy(source, target, sems.at[at])
        for at, (source, target) in enumerate((
            (pair_hbm, pair), (weight_hbm.at[0], weight), (in_gain_hbm, in_gain), (in_bias_hbm, in_bias),
            (out_gain_hbm, out_gain), (out_bias_hbm, out_bias), (lengths_hbm, lengths),
        ))
    ]
    for copy in copies:
        copy.start()
    cells[...] = jnp.zeros_like(cells)
    norms[...] = jnp.zeros_like(norms)
    for copy in copies:
        copy.wait()
    mask = cell_mask(place, lengths)
    mask_ref[...] = mask
    for at, pair_of in enumerate((in_gain, in_bias, out_gain, out_bias)):
        norms[pl.ds(2 * at, 2), :] = pair_of[...]
    vectors = norms[...].T
    vectors_ref[...] = vectors
    for a in range(ROWS):
        cells[pl.ds(a * WIDE, COLS), :] = pair[a].astype(F32)
    columns = cells[...].T
    columns_ref[...] = columns
    project(columns, mask, vectors[:, 0:1], vectors[:, 2:3], weight[...], send, send_ref, gate_ref)


def finish(home, source_rows, gain, bias, gate, columns, weight_out, got):
    got[pl.ds(0, 1024), :] = home[...].astype(F32)
    parts = []
    for m in range(GROUPS):
        lanes = slice(m * LANES, (m + 1) * LANES)
        triangle = source_rows(got, 0, m) + source_rows(got, 1, m)
        change = tn_dot(weight_out, norm_rows(triangle, gain, bias))
        parts.append(columns[:, lanes] + gate[:, lanes] * change)
    return jnp.concatenate(parts, axis=1).astype(BF16)


def rows_after_first(got, xh, m):
    return stack(
        got[pl.ds(zh * 256 + xh * 8 + xl * 4 + m, 16, stride=16), :] for zh in range(4) for xl in range(2)
    )


def rows_after_second(got, yh, m):
    return stack(
        got[pl.ds((zh * 2 + yh) * 128 + x * 4 + m, 8, stride=16), :] for zh in range(4) for x in range(4)
    )


def middle_kernel(
    home, gate, columns, vectors, mask, weight, weight_out, send_ref, gate_ref, columns_ref, got, send
):
    middle = finish(
        home, rows_after_first, vectors[:, 4:5], vectors[:, 6:7], gate, columns, weight_out[0], got
    ).astype(F32)
    columns_ref[...] = middle
    project(middle, mask, vectors[:, 1:2], vectors[:, 3:4], weight[1], send, send_ref, gate_ref)


def last_kernel(home, gate, columns, vectors, weight_out, out_ref, got, cells):
    updated = finish(
        home, rows_after_second, vectors[:, 5:6], vectors[:, 7:8], gate, columns, weight_out[1], got
    ).astype(F32)
    cells[...] = updated.T
    for a in range(ROWS):
        out_ref[a] = cells[pl.ds(a * WIDE, COLS), :].astype(BF16)


def send_home(triangle, out_ref, out_f):
    tiles = swap_groups([
        stack(
            triangle[((q * 4 + m) * 2 + yh) * 8 : ((q * 4 + m) * 2 + yh) * 8 + 8, x * 128 : x * 128 + 128]
            for m in range(GROUPS) for yh in range(2) for x in range(4)
        )
        for q in range(4)
    ])
    for m in range(GROUPS):
        for yh in range(2):
            for x in range(4):
                at = ((m * 2 + yh) * 4 + x) * 8
                for zh in range(4):
                    out_f[pl.ds((zh * 2 + yh) * 128 + x * 4 + m, 8, stride=16), :] = tiles[zh][at : at + 8]
    out_ref[...] = out_f[pl.ds(0, 1024), :].astype(BF16)


def outgoing_kernel(mine, both, out_ref, mine_f, both_f, out_f):
    mine_f[pl.ds(0, 1024), :] = mine[...].astype(F32)
    both_f[pl.ds(0, 2048), :] = both[...].astype(F32)

    def matrix(source, base):
        tiles = swap_groups([
            stack(
                source[pl.ds(base + ((zh * 2 + xl) * 2 + yh) * 64 + m, 8, stride=8), :]
                for xl in range(2) for m in range(GROUPS) for yh in range(2)
            )
            for zh in range(4)
        ])
        half = tiles[0].shape[0] // 2
        return stack(jnp.concatenate([tile[:half], tile[half:]], axis=1) for tile in tiles).astype(BF16)

    left = matrix(mine_f, 0)
    right = stack(matrix(both_f, core * 1024 + 4) for core in range(2))
    triangle = nt_dot(left, right).astype(BF16)
    send_home(nn_dot(triangle, token_matrix()), out_ref, out_f)


def incoming_kernel(place, both, out_ref, both_f, out_f):
    both_f[pl.ds(0, 2048), :] = both[...].astype(F32)

    def matrix(base):
        tiles = swap_groups([
            stack(
                both_f[pl.ds(base + core * 1024 + (zh * 4 + x) * 64 + m, 8, stride=8), :]
                for x in range(4) for m in range(GROUPS) for core in range(2)
            )
            for zh in range(4)
        ])
        return stack(
            jnp.concatenate([tile[x * 64 : x * 64 + 64] for x in range(4)], axis=1) for tile in tiles
        ).astype(BF16)

    left = nn_dot(matrix(0), own_matrix(place[0:1, 0:1] & 1)).astype(BF16)
    send_home(tn_dot(left, matrix(4)), out_ref, out_f)


def call(kernel, outs, scratch, name, held=()):
    def run(*args):
        return pl.pallas_call(
            kernel,
            out_shape=outs,
            in_specs=[pl.BlockSpec(memory_space=pltpu.HBM if at in held else pltpu.VMEM) for at in range(len(args))],
            out_specs=jax.tree.map(lambda _: pl.BlockSpec(memory_space=pltpu.VMEM), outs),
            scratch_shapes=[pltpu.VMEM(entry, F32) if isinstance(entry, tuple) else entry for entry in scratch],
            compiler_params=pltpu.CompilerParams(vmem_limit_bytes=32 * 1024 * 1024),
            name=name,
        )(*args)

    return run


def in_hbm(array):
    return pltpu.with_memory_space_constraint(array, pltpu.HBM)


def exchange(array, axes):
    return lax.all_to_all(array, axes, 0, 0, tiled=True)


def on_device(pair_rep, chain_lengths, in_gain, in_bias, weight_in, out_gain, out_bias, weight_out):
    place = jnp.concatenate([
        jnp.full((8, LANES), lax.axis_index(axes), jnp.int32) for axes in (ROW_AXES, COL_AXES)
    ])
    tile = jax.ShapeDtypeStruct((LANES, CELLS), F32)
    sent = jax.ShapeDtypeStruct((1024, LANES), BF16)

    strided = (1024 + SPARE, LANES)
    small = (jax.ShapeDtypeStruct((LANES, 8), F32), jax.ShapeDtypeStruct((1, CELLS), F32))
    send, gate, columns, vectors, mask = call(
        first_kernel, (sent, tile, tile) + small, [
            (CELLS, LANES), strided, (8, LANES), pltpu.SMEM(chain_lengths.shape, jnp.int32),
            pltpu.VMEM(pair_rep.shape, BF16), in_gain.shape, in_bias.shape, out_gain.shape, out_bias.shape,
            pltpu.VMEM(weight_in.shape[1:], BF16), pltpu.SemaphoreType.DMA((7,)),
        ], "first", range(1, 8),
    )(place, *map(in_hbm, (chain_lengths, pair_rep, in_gain, in_bias, weight_in, out_gain, out_bias)))
    mine = exchange(send.reshape(128, 8, LANES), GROUP1).reshape(1024, LANES)
    both = lax.all_gather(mine, "core", axis=0, tiled=True)
    home = call(
        outgoing_kernel, sent, [strided, (2048 + SPARE, LANES), strided], "outgoing"
    )(mine, both)
    home = exchange(home.reshape(256, 4, LANES), BACK).reshape(1024, LANES)

    send, gate, columns = call(
        middle_kernel, (sent, tile, tile), [strided, strided], "middle"
    )(home, gate, columns, vectors, mask, weight_in, weight_out)
    mine = exchange(send.reshape(128, 8, LANES), GROUP2).reshape(1024, LANES)
    both = lax.all_gather(mine, "core", axis=0, tiled=True)
    home = call(
        incoming_kernel, sent, [(2048 + SPARE, LANES), strided], "incoming"
    )(place, both)
    home = exchange(home.reshape(256, 4, LANES), BACK).reshape(1024, LANES)

    out = jax.ShapeDtypeStruct(pair_rep.shape, BF16)
    return call(last_kernel, out, [strided, (CELLS, LANES)], "last")(home, gate, columns, vectors, weight_out)


def solution(mesh):
    fine = Mesh(mesh.devices.reshape(2, 4, 2, 2, 2, 2, 4), ROW_AXES + COL_AXES)
    placed = P(ROW_AXES, COL_AXES, None)
    return jax.shard_map(
        on_device, mesh=fine, in_specs=(placed,) + (P(),) * 7, out_specs=placed, check_vma=False
    )
```

```python
import jax
import jax.numpy as jnp
from jax import lax
from jax.experimental import pallas as pl
from jax.experimental.pallas import tpu as pltpu
from jax.sharding import Mesh, PartitionSpec as P

EPSILON = 1e-05
F32 = jnp.float32
BF16 = jnp.bfloat16

SPARE = 16

ROWS = 14
COLS = 28
WIDE = 32
CELLS = 512
GROUPS = 4
LANES = 128
SLOT = 112
CHAINS = 4

ROW_AXES = ("yh", "ym", "yl", "zl", "core")
COL_AXES = ("xh", "xl", "zh")
GROUP1 = ("xh", "xl", "yh", "ym", "yl", "zl")
GROUP2 = ("xh", "xl", "zh", "yl", "zl")
BACK = ("zh", "xh", "xl", "yh", "ym", "yl", "zl")


def nt_dot(left, right):
    return lax.dot_general(left, right, (((1,), (1,)), ((), ())), preferred_element_type=F32)


def tn_dot(left, right):
    return lax.dot_general(left, right, (((0,), (0,)), ((), ())), preferred_element_type=F32)


def nn_dot(left, right):
    return jnp.dot(left, right, preferred_element_type=F32)


def stack(pieces):
    return jnp.concatenate(list(pieces), axis=0)


def norm_rows(values, gain, bias):
    average = jnp.mean(values, axis=0, keepdims=True)
    centered = values - average
    variance = jnp.mean(centered * centered, axis=0, keepdims=True)
    return (centered * lax.rsqrt(variance + EPSILON) * gain + bias).astype(BF16)


def swap_groups(tiles):
    group = lax.broadcasted_iota(jnp.int32, tiles[0].shape, 1) >> 5
    for bit in (1, 2):
        keep = (group & bit) == 0
        out = list(tiles)
        for p in range(4):
            if p & bit == 0:
                low, high = tiles[p], tiles[p + bit]
                out[p] = jnp.where(keep, low, pltpu.roll(high, 32 * bit, 1))
                out[p + bit] = jnp.where(keep, pltpu.roll(low, LANES - 32 * bit, 1), high)
        tiles = out
    return tiles


def fields(code, *widths):
    out = []
    for width in reversed(widths):
        out.append(code & (width - 1))
        code = code >> (width.bit_length() - 1)
    return out[::-1]


def token_matrix(core=None):
    lane = lax.broadcasted_iota(jnp.int32, (8, CELLS if core is None else CELLS // 2), 1)
    lane_core, q, m, yh, s = fields(lane, 2, 4, 4, 2, 8)
    core = lane_core if core is None else core
    a = 4 * m + q
    sub = lax.broadcasted_iota(jnp.int32, lane.shape, 0)
    token = jnp.where(a < ROWS, ((yh * 8 + s) * 2 + core) * ROWS + a, -4096) - sub
    last = jnp.where(sub < COLS - 24, token, -4096)
    return stack(
        jnp.where((last if b == 24 else token) == c * COLS + b, 1.0, 0.0).astype(F32)
        for c in range(16) for b in range(0, WIDE, 8)
    ).astype(BF16)


def valid_token(token, lengths_ref):
    valid = jnp.zeros(token.shape, jnp.bool_)
    for chain in range(CHAINS):
        start = chain * SLOT
        valid = valid | ((token >= start) & (token < start + lengths_ref[chain]))
    return valid


def cell_mask(place, lengths_ref):
    lane = lax.broadcasted_iota(jnp.int32, (1, CELLS), 1)
    a, b = lane >> 5, lane & 31
    row = valid_token(place[0:1, 0:1] * ROWS + a, lengths_ref)
    col = valid_token(place[8:9, 0:1] * COLS + b, lengths_ref)
    inside = (a < ROWS) & (b < COLS)
    return jnp.where(row & col & inside, 1.0, 0.0).astype(F32)


def project(columns, mask, gain, bias, weight, send, send_ref, gate_ref):
    for m in range(GROUPS):
        lanes = slice(m * LANES, (m + 1) * LANES)
        normed = norm_rows(columns[:, lanes], gain, bias)
        projected = tn_dot(weight, normed)
        weighting = mask[:, lanes]
        left = weighting * jax.nn.sigmoid(projected[128:256]) * projected[0:128]
        right = weighting * jax.nn.sigmoid(projected[384:512]) * projected[256:384]
        for channel in range(2):
            half = slice(channel * 64, channel * 64 + 64)
            send[pl.ds(channel * 8 + m, 64, stride=16), :] = left[half]
            send[pl.ds(channel * 8 + 4 + m, 64, stride=16), :] = right[half]
        gate_ref[:, lanes] = jax.nn.sigmoid(projected[512:640])
    send_ref[...] = send[pl.ds(0, 1024), :].astype(BF16)


def first_kernel(
    place, lengths_hbm, pair_hbm, in_gain_hbm, in_bias_hbm, weight_hbm, out_gain_hbm, out_bias_hbm,
    send_ref, gate_ref, columns_ref, vectors_ref, mask_ref, cells, send, norms, lengths, pair, in_gain, in_bias, out_gain, out_bias, weight, sems,
):
    copies = [
        pltpu.make_async_copy(source, target, sems.at[at])
        for at, (source, target) in enumerate((
            (pair_hbm, pair), (weight_hbm.at[0], weight), (in_gain_hbm, in_gain), (in_bias_hbm, in_bias),
            (out_gain_hbm, out_gain), (out_bias_hbm, out_bias), (lengths_hbm, lengths),
        ))
    ]
    for copy in copies:
        copy.start()
    cells[...] = jnp.zeros_like(cells)
    norms[...] = jnp.zeros_like(norms)
    for copy in copies:
        copy.wait()
    mask = cell_mask(place, lengths)
    mask_ref[...] = mask
    for at, pair_of in enumerate((in_gain, in_bias, out_gain, out_bias)):
        norms[pl.ds(2 * at, 2), :] = pair_of[...]
    vectors = norms[...].T
    vectors_ref[...] = vectors
    for a in range(ROWS):
        cells[pl.ds(a * WIDE, COLS), :] = pair[a].astype(F32)
    columns = cells[...].T
    columns_ref[...] = columns
    project(columns, mask, vectors[:, 0:1], vectors[:, 2:3], weight[...], send, send_ref, gate_ref)


def finish(home, source_rows, gain, bias, gate, columns, weight_out, got):
    got[pl.ds(0, 2048), :] = home[...].astype(F32)
    parts = []
    for m in range(GROUPS):
        lanes = slice(m * LANES, (m + 1) * LANES)
        change = tn_dot(weight_out, norm_rows(source_rows(got, m), gain, bias))
        parts.append(columns[:, lanes] + gate[:, lanes] * change)
    return jnp.concatenate(parts, axis=1).astype(BF16)


def rows_after_first(got, m):
    return stack(
        sum(got[pl.ds((zh * 4 + x) * 128 + channel * 4 + m, 16, stride=8), :] for zh in range(4))
        for channel in range(2) for x in range(4)
    )


def rows_after_second(got, m):
    low = lax.broadcasted_iota(jnp.int32, (8, LANES), 0) < 4

    def total(channel, x, zh):
        half = sum(got[pl.ds(((zh * 4 + x) * 2 + yh) * 64 + channel * 4 + m, 8, stride=8), :] for yh in range(2))
        return half + pltpu.roll(half, 4, 0)

    return stack(
        jnp.where(low, total(channel, x, zh), total(channel, x, zh + 1))
        for channel in range(2) for x in range(4) for zh in range(0, 4, 2)
    )


def middle_kernel(
    home, gate, columns, vectors, mask, weight, weight_out, send_ref, gate_ref, columns_ref, got, send
):
    middle = finish(
        home, rows_after_first, vectors[:, 4:5], vectors[:, 6:7], gate, columns, weight_out[0], got
    ).astype(F32)
    columns_ref[...] = middle
    project(middle, mask, vectors[:, 1:2], vectors[:, 3:4], weight[1], send, send_ref, gate_ref)


def last_kernel(home, gate, columns, vectors, weight_out, out_ref, got, cells):
    updated = finish(
        home, rows_after_second, vectors[:, 5:6], vectors[:, 7:8], gate, columns, weight_out[1], got
    ).astype(F32)
    cells[...] = updated.T
    for a in range(ROWS):
        out_ref[a] = cells[pl.ds(a * WIDE, COLS), :].astype(BF16)


def send_home(triangles, out_ref, out_f):
    for channel, triangle in enumerate(triangles):
        tiles = swap_groups([
            stack(
                triangle[((q * 4 + m) * 2 + yh) * 8 : ((q * 4 + m) * 2 + yh) * 8 + 8, x * 128 : x * 128 + 128]
                for m in range(GROUPS) for yh in range(2) for x in range(4)
            )
            for q in range(4)
        ])
        for m in range(GROUPS):
            for yh in range(2):
                for x in range(4):
                    at = ((m * 2 + yh) * 4 + x) * 8
                    for zh in range(4):
                        out_f[pl.ds(((zh * 4 + x) * 2 + yh) * 64 + channel * 4 + m, 8, stride=8), :] = tiles[zh][
                            at : at + 8
                        ]
    out_ref[...] = out_f[pl.ds(0, 2048), :].astype(BF16)


def outgoing_kernel(mine, both, out_ref, mine_f, both_f, out_f):
    mine_f[pl.ds(0, 1024), :] = mine[...].astype(F32)
    both_f[pl.ds(0, 2048), :] = both[...].astype(F32)

    def matrix(source, base):
        return stack(swap_groups([
            stack(
                source[pl.ds(base + (x * 2 + yh) * 128 + m, 8, stride=16), :]
                for m in range(GROUPS) for yh in range(2)
            )
            for x in range(4)
        ])).astype(BF16)

    right = jnp.concatenate([
        stack(matrix(both_f, core * 1024 + channel * 8 + 4) for core in range(2)) for channel in range(2)
    ], axis=1)
    right = nn_dot(token_matrix(), right).astype(BF16)
    send_home([
        nt_dot(matrix(mine_f, channel * 8), right[:, channel * LANES : (channel + 1) * LANES]) for channel in range(2)
    ], out_ref, out_f)


def incoming_kernel(place, both, out_ref, both_f, out_f):
    for core in range(2):
        for at in range(64):
            both_f[pl.ds((at * 2 + core) * 16, 16), :] = both[pl.ds((core * 64 + at) * 16, 16), :].astype(F32)

    def matrix(base):
        tiles = swap_groups([
            stack(
                both_f[pl.ds(base + (x * 4 + zh) * 128 + m, 8, stride=16), :]
                for x in range(4) for m in range(GROUPS)
            )
            for zh in range(4)
        ])
        return stack(
            jnp.concatenate([tile[x * 32 : x * 32 + 32] for x in range(4)], axis=1) for tile in tiles
        ).astype(BF16)

    left = stack(matrix(channel * 8) for channel in range(2))
    left = nn_dot(left, token_matrix(place[0:1, 0:1] & 1)).astype(BF16)
    send_home([
        tn_dot(left[channel * 128 : channel * 128 + 128], matrix(channel * 8 + 4)) for channel in range(2)
    ], out_ref, out_f)


def call(kernel, outs, scratch, name, held=()):
    def run(*args):
        return pl.pallas_call(
            kernel,
            out_shape=outs,
            in_specs=[pl.BlockSpec(memory_space=pltpu.HBM if at in held else pltpu.VMEM) for at in range(len(args))],
            out_specs=jax.tree.map(lambda _: pl.BlockSpec(memory_space=pltpu.VMEM), outs),
            scratch_shapes=[pltpu.VMEM(entry, F32) if isinstance(entry, tuple) else entry for entry in scratch],
            compiler_params=pltpu.CompilerParams(vmem_limit_bytes=32 * 1024 * 1024),
            name=name,
        )(*args)

    return run


def in_hbm(array):
    return pltpu.with_memory_space_constraint(array, pltpu.HBM)


def exchange(array, axes):
    return lax.all_to_all(array, axes, 0, 0, tiled=True)


def on_device(pair_rep, chain_lengths, in_gain, in_bias, weight_in, out_gain, out_bias, weight_out):
    place = jnp.concatenate([
        jnp.full((8, LANES), lax.axis_index(axes), jnp.int32) for axes in (ROW_AXES, COL_AXES)
    ])
    tile = jax.ShapeDtypeStruct((LANES, CELLS), F32)
    sent = jax.ShapeDtypeStruct((1024, LANES), BF16)
    returned = jax.ShapeDtypeStruct((2048, LANES), BF16)

    strided, longer = (1024 + SPARE, LANES), (2048 + SPARE, LANES)
    small = (jax.ShapeDtypeStruct((LANES, 8), F32), jax.ShapeDtypeStruct((1, CELLS), F32))
    send, gate, columns, vectors, mask = call(
        first_kernel, (sent, tile, tile) + small, [
            (CELLS, LANES), strided, (8, LANES), pltpu.SMEM(chain_lengths.shape, jnp.int32),
            pltpu.VMEM(pair_rep.shape, BF16), in_gain.shape, in_bias.shape, out_gain.shape, out_bias.shape,
            pltpu.VMEM(weight_in.shape[1:], BF16), pltpu.SemaphoreType.DMA((7,)),
        ], "first", range(1, 8),
    )(place, *map(in_hbm, (chain_lengths, pair_rep, in_gain, in_bias, weight_in, out_gain, out_bias)))
    mine = exchange(send.reshape(64, 16, LANES), GROUP1).reshape(1024, LANES)
    both = lax.all_gather(mine, "core", axis=0, tiled=True)
    home = call(
        outgoing_kernel, returned, [strided, longer, longer], "outgoing"
    )(mine, both)
    home = exchange(home.reshape(256, 8, LANES), BACK).reshape(2048, LANES)

    send, gate, columns = call(
        middle_kernel, (sent, tile, tile), [longer, strided], "middle"
    )(home, gate, columns, vectors, mask, weight_in, weight_out)
    mine = exchange(send.reshape(64, 16, LANES), GROUP2).reshape(1024, LANES)
    both = lax.all_gather(mine, "core", axis=0, tiled=True)
    home = call(
        incoming_kernel, returned, [longer, longer], "incoming"
    )(place, both)
    home = exchange(home.reshape(256, 8, LANES), BACK).reshape(2048, LANES)

    out = jax.ShapeDtypeStruct(pair_rep.shape, BF16)
    return call(last_kernel, out, [longer, (CELLS, LANES)], "last")(home, gate, columns, vectors, weight_out)


def solution(mesh):
    fine = Mesh(mesh.devices.reshape(2, 2, 2, 2, 2, 2, 2, 4), ROW_AXES + COL_AXES)
    placed = P(ROW_AXES, COL_AXES, None)
    return jax.shard_map(
        on_device, mesh=fine, in_specs=(placed,) + (P(),) * 7, out_specs=placed, check_vma=False
    )
```

```python
import jax
import jax.numpy as jnp
from jax import lax
from jax.experimental import pallas as pl
from jax.experimental.pallas import tpu as pltpu
from jax.sharding import Mesh, PartitionSpec as P

EPSILON = 1e-05
F32 = jnp.float32
BF16 = jnp.bfloat16

SPARE = 16

ROWS = 14
COLS = 28
WIDE = 32
CELLS = 512
GROUPS = 4
LANES = 128
SLOT = 112
CHAINS = 4

ROW_AXES = ("yh", "yl", "zl", "core")
COL_AXES = ("xh", "xl", "zh")
GROUP1 = ("zh", "xl", "yh", "yl", "zl")
GROUP2 = ("zh", "xh", "xl", "yl", "zl")
BACK = ("zh", "xh", "xl", "yh", "yl", "zl")


def nt_dot(left, right):
    return lax.dot_general(left, right, (((1,), (1,)), ((), ())), preferred_element_type=F32)


def tn_dot(left, right):
    return lax.dot_general(left, right, (((0,), (0,)), ((), ())), preferred_element_type=F32)


def nn_dot(left, right):
    return jnp.dot(left, right, preferred_element_type=F32)


def stack(pieces):
    return jnp.concatenate(list(pieces), axis=0)


def norm_rows(values, gain, bias):
    average = jnp.mean(values, axis=0, keepdims=True)
    centered = values - average
    variance = jnp.mean(centered * centered, axis=0, keepdims=True)
    return (centered * lax.rsqrt(variance + EPSILON) * gain + bias).astype(BF16)


def swap_groups(tiles):
    group = lax.broadcasted_iota(jnp.int32, tiles[0].shape, 1) >> 5
    for bit in (1, 2):
        keep = (group & bit) == 0
        out = list(tiles)
        for p in range(4):
            if p & bit == 0:
                low, high = tiles[p], tiles[p + bit]
                out[p] = jnp.where(keep, low, pltpu.roll(high, 32 * bit, 1))
                out[p + bit] = jnp.where(keep, pltpu.roll(low, LANES - 32 * bit, 1), high)
        tiles = out
    return tiles


def token_matrix():
    code = lax.broadcasted_iota(jnp.int32, (8, CELLS), 1)
    token = jnp.where(code & 31 < COLS, (code >> 5) * COLS + (code & 31), -4096)
    token = token - COLS * lax.broadcasted_iota(jnp.int32, (8, CELLS), 0)
    none = jnp.zeros((8, CELLS), F32)
    rows = []
    for core in range(2):
        for q in range(4):
            for m in range(GROUPS):
                for yh in range(2):
                    a = 4 * m + q
                    first = yh * 8 * COLS + core * ROWS + a
                    rows.append(jnp.where(token == first, 1.0, 0.0).astype(F32) if a < ROWS else none)
    return jnp.concatenate(rows, axis=0).astype(BF16)


def fields(code, *widths):
    out = []
    for width in reversed(widths):
        out.append(code & (width - 1))
        code = code >> (width.bit_length() - 1)
    return out[::-1]


def own_matrix(core):
    q, m, yh, s = fields(lax.broadcasted_iota(jnp.int32, (8, CELLS // 2), 1), 4, 4, 2, 8)
    a = 4 * m + q
    sub = lax.broadcasted_iota(jnp.int32, (8, CELLS // 2), 0)
    token = jnp.where(a < ROWS, ((yh * 8 + s) * 2 + core) * ROWS + a, -4096) - sub
    last = jnp.where(sub < COLS - 24, token, -4096)
    return jnp.concatenate([
        jnp.where((last if b == 24 else token) == c * COLS + b, 1.0, 0.0).astype(F32)
        for c in range(16) for b in range(0, WIDE, 8)
    ], axis=0).astype(BF16)


def valid_token(token, lengths_ref):
    valid = jnp.zeros(token.shape, jnp.bool_)
    for chain in range(CHAINS):
        start = chain * SLOT
        valid = valid | ((token >= start) & (token < start + lengths_ref[chain]))
    return valid


def cell_mask(place, lengths_ref):
    lane = lax.broadcasted_iota(jnp.int32, (1, CELLS), 1)
    a, b = lane >> 5, lane & 31
    row = valid_token(place[0:1, 0:1] * ROWS + a, lengths_ref)
    col = valid_token(place[8:9, 0:1] * COLS + b, lengths_ref)
    inside = (a < ROWS) & (b < COLS)
    return jnp.where(row & col & inside, 1.0, 0.0).astype(F32)


def project(columns, mask, gain, bias, weight, send, send_ref, gate_ref):
    for m in range(GROUPS):
        lanes = slice(m * LANES, (m + 1) * LANES)
        normed = norm_rows(columns[:, lanes], gain, bias)
        projected = tn_dot(weight, normed)
        weighting = mask[:, lanes]
        left = weighting * jax.nn.sigmoid(projected[128:256]) * projected[0:128]
        right = weighting * jax.nn.sigmoid(projected[384:512]) * projected[256:384]
        send[pl.ds(m, 128, stride=8), :] = left
        send[pl.ds(4 + m, 128, stride=8), :] = right
        gate_ref[:, lanes] = jax.nn.sigmoid(projected[512:640])
    send_ref[...] = send[pl.ds(0, 1024), :].astype(BF16)


def first_kernel(
    place, lengths_hbm, pair_hbm, in_gain_hbm, in_bias_hbm, weight_hbm, out_gain_hbm, out_bias_hbm,
    send_ref, gate_ref, columns_ref, vectors_ref, mask_ref, cells, send, norms, lengths, pair, in_gain, in_bias, out_gain, out_bias, weight, sems,
):
    copies = [
        pltpu.make_async_copy(source, target, sems.at[at])
        for at, (source, target) in enumerate((
            (pair_hbm, pair), (weight_hbm.at[0], weight), (in_gain_hbm, in_gain), (in_bias_hbm, in_bias),
            (out_gain_hbm, out_gain), (out_bias_hbm, out_bias), (lengths_hbm, lengths),
        ))
    ]
    for copy in copies:
        copy.start()
    cells[...] = jnp.zeros_like(cells)
    norms[...] = jnp.zeros_like(norms)
    for copy in copies:
        copy.wait()
    mask = cell_mask(place, lengths)
    mask_ref[...] = mask
    for at, pair_of in enumerate((in_gain, in_bias, out_gain, out_bias)):
        norms[pl.ds(2 * at, 2), :] = pair_of[...]
    vectors = norms[...].T
    vectors_ref[...] = vectors
    for a in range(ROWS):
        cells[pl.ds(a * WIDE, COLS), :] = pair[a].astype(F32)
    columns = cells[...].T
    columns_ref[...] = columns
    project(columns, mask, vectors[:, 0:1], vectors[:, 2:3], weight[...], send, send_ref, gate_ref)


def finish(home, source_rows, gain, bias, gate, columns, weight_out, got):
    got[pl.ds(0, 1024), :] = home[...].astype(F32)
    parts = []
    for m in range(GROUPS):
        lanes = slice(m * LANES, (m + 1) * LANES)
        triangle = source_rows(got, 0, m) + source_rows(got, 1, m)
        change = tn_dot(weight_out, norm_rows(triangle, gain, bias))
        parts.append(columns[:, lanes] + gate[:, lanes] * change)
    return jnp.concatenate(parts, axis=1).astype(BF16)


def rows_after_first(got, xh, m):
    return stack(
        got[pl.ds((zh * 4 + xh * 2 + xl) * 64 + m, 16, stride=4), :] for zh in range(4) for xl in range(2)
    )


def rows_after_second(got, yh, m):
    return stack(
        got[pl.ds(((zh * 4 + x) * 2 + yh) * 32 + m, 8, stride=4), :] for zh in range(4) for x in range(4)
    )


def middle_kernel(
    home, gate, columns, vectors, mask, weight, weight_out, send_ref, gate_ref, columns_ref, got, send
):
    middle = finish(
        home, rows_after_first, vectors[:, 4:5], vectors[:, 6:7], gate, columns, weight_out[0], got
    ).astype(F32)
    columns_ref[...] = middle
    project(middle, mask, vectors[:, 1:2], vectors[:, 3:4], weight[1], send, send_ref, gate_ref)


def last_kernel(home, gate, columns, vectors, weight_out, out_ref, got, cells):
    updated = finish(
        home, rows_after_second, vectors[:, 5:6], vectors[:, 7:8], gate, columns, weight_out[1], got
    ).astype(F32)
    cells[...] = updated.T
    for a in range(ROWS):
        out_ref[a] = cells[pl.ds(a * WIDE, COLS), :].astype(BF16)


def send_home(triangle, out_ref, out_f):
    tiles = swap_groups([
        stack(
            triangle[((q * 4 + m) * 2 + yh) * 8 : ((q * 4 + m) * 2 + yh) * 8 + 8, x * 128 : x * 128 + 128]
            for m in range(GROUPS) for yh in range(2) for x in range(4)
        )
        for q in range(4)
    ])
    for m in range(GROUPS):
        for yh in range(2):
            for x in range(4):
                at = ((m * 2 + yh) * 4 + x) * 8
                for zh in range(4):
                    out_f[pl.ds(((zh * 4 + x) * 2 + yh) * 32 + m, 8, stride=4), :] = tiles[zh][at : at + 8]
    out_ref[...] = out_f[pl.ds(0, 1024), :].astype(BF16)


def outgoing_kernel(mine, both, out_ref, mine_f, both_f, out_f):
    mine_f[pl.ds(0, 1024), :] = mine[...].astype(F32)
    both_f[pl.ds(0, 2048), :] = both[...].astype(F32)

    def matrix(source, base):
        tiles = swap_groups([
            stack(
                source[pl.ds(base + ((zh * 2 + xl) * 2 + yh) * 64 + m, 8, stride=8), :]
                for xl in range(2) for m in range(GROUPS) for yh in range(2)
            )
            for zh in range(4)
        ])
        half = tiles[0].shape[0] // 2
        return stack(jnp.concatenate([tile[:half], tile[half:]], axis=1) for tile in tiles).astype(BF16)

    left = matrix(mine_f, 0)
    right = stack(matrix(both_f, core * 1024 + 4) for core in range(2))
    triangle = nt_dot(left, right).astype(BF16)
    send_home(nn_dot(triangle, token_matrix()), out_ref, out_f)


def incoming_kernel(place, both, out_ref, both_f, out_f):
    both_f[pl.ds(0, 2048), :] = both[...].astype(F32)

    def matrix(base):
        tiles = swap_groups([
            stack(
                both_f[pl.ds(base + core * 1024 + (zh * 4 + x) * 64 + m, 8, stride=8), :]
                for x in range(4) for m in range(GROUPS) for core in range(2)
            )
            for zh in range(4)
        ])
        return stack(
            jnp.concatenate([tile[x * 64 : x * 64 + 64] for x in range(4)], axis=1) for tile in tiles
        ).astype(BF16)

    left = nn_dot(matrix(0), own_matrix(place[0:1, 0:1] & 1)).astype(BF16)
    send_home(tn_dot(left, matrix(4)), out_ref, out_f)


def call(kernel, outs, scratch, name, held=()):
    def run(*args):
        return pl.pallas_call(
            kernel,
            out_shape=outs,
            in_specs=[pl.BlockSpec(memory_space=pltpu.HBM if at in held else pltpu.VMEM) for at in range(len(args))],
            out_specs=jax.tree.map(lambda _: pl.BlockSpec(memory_space=pltpu.VMEM), outs),
            scratch_shapes=[pltpu.VMEM(entry, F32) if isinstance(entry, tuple) else entry for entry in scratch],
            compiler_params=pltpu.CompilerParams(vmem_limit_bytes=32 * 1024 * 1024),
            name=name,
        )(*args)

    return run


def in_hbm(array):
    return pltpu.with_memory_space_constraint(array, pltpu.HBM)


def exchange(array, axes):
    return lax.all_to_all(array, axes, 0, 0, tiled=True)


def on_device(pair_rep, chain_lengths, in_gain, in_bias, weight_in, out_gain, out_bias, weight_out):
    place = jnp.concatenate([
        jnp.full((8, LANES), lax.axis_index(axes), jnp.int32) for axes in (ROW_AXES, COL_AXES)
    ])
    tile = jax.ShapeDtypeStruct((LANES, CELLS), F32)
    sent = jax.ShapeDtypeStruct((1024, LANES), BF16)

    strided = (1024 + SPARE, LANES)
    small = (jax.ShapeDtypeStruct((LANES, 8), F32), jax.ShapeDtypeStruct((1, CELLS), F32))
    send, gate, columns, vectors, mask = call(
        first_kernel, (sent, tile, tile) + small, [
            (CELLS, LANES), strided, (8, LANES), pltpu.SMEM(chain_lengths.shape, jnp.int32),
            pltpu.VMEM(pair_rep.shape, BF16), in_gain.shape, in_bias.shape, out_gain.shape, out_bias.shape,
            pltpu.VMEM(weight_in.shape[1:], BF16), pltpu.SemaphoreType.DMA((7,)),
        ], "first", range(1, 8),
    )(place, *map(in_hbm, (chain_lengths, pair_rep, in_gain, in_bias, weight_in, out_gain, out_bias)))
    mine = exchange(send.reshape(128, 8, LANES), GROUP1).reshape(1024, LANES)
    both = lax.all_gather(mine, "core", axis=0, tiled=True)
    home = call(
        outgoing_kernel, sent, [strided, (2048 + SPARE, LANES), strided], "outgoing"
    )(mine, both)
    home = exchange(home.reshape(256, 4, LANES), BACK).reshape(1024, LANES)

    send, gate, columns = call(
        middle_kernel, (sent, tile, tile), [strided, strided], "middle"
    )(home, gate, columns, vectors, mask, weight_in, weight_out)
    mine = exchange(send.reshape(128, 8, LANES), GROUP2).reshape(1024, LANES)
    both = lax.all_gather(mine, "core", axis=0, tiled=True)
    home = call(
        incoming_kernel, sent, [(2048 + SPARE, LANES), strided], "incoming"
    )(place, both)
    home = exchange(home.reshape(256, 4, LANES), BACK).reshape(1024, LANES)

    out = jax.ShapeDtypeStruct(pair_rep.shape, BF16)
    return call(last_kernel, out, [strided, (CELLS, LANES)], "last")(home, gate, columns, vectors, weight_out)


def solution(mesh):
    fine = Mesh(mesh.devices.reshape(2, 4, 2, 2, 2, 2, 4), ROW_AXES + COL_AXES)
    placed = P(ROW_AXES, COL_AXES, None)
    return jax.shard_map(
        on_device, mesh=fine, in_specs=(placed,) + (P(),) * 7, out_specs=placed, check_vma=False
    )
```

```python
import jax
import jax.numpy as jnp
from jax import lax
from jax.experimental import pallas as pl
from jax.experimental.pallas import tpu as pltpu
from jax.sharding import Mesh, PartitionSpec as P

EPSILON = 1e-05
F32 = jnp.float32
BF16 = jnp.bfloat16

SPARE = 64

ROWS = 14
COLS = 28
WIDE = 32
CELLS = 512
GROUPS = 4
LANES = 128
SLOT = 112
CHAINS = 4

ROW_AXES = ("yh", "yl", "zl", "core")
COL_AXES = ("xh", "xl", "zh")
GROUP1 = ("zh", "xl", "yh", "yl", "zl")
GROUP2 = ("zh", "xh", "xl", "yl", "zl")
BACK = ("yh", "yl", "zl", "xh", "xl", "zh")


def nt_dot(left, right):
    return lax.dot_general(left, right, (((1,), (1,)), ((), ())), preferred_element_type=F32)


def tn_dot(left, right):
    return lax.dot_general(left, right, (((0,), (0,)), ((), ())), preferred_element_type=F32)


def nn_dot(left, right):
    return jnp.dot(left, right, preferred_element_type=F32)


def stack(pieces):
    return jnp.concatenate(list(pieces), axis=0)


def norm_rows(values, gain, bias):
    average = jnp.mean(values, axis=0, keepdims=True)
    centered = values - average
    variance = jnp.mean(centered * centered, axis=0, keepdims=True)
    return (centered * lax.rsqrt(variance + EPSILON) * gain + bias).astype(BF16)


def swap_groups(tiles):
    group = lax.broadcasted_iota(jnp.int32, tiles[0].shape, 1) >> 5
    for bit in (1, 2):
        keep = (group & bit) == 0
        out = list(tiles)
        for p in range(4):
            if p & bit == 0:
                low, high = tiles[p], tiles[p + bit]
                out[p] = jnp.where(keep, low, pltpu.roll(high, 32 * bit, 1))
                out[p + bit] = jnp.where(keep, pltpu.roll(low, LANES - 32 * bit, 1), high)
        tiles = out
    return tiles


def token_matrix():
    code = lax.broadcasted_iota(jnp.int32, (8, CELLS), 1)
    token = jnp.where(code & 31 < COLS, (code >> 5) * COLS + (code & 31), -4096)
    token = token - COLS * lax.broadcasted_iota(jnp.int32, (8, CELLS), 0)
    none = jnp.zeros((8, CELLS), F32)
    rows = []
    for core in range(2):
        for q in range(4):
            for m in range(GROUPS):
                for yh in range(2):
                    a = 4 * m + q
                    first = yh * 8 * COLS + core * ROWS + a
                    rows.append(jnp.where(token == first, 1.0, 0.0).astype(F32) if a < ROWS else none)
    return jnp.concatenate(rows, axis=0).astype(BF16)


def fields(code, *widths):
    out = []
    for width in reversed(widths):
        out.append(code & (width - 1))
        code = code >> (width.bit_length() - 1)
    return out[::-1]


def own_matrix(core):
    q, m, yh, s = fields(lax.broadcasted_iota(jnp.int32, (8, CELLS // 2), 1), 4, 4, 2, 8)
    a = 4 * m + q
    sub = lax.broadcasted_iota(jnp.int32, (8, CELLS // 2), 0)
    token = jnp.where(a < ROWS, ((yh * 8 + s) * 2 + core) * ROWS + a, -4096) - sub
    last = jnp.where(sub < COLS - 24, token, -4096)
    return jnp.concatenate([
        jnp.where((last if b == 24 else token) == c * COLS + b, 1.0, 0.0).astype(F32)
        for c in range(16) for b in range(0, WIDE, 8)
    ], axis=0).astype(BF16)


def valid_token(token, lengths_ref):
    valid = jnp.zeros(token.shape, jnp.bool_)
    for chain in range(CHAINS):
        start = chain * SLOT
        valid = valid | ((token >= start) & (token < start + lengths_ref[chain]))
    return valid


def cell_mask(place, lengths_ref):
    lane = lax.broadcasted_iota(jnp.int32, (1, CELLS), 1)
    a, b = lane >> 5, lane & 31
    row = valid_token(place[0:1, 0:1] * ROWS + a, lengths_ref)
    col = valid_token(place[8:9, 0:1] * COLS + b, lengths_ref)
    inside = (a < ROWS) & (b < COLS)
    return jnp.where(row & col & inside, 1.0, 0.0).astype(F32)


def project(columns, mask, gain, bias, weight, send, send_ref, gate_ref):
    for m in range(GROUPS):
        lanes = slice(m * LANES, (m + 1) * LANES)
        normed = norm_rows(columns[:, lanes], gain, bias)
        projected = tn_dot(weight, normed)
        weighting = mask[:, lanes]
        left = weighting * jax.nn.sigmoid(projected[128:256]) * projected[0:128]
        right = weighting * jax.nn.sigmoid(projected[384:512]) * projected[256:384]
        send[pl.ds(m, 128, stride=8), :] = left
        send[pl.ds(4 + m, 128, stride=8), :] = right
        gate_ref[:, lanes] = jax.nn.sigmoid(projected[512:640])
    send_ref[...] = send[pl.ds(0, 1024), :].astype(BF16)


def first_kernel(
    place, lengths_hbm, pair_hbm, in_gain_hbm, in_bias_hbm, weight_hbm, out_gain_hbm, out_bias_hbm,
    send_ref, gate_ref, columns_ref, vectors_ref, mask_ref, cells, send, norms, lengths, pair, in_gain, in_bias, out_gain, out_bias, weight, sems,
):
    copies = [
        pltpu.make_async_copy(source, target, sems.at[at])
        for at, (source, target) in enumerate((
            (pair_hbm, pair), (weight_hbm.at[0], weight), (in_gain_hbm, in_gain), (in_bias_hbm, in_bias),
            (out_gain_hbm, out_gain), (out_bias_hbm, out_bias), (lengths_hbm, lengths),
        ))
    ]
    for copy in copies:
        copy.start()
    cells[...] = jnp.zeros_like(cells)
    norms[...] = jnp.zeros_like(norms)
    for copy in copies:
        copy.wait()
    mask = cell_mask(place, lengths)
    mask_ref[...] = mask
    for at, pair_of in enumerate((in_gain, in_bias, out_gain, out_bias)):
        norms[pl.ds(2 * at, 2), :] = pair_of[...]
    vectors = norms[...].T
    vectors_ref[...] = vectors
    for a in range(ROWS):
        cells[pl.ds(a * WIDE, COLS), :] = pair[a].astype(F32)
    columns = cells[...].T
    columns_ref[...] = columns
    project(columns, mask, vectors[:, 0:1], vectors[:, 2:3], weight[...], send, send_ref, gate_ref)


def finish(home, source_rows, gain, bias, gate, columns, weight_out, got):
    got[pl.ds(0, 1024), :] = home[...].astype(F32)
    parts = []
    for m in range(GROUPS):
        lanes = slice(m * LANES, (m + 1) * LANES)
        triangle = source_rows(got, 0, m) + source_rows(got, 1, m)
        change = tn_dot(weight_out, norm_rows(triangle, gain, bias))
        parts.append(columns[:, lanes] + gate[:, lanes] * change)
    return jnp.concatenate(parts, axis=1).astype(BF16)


def rows_after_first(got, xh, m):
    return stack(
        got[pl.ds((xh * 2 + xl) * 16 + zh * 4 + m, 16, stride=64), :] for zh in range(4) for xl in range(2)
    )


def rows_after_second(got, yh, m):
    return stack(
        got[pl.ds(yh * 512 + x * 16 + zh * 4 + m, 8, stride=64), :] for zh in range(4) for x in range(4)
    )


def middle_kernel(
    home, gate, columns, vectors, mask, weight, weight_out, send_ref, gate_ref, columns_ref, got, send
):
    middle = finish(
        home, rows_after_first, vectors[:, 4:5], vectors[:, 6:7], gate, columns, weight_out[0], got
    ).astype(F32)
    columns_ref[...] = middle
    project(middle, mask, vectors[:, 1:2], vectors[:, 3:4], weight[1], send, send_ref, gate_ref)


def last_kernel(home, gate, columns, vectors, weight_out, out_ref, got, cells):
    updated = finish(
        home, rows_after_second, vectors[:, 5:6], vectors[:, 7:8], gate, columns, weight_out[1], got
    ).astype(F32)
    cells[...] = updated.T
    for a in range(ROWS):
        out_ref[a] = cells[pl.ds(a * WIDE, COLS), :].astype(BF16)


def send_home(triangle, out_ref, out_f):
    tiles = swap_groups([
        stack(
            triangle[((q * 4 + m) * 2 + yh) * 8 : ((q * 4 + m) * 2 + yh) * 8 + 8, x * 128 : x * 128 + 128]
            for m in range(GROUPS) for yh in range(2) for x in range(4)
        )
        for q in range(4)
    ])
    for m in range(GROUPS):
        for yh in range(2):
            for x in range(4):
                at = ((m * 2 + yh) * 4 + x) * 8
                for zh in range(4):
                    out_f[pl.ds(yh * 512 + x * 16 + zh * 4 + m, 8, stride=64), :] = tiles[zh][at : at + 8]
    out_ref[...] = out_f[pl.ds(0, 1024), :].astype(BF16)


def outgoing_kernel(mine, both, out_ref, mine_f, both_f, out_f):
    mine_f[pl.ds(0, 1024), :] = mine[...].astype(F32)
    both_f[pl.ds(0, 2048), :] = both[...].astype(F32)

    def matrix(source, base):
        tiles = swap_groups([
            stack(
                source[pl.ds(base + ((zh * 2 + xl) * 2 + yh) * 64 + m, 8, stride=8), :]
                for xl in range(2) for m in range(GROUPS) for yh in range(2)
            )
            for zh in range(4)
        ])
        half = tiles[0].shape[0] // 2
        return stack(jnp.concatenate([tile[:half], tile[half:]], axis=1) for tile in tiles).astype(BF16)

    left = matrix(mine_f, 0)
    right = stack(matrix(both_f, core * 1024 + 4) for core in range(2))
    triangle = nt_dot(left, right).astype(BF16)
    send_home(nn_dot(triangle, token_matrix()), out_ref, out_f)


def incoming_kernel(place, both, out_ref, both_f, out_f):
    both_f[pl.ds(0, 2048), :] = both[...].astype(F32)

    def matrix(base):
        tiles = swap_groups([
            stack(
                both_f[pl.ds(base + core * 1024 + (zh * 4 + x) * 64 + m, 8, stride=8), :]
                for x in range(4) for m in range(GROUPS) for core in range(2)
            )
            for zh in range(4)
        ])
        return stack(
            jnp.concatenate([tile[x * 64 : x * 64 + 64] for x in range(4)], axis=1) for tile in tiles
        ).astype(BF16)

    left = nn_dot(matrix(0), own_matrix(place[0:1, 0:1] & 1)).astype(BF16)
    send_home(tn_dot(left, matrix(4)), out_ref, out_f)


def call(kernel, outs, scratch, name, held=()):
    def run(*args):
        return pl.pallas_call(
            kernel,
            out_shape=outs,
            in_specs=[pl.BlockSpec(memory_space=pltpu.HBM if at in held else pltpu.VMEM) for at in range(len(args))],
            out_specs=jax.tree.map(lambda _: pl.BlockSpec(memory_space=pltpu.VMEM), outs),
            scratch_shapes=[pltpu.VMEM(entry, F32) if isinstance(entry, tuple) else entry for entry in scratch],
            compiler_params=pltpu.CompilerParams(vmem_limit_bytes=32 * 1024 * 1024),
            name=name,
        )(*args)

    return run


def in_hbm(array):
    return pltpu.with_memory_space_constraint(array, pltpu.HBM)


def exchange(array, axes):
    return lax.all_to_all(array, axes, 0, 0, tiled=True)


def on_device(pair_rep, chain_lengths, in_gain, in_bias, weight_in, out_gain, out_bias, weight_out):
    place = jnp.concatenate([
        jnp.full((8, LANES), lax.axis_index(axes), jnp.int32) for axes in (ROW_AXES, COL_AXES)
    ])
    tile = jax.ShapeDtypeStruct((LANES, CELLS), F32)
    sent = jax.ShapeDtypeStruct((1024, LANES), BF16)

    strided = (1024 + SPARE, LANES)
    small = (jax.ShapeDtypeStruct((LANES, 8), F32), jax.ShapeDtypeStruct((1, CELLS), F32))
    send, gate, columns, vectors, mask = call(
        first_kernel, (sent, tile, tile) + small, [
            (CELLS, LANES), strided, (8, LANES), pltpu.SMEM(chain_lengths.shape, jnp.int32),
            pltpu.VMEM(pair_rep.shape, BF16), in_gain.shape, in_bias.shape, out_gain.shape, out_bias.shape,
            pltpu.VMEM(weight_in.shape[1:], BF16), pltpu.SemaphoreType.DMA((7,)),
        ], "first", range(1, 8),
    )(place, *map(in_hbm, (chain_lengths, pair_rep, in_gain, in_bias, weight_in, out_gain, out_bias)))
    mine = exchange(send.reshape(128, 8, LANES), GROUP1).reshape(1024, LANES)
    both = lax.all_gather(mine, "core", axis=0, tiled=True)
    home = call(
        outgoing_kernel, sent, [strided, (2048 + SPARE, LANES), strided], "outgoing"
    )(mine, both)
    home = exchange(home.reshape(256, 4, LANES), BACK).reshape(1024, LANES)

    send, gate, columns = call(
        middle_kernel, (sent, tile, tile), [strided, strided], "middle"
    )(home, gate, columns, vectors, mask, weight_in, weight_out)
    mine = exchange(send.reshape(128, 8, LANES), GROUP2).reshape(1024, LANES)
    both = lax.all_gather(mine, "core", axis=0, tiled=True)
    home = call(
        incoming_kernel, sent, [(2048 + SPARE, LANES), strided], "incoming"
    )(place, both)
    home = exchange(home.reshape(256, 4, LANES), BACK).reshape(1024, LANES)

    out = jax.ShapeDtypeStruct(pair_rep.shape, BF16)
    return call(last_kernel, out, [strided, (CELLS, LANES)], "last")(home, gate, columns, vectors, weight_out)


def solution(mesh):
    fine = Mesh(mesh.devices.reshape(2, 4, 2, 2, 2, 2, 4), ROW_AXES + COL_AXES)
    placed = P(ROW_AXES, COL_AXES, None)
    return jax.shard_map(
        on_device, mesh=fine, in_specs=(placed,) + (P(),) * 7, out_specs=placed, check_vma=False
    )
```

```python
import jax
import jax.numpy as jnp
from jax import lax
from jax.experimental import pallas as pl
from jax.experimental.pallas import tpu as pltpu
from jax.sharding import Mesh, PartitionSpec as P

EPSILON = 1e-05
F32 = jnp.float32
BF16 = jnp.bfloat16

SPARE = 8
PITCH = 72

ROWS = 14
COLS = 28
WIDE = 32
CELLS = 512
GROUPS = 4
LANES = 128
SLOT = 112
CHAINS = 4

ROW_AXES = ("yh", "yl", "zl", "core")
COL_AXES = ("xh", "xl", "zh")
GROUP1 = ("zh", "xl", "yh", "yl", "zl")
GROUP2 = ("zh", "xh", "xl", "yl", "zl")
BACK = ("yh", "yl", "zl", "xh", "xl", "zh")


def nt_dot(left, right):
    return lax.dot_general(left, right, (((1,), (1,)), ((), ())), preferred_element_type=F32)


def tn_dot(left, right):
    return lax.dot_general(left, right, (((0,), (0,)), ((), ())), preferred_element_type=F32)


def nn_dot(left, right):
    return jnp.dot(left, right, preferred_element_type=F32)


def stack(pieces):
    return jnp.concatenate(list(pieces), axis=0)


def norm_rows(values, gain, bias):
    average = jnp.mean(values, axis=0, keepdims=True)
    centered = values - average
    variance = jnp.mean(centered * centered, axis=0, keepdims=True)
    return (centered * lax.rsqrt(variance + EPSILON) * gain + bias).astype(BF16)


def swap_groups(tiles):
    group = lax.broadcasted_iota(jnp.int32, tiles[0].shape, 1) >> 5
    for bit in (1, 2):
        keep = (group & bit) == 0
        out = list(tiles)
        for p in range(4):
            if p & bit == 0:
                low, high = tiles[p], tiles[p + bit]
                out[p] = jnp.where(keep, low, pltpu.roll(high, 32 * bit, 1))
                out[p + bit] = jnp.where(keep, pltpu.roll(low, LANES - 32 * bit, 1), high)
        tiles = out
    return tiles


def token_matrix():
    code = lax.broadcasted_iota(jnp.int32, (8, CELLS), 1)
    token = jnp.where(code & 31 < COLS, (code >> 5) * COLS + (code & 31), -4096)
    token = token - COLS * lax.broadcasted_iota(jnp.int32, (8, CELLS), 0)
    none = jnp.zeros((8, CELLS), F32)
    rows = []
    for core in range(2):
        for q in range(4):
            for m in range(GROUPS):
                for yh in range(2):
                    a = 4 * m + q
                    first = yh * 8 * COLS + core * ROWS + a
                    rows.append(jnp.where(token == first, 1.0, 0.0).astype(F32) if a < ROWS else none)
    return jnp.concatenate(rows, axis=0).astype(BF16)


def fields(code, *widths):
    out = []
    for width in reversed(widths):
        out.append(code & (width - 1))
        code = code >> (width.bit_length() - 1)
    return out[::-1]


def own_matrix(core):
    q, m, yh, s = fields(lax.broadcasted_iota(jnp.int32, (8, CELLS // 2), 1), 4, 4, 2, 8)
    a = 4 * m + q
    sub = lax.broadcasted_iota(jnp.int32, (8, CELLS // 2), 0)
    token = jnp.where(a < ROWS, ((yh * 8 + s) * 2 + core) * ROWS + a, -4096) - sub
    last = jnp.where(sub < COLS - 24, token, -4096)
    return jnp.concatenate([
        jnp.where((last if b == 24 else token) == c * COLS + b, 1.0, 0.0).astype(F32)
        for c in range(16) for b in range(0, WIDE, 8)
    ], axis=0).astype(BF16)


def valid_token(token, lengths_ref):
    valid = jnp.zeros(token.shape, jnp.bool_)
    for chain in range(CHAINS):
        start = chain * SLOT
        valid = valid | ((token >= start) & (token < start + lengths_ref[chain]))
    return valid


def cell_mask(place, lengths_ref):
    lane = lax.broadcasted_iota(jnp.int32, (1, CELLS), 1)
    a, b = lane >> 5, lane & 31
    row = valid_token(place[0:1, 0:1] * ROWS + a, lengths_ref)
    col = valid_token(place[8:9, 0:1] * COLS + b, lengths_ref)
    inside = (a < ROWS) & (b < COLS)
    return jnp.where(row & col & inside, 1.0, 0.0).astype(F32)


def project(columns, mask, gain, bias, weight, send, send_ref, gate_ref):
    for m in range(GROUPS):
        lanes = slice(m * LANES, (m + 1) * LANES)
        normed = norm_rows(columns[:, lanes], gain, bias)
        projected = tn_dot(weight, normed)
        weighting = mask[:, lanes]
        left = weighting * jax.nn.sigmoid(projected[128:256]) * projected[0:128]
        right = weighting * jax.nn.sigmoid(projected[384:512]) * projected[256:384]
        send[pl.ds(m, 128, stride=8), :] = left
        send[pl.ds(4 + m, 128, stride=8), :] = right
        gate_ref[:, lanes] = jax.nn.sigmoid(projected[512:640])
    send_ref[...] = send[pl.ds(0, 1024), :].astype(BF16)


def first_kernel(
    place, lengths_hbm, pair_hbm, in_gain_hbm, in_bias_hbm, weight_hbm, out_gain_hbm, out_bias_hbm,
    send_ref, gate_ref, columns_ref, vectors_ref, mask_ref, cells, send, norms, lengths, pair, in_gain, in_bias, out_gain, out_bias, weight, sems,
):
    copies = [
        pltpu.make_async_copy(source, target, sems.at[at])
        for at, (source, target) in enumerate((
            (pair_hbm, pair), (weight_hbm.at[0], weight), (in_gain_hbm, in_gain), (in_bias_hbm, in_bias),
            (out_gain_hbm, out_gain), (out_bias_hbm, out_bias), (lengths_hbm, lengths),
        ))
    ]
    for copy in copies:
        copy.start()
    cells[...] = jnp.zeros_like(cells)
    norms[...] = jnp.zeros_like(norms)
    for copy in copies:
        copy.wait()
    mask = cell_mask(place, lengths)
    mask_ref[...] = mask
    for at, pair_of in enumerate((in_gain, in_bias, out_gain, out_bias)):
        norms[pl.ds(2 * at, 2), :] = pair_of[...]
    vectors = norms[...].T
    vectors_ref[...] = vectors
    for a in range(ROWS):
        cells[pl.ds(a * WIDE, COLS), :] = pair[a].astype(F32)
    columns = cells[...].T
    columns_ref[...] = columns
    project(columns, mask, vectors[:, 0:1], vectors[:, 2:3], weight[...], send, send_ref, gate_ref)


def finish(home, source_rows, gain, bias, gate, columns, weight_out, got):
    for at in range(16):
        got[pl.ds(at * PITCH, 64), :] = home[pl.ds(at * 64, 64), :].astype(F32)
    parts = []
    for m in range(GROUPS):
        lanes = slice(m * LANES, (m + 1) * LANES)
        triangle = source_rows(got, 0, m) + source_rows(got, 1, m)
        change = tn_dot(weight_out, norm_rows(triangle, gain, bias))
        parts.append(columns[:, lanes] + gate[:, lanes] * change)
    return jnp.concatenate(parts, axis=1).astype(BF16)


def rows_after_first(got, xh, m):
    return stack(
        got[pl.ds((xh * 2 + xl) * 16 + zh * 4 + m, 16, stride=PITCH), :] for zh in range(4) for xl in range(2)
    )


def rows_after_second(got, yh, m):
    return stack(
        got[pl.ds(yh * 8 * PITCH + x * 16 + zh * 4 + m, 8, stride=PITCH), :] for zh in range(4) for x in range(4)
    )


def middle_kernel(
    home, gate, columns, vectors, mask, weight, weight_out, send_ref, gate_ref, columns_ref, got, send
):
    middle = finish(
        home, rows_after_first, vectors[:, 4:5], vectors[:, 6:7], gate, columns, weight_out[0], got
    ).astype(F32)
    columns_ref[...] = middle
    project(middle, mask, vectors[:, 1:2], vectors[:, 3:4], weight[1], send, send_ref, gate_ref)


def last_kernel(home, gate, columns, vectors, weight_out, out_ref, got, cells):
    updated = finish(
        home, rows_after_second, vectors[:, 5:6], vectors[:, 7:8], gate, columns, weight_out[1], got
    ).astype(F32)
    cells[...] = updated.T
    for a in range(ROWS):
        out_ref[a] = cells[pl.ds(a * WIDE, COLS), :].astype(BF16)


def send_home(triangle, out_ref, out_f):
    tiles = swap_groups([
        stack(
            triangle[((q * 4 + m) * 2 + yh) * 8 : ((q * 4 + m) * 2 + yh) * 8 + 8, x * 128 : x * 128 + 128]
            for m in range(GROUPS) for yh in range(2) for x in range(4)
        )
        for q in range(4)
    ])
    for m in range(GROUPS):
        for yh in range(2):
            for x in range(4):
                at = ((m * 2 + yh) * 4 + x) * 8
                for zh in range(4):
                    out_f[pl.ds(yh * 8 * PITCH + x * 16 + zh * 4 + m, 8, stride=PITCH), :] = tiles[zh][at : at + 8]
    for at in range(16):
        out_ref[pl.ds(at * 64, 64), :] = out_f[pl.ds(at * PITCH, 64), :].astype(BF16)


def outgoing_kernel(mine, both, out_ref, mine_f, both_f, out_f):
    mine_f[pl.ds(0, 1024), :] = mine[...].astype(F32)
    both_f[pl.ds(0, 2048), :] = both[...].astype(F32)

    def matrix(source, base):
        tiles = swap_groups([
            stack(
                source[pl.ds(base + ((zh * 2 + xl) * 2 + yh) * 64 + m, 8, stride=8), :]
                for xl in range(2) for m in range(GROUPS) for yh in range(2)
            )
            for zh in range(4)
        ])
        half = tiles[0].shape[0] // 2
        return stack(jnp.concatenate([tile[:half], tile[half:]], axis=1) for tile in tiles).astype(BF16)

    left = matrix(mine_f, 0)
    right = stack(matrix(both_f, core * 1024 + 4) for core in range(2))
    triangle = nt_dot(left, right).astype(BF16)
    send_home(nn_dot(triangle, token_matrix()), out_ref, out_f)


def incoming_kernel(place, both, out_ref, both_f, out_f):
    both_f[pl.ds(0, 2048), :] = both[...].astype(F32)

    def matrix(base):
        tiles = swap_groups([
            stack(
                both_f[pl.ds(base + core * 1024 + (zh * 4 + x) * 64 + m, 8, stride=8), :]
                for x in range(4) for m in range(GROUPS) for core in range(2)
            )
            for zh in range(4)
        ])
        return stack(
            jnp.concatenate([tile[x * 64 : x * 64 + 64] for x in range(4)], axis=1) for tile in tiles
        ).astype(BF16)

    left = nn_dot(matrix(0), own_matrix(place[0:1, 0:1] & 1)).astype(BF16)
    send_home(tn_dot(left, matrix(4)), out_ref, out_f)


def call(kernel, outs, scratch, name, held=()):
    def run(*args):
        return pl.pallas_call(
            kernel,
            out_shape=outs,
            in_specs=[pl.BlockSpec(memory_space=pltpu.HBM if at in held else pltpu.VMEM) for at in range(len(args))],
            out_specs=jax.tree.map(lambda _: pl.BlockSpec(memory_space=pltpu.VMEM), outs),
            scratch_shapes=[pltpu.VMEM(entry, F32) if isinstance(entry, tuple) else entry for entry in scratch],
            compiler_params=pltpu.CompilerParams(vmem_limit_bytes=32 * 1024 * 1024),
            name=name,
        )(*args)

    return run


def in_hbm(array):
    return pltpu.with_memory_space_constraint(array, pltpu.HBM)


def exchange(array, axes):
    return lax.all_to_all(array, axes, 0, 0, tiled=True)


def on_device(pair_rep, chain_lengths, in_gain, in_bias, weight_in, out_gain, out_bias, weight_out):
    place = jnp.concatenate([
        jnp.full((8, LANES), lax.axis_index(axes), jnp.int32) for axes in (ROW_AXES, COL_AXES)
    ])
    tile = jax.ShapeDtypeStruct((LANES, CELLS), F32)
    sent = jax.ShapeDtypeStruct((1024, LANES), BF16)

    strided, spread = (1024 + SPARE, LANES), (17 * PITCH, LANES)
    small = (jax.ShapeDtypeStruct((LANES, 8), F32), jax.ShapeDtypeStruct((1, CELLS), F32))
    send, gate, columns, vectors, mask = call(
        first_kernel, (sent, tile, tile) + small, [
            (CELLS, LANES), strided, (8, LANES), pltpu.SMEM(chain_lengths.shape, jnp.int32),
            pltpu.VMEM(pair_rep.shape, BF16), in_gain.shape, in_bias.shape, out_gain.shape, out_bias.shape,
            pltpu.VMEM(weight_in.shape[1:], BF16), pltpu.SemaphoreType.DMA((7,)),
        ], "first", range(1, 8),
    )(place, *map(in_hbm, (chain_lengths, pair_rep, in_gain, in_bias, weight_in, out_gain, out_bias)))
    mine = exchange(send.reshape(128, 8, LANES), GROUP1).reshape(1024, LANES)
    both = lax.all_gather(mine, "core", axis=0, tiled=True)
    home = call(
        outgoing_kernel, sent, [strided, (2048 + SPARE, LANES), spread], "outgoing"
    )(mine, both)
    home = exchange(home.reshape(256, 4, LANES), BACK).reshape(1024, LANES)

    send, gate, columns = call(
        middle_kernel, (sent, tile, tile), [spread, strided], "middle"
    )(home, gate, columns, vectors, mask, weight_in, weight_out)
    mine = exchange(send.reshape(128, 8, LANES), GROUP2).reshape(1024, LANES)
    both = lax.all_gather(mine, "core", axis=0, tiled=True)
    home = call(
        incoming_kernel, sent, [(2048 + SPARE, LANES), spread], "incoming"
    )(place, both)
    home = exchange(home.reshape(256, 4, LANES), BACK).reshape(1024, LANES)

    out = jax.ShapeDtypeStruct(pair_rep.shape, BF16)
    return call(last_kernel, out, [spread, (CELLS, LANES)], "last")(home, gate, columns, vectors, weight_out)


def solution(mesh):
    fine = Mesh(mesh.devices.reshape(2, 4, 2, 2, 2, 2, 4), ROW_AXES + COL_AXES)
    placed = P(ROW_AXES, COL_AXES, None)
    return jax.shard_map(
        on_device, mesh=fine, in_specs=(placed,) + (P(),) * 7, out_specs=placed, check_vma=False
    )
```

```python
import jax
import jax.numpy as jnp
from jax import lax
from jax.experimental import pallas as pl
from jax.experimental.pallas import tpu as pltpu
from jax.sharding import Mesh, PartitionSpec as P

EPSILON = 1e-05
F32 = jnp.float32
BF16 = jnp.bfloat16

SPARE = 8
PITCH = 72
WIDE_PITCH = 136

ROWS = 14
COLS = 28
WIDE = 32
CELLS = 512
GROUPS = 4
LANES = 128
SLOT = 112
CHAINS = 4

ROW_AXES = ("yh", "yl", "zl", "core")
COL_AXES = ("xh", "xl", "zh")
GROUP1 = ("zh", "xl", "yh", "yl", "zl")
GROUP2 = ("yl", "zl", "xh", "xl", "zh")
BACK = ("yh", "yl", "zl", "xh", "xl", "zh")


def nt_dot(left, right):
    return lax.dot_general(left, right, (((1,), (1,)), ((), ())), preferred_element_type=F32)


def tn_dot(left, right):
    return lax.dot_general(left, right, (((0,), (0,)), ((), ())), preferred_element_type=F32)


def nn_dot(left, right):
    return jnp.dot(left, right, preferred_element_type=F32)


def stack(pieces):
    return jnp.concatenate(list(pieces), axis=0)


def norm_rows(values, gain, bias):
    average = jnp.mean(values, axis=0, keepdims=True)
    centered = values - average
    variance = jnp.mean(centered * centered, axis=0, keepdims=True)
    return (centered * lax.rsqrt(variance + EPSILON) * gain + bias).astype(BF16)


def swap_groups(tiles):
    group = lax.broadcasted_iota(jnp.int32, tiles[0].shape, 1) >> 5
    for bit in (1, 2):
        keep = (group & bit) == 0
        out = list(tiles)
        for p in range(4):
            if p & bit == 0:
                low, high = tiles[p], tiles[p + bit]
                out[p] = jnp.where(keep, low, pltpu.roll(high, 32 * bit, 1))
                out[p + bit] = jnp.where(keep, pltpu.roll(low, LANES - 32 * bit, 1), high)
        tiles = out
    return tiles


def token_matrix():
    code = lax.broadcasted_iota(jnp.int32, (8, CELLS), 1)
    token = jnp.where(code & 31 < COLS, (code >> 5) * COLS + (code & 31), -4096)
    token = token - COLS * lax.broadcasted_iota(jnp.int32, (8, CELLS), 0)
    none = jnp.zeros((8, CELLS), F32)
    rows = []
    for core in range(2):
        for q in range(4):
            for m in range(GROUPS):
                for yh in range(2):
                    a = 4 * m + q
                    first = yh * 8 * COLS + core * ROWS + a
                    rows.append(jnp.where(token == first, 1.0, 0.0).astype(F32) if a < ROWS else none)
    return jnp.concatenate(rows, axis=0).astype(BF16)


def fields(code, *widths):
    out = []
    for width in reversed(widths):
        out.append(code & (width - 1))
        code = code >> (width.bit_length() - 1)
    return out[::-1]


def own_matrix(core):
    q, m, yh, s = fields(lax.broadcasted_iota(jnp.int32, (8, CELLS // 2), 1), 4, 4, 2, 8)
    a = 4 * m + q
    sub = lax.broadcasted_iota(jnp.int32, (8, CELLS // 2), 0)
    token = jnp.where(a < ROWS, ((yh * 8 + s) * 2 + core) * ROWS + a, -4096) - sub
    last = jnp.where(sub < COLS - 24, token, -4096)
    return jnp.concatenate([
        jnp.where((last if b == 24 else token) == c * COLS + b, 1.0, 0.0).astype(F32)
        for c in range(16) for b in range(0, WIDE, 8)
    ], axis=0).astype(BF16)


def valid_token(token, lengths_ref):
    valid = jnp.zeros(token.shape, jnp.bool_)
    for chain in range(CHAINS):
        start = chain * SLOT
        valid = valid | ((token >= start) & (token < start + lengths_ref[chain]))
    return valid


def cell_mask(place, lengths_ref):
    lane = lax.broadcasted_iota(jnp.int32, (1, CELLS), 1)
    a, b = lane >> 5, lane & 31
    row = valid_token(place[0:1, 0:1] * ROWS + a, lengths_ref)
    col = valid_token(place[8:9, 0:1] * COLS + b, lengths_ref)
    inside = (a < ROWS) & (b < COLS)
    return jnp.where(row & col & inside, 1.0, 0.0).astype(F32)


def store_in_order(send, values, row):
    send[pl.ds(row, 128, stride=8), :] = values


def store_across(send, values, row):
    for at in range(16):
        start = (at % 4 * 4 + at // 4) * 8 + row
        send[pl.ds(start, 8, stride=WIDE_PITCH), :] = values[at * 8 : at * 8 + 8]


def project(columns, mask, gain, bias, weight, store, send, gate_ref):
    for m in range(GROUPS):
        lanes = slice(m * LANES, (m + 1) * LANES)
        normed = norm_rows(columns[:, lanes], gain, bias)
        projected = tn_dot(weight, normed)
        weighting = mask[:, lanes]
        left = weighting * jax.nn.sigmoid(projected[128:256]) * projected[0:128]
        right = weighting * jax.nn.sigmoid(projected[384:512]) * projected[256:384]
        store(send, left, m)
        store(send, right, 4 + m)
        gate_ref[:, lanes] = jax.nn.sigmoid(projected[512:640])


def first_kernel(
    place, lengths_hbm, pair_hbm, in_gain_hbm, in_bias_hbm, weight_hbm, out_gain_hbm, out_bias_hbm,
    send_ref, gate_ref, columns_ref, vectors_ref, mask_ref, cells, send, norms, lengths, pair, in_gain, in_bias, out_gain, out_bias, weight, sems,
):
    copies = [
        pltpu.make_async_copy(source, target, sems.at[at])
        for at, (source, target) in enumerate((
            (pair_hbm, pair), (weight_hbm.at[0], weight), (in_gain_hbm, in_gain), (in_bias_hbm, in_bias),
            (out_gain_hbm, out_gain), (out_bias_hbm, out_bias), (lengths_hbm, lengths),
        ))
    ]
    for copy in copies:
        copy.start()
    cells[...] = jnp.zeros_like(cells)
    norms[...] = jnp.zeros_like(norms)
    for copy in copies:
        copy.wait()
    mask = cell_mask(place, lengths)
    mask_ref[...] = mask
    for at, pair_of in enumerate((in_gain, in_bias, out_gain, out_bias)):
        norms[pl.ds(2 * at, 2), :] = pair_of[...]
    vectors = norms[...].T
    vectors_ref[...] = vectors
    for a in range(ROWS):
        cells[pl.ds(a * WIDE, COLS), :] = pair[a].astype(F32)
    columns = cells[...].T
    columns_ref[...] = columns
    project(columns, mask, vectors[:, 0:1], vectors[:, 2:3], weight[...], store_in_order, send, gate_ref)
    send_ref[...] = send[pl.ds(0, 1024), :].astype(BF16)


def finish(home, source_rows, gain, bias, gate, columns, weight_out, got):
    for at in range(16):
        got[pl.ds(at * PITCH, 64), :] = home[pl.ds(at * 64, 64), :].astype(F32)
    parts = []
    for m in range(GROUPS):
        lanes = slice(m * LANES, (m + 1) * LANES)
        triangle = source_rows(got, 0, m) + source_rows(got, 1, m)
        change = tn_dot(weight_out, norm_rows(triangle, gain, bias))
        parts.append(columns[:, lanes] + gate[:, lanes] * change)
    return jnp.concatenate(parts, axis=1).astype(BF16)


def rows_after_first(got, xh, m):
    return stack(
        got[pl.ds((xh * 2 + xl) * 16 + zh * 4 + m, 16, stride=PITCH), :] for zh in range(4) for xl in range(2)
    )


def rows_after_second(got, yh, m):
    return stack(
        got[pl.ds(yh * 8 * PITCH + x * 16 + zh * 4 + m, 8, stride=PITCH), :] for zh in range(4) for x in range(4)
    )


def middle_kernel(
    home, gate, columns, vectors, mask, weight, weight_out, send_ref, gate_ref, columns_ref, got, send
):
    middle = finish(
        home, rows_after_first, vectors[:, 4:5], vectors[:, 6:7], gate, columns, weight_out[0], got
    ).astype(F32)
    columns_ref[...] = middle
    project(middle, mask, vectors[:, 1:2], vectors[:, 3:4], weight[1], store_across, send, gate_ref)
    for at in range(8):
        send_ref[pl.ds(at * 128, 128), :] = send[pl.ds(at * WIDE_PITCH, 128), :].astype(BF16)


def last_kernel(home, gate, columns, vectors, weight_out, out_ref, got, cells):
    updated = finish(
        home, rows_after_second, vectors[:, 5:6], vectors[:, 7:8], gate, columns, weight_out[1], got
    ).astype(F32)
    cells[...] = updated.T
    for a in range(ROWS):
        out_ref[a] = cells[pl.ds(a * WIDE, COLS), :].astype(BF16)


def send_home(triangle, out_ref, out_f):
    tiles = swap_groups([
        stack(
            triangle[((q * 4 + m) * 2 + yh) * 8 : ((q * 4 + m) * 2 + yh) * 8 + 8, x * 128 : x * 128 + 128]
            for m in range(GROUPS) for yh in range(2) for x in range(4)
        )
        for q in range(4)
    ])
    for m in range(GROUPS):
        for yh in range(2):
            for x in range(4):
                at = ((m * 2 + yh) * 4 + x) * 8
                for zh in range(4):
                    out_f[pl.ds(yh * 8 * PITCH + x * 16 + zh * 4 + m, 8, stride=PITCH), :] = tiles[zh][at : at + 8]
    for at in range(16):
        out_ref[pl.ds(at * 64, 64), :] = out_f[pl.ds(at * PITCH, 64), :].astype(BF16)


def outgoing_kernel(mine, both, out_ref, mine_f, both_f, out_f):
    mine_f[pl.ds(0, 1024), :] = mine[...].astype(F32)
    both_f[pl.ds(0, 2048), :] = both[...].astype(F32)

    def matrix(source, base):
        tiles = swap_groups([
            stack(
                source[pl.ds(base + ((zh * 2 + xl) * 2 + yh) * 64 + m, 8, stride=8), :]
                for xl in range(2) for m in range(GROUPS) for yh in range(2)
            )
            for zh in range(4)
        ])
        half = tiles[0].shape[0] // 2
        return stack(jnp.concatenate([tile[:half], tile[half:]], axis=1) for tile in tiles).astype(BF16)

    left = matrix(mine_f, 0)
    right = stack(matrix(both_f, core * 1024 + 4) for core in range(2))
    triangle = nt_dot(left, right).astype(BF16)
    send_home(nn_dot(triangle, token_matrix()), out_ref, out_f)


def incoming_kernel(place, both, out_ref, both_f, out_f):
    for at in range(16):
        both_f[pl.ds(at * WIDE_PITCH, 128), :] = both[pl.ds(at * 128, 128), :].astype(F32)

    def matrix(base):
        tiles = swap_groups([
            stack(
                both_f[pl.ds(base + core * 8 * WIDE_PITCH + (x * 4 + zh) * 8 + m, 8, stride=WIDE_PITCH), :]
                for x in range(4) for m in range(GROUPS) for core in range(2)
            )
            for zh in range(4)
        ])
        return stack(
            jnp.concatenate([tile[x * 64 : x * 64 + 64] for x in range(4)], axis=1) for tile in tiles
        ).astype(BF16)

    left = nn_dot(matrix(0), own_matrix(place[0:1, 0:1] & 1)).astype(BF16)
    send_home(tn_dot(left, matrix(4)), out_ref, out_f)


def call(kernel, outs, scratch, name, held=()):
    def run(*args):
        return pl.pallas_call(
            kernel,
            out_shape=outs,
            in_specs=[pl.BlockSpec(memory_space=pltpu.HBM if at in held else pltpu.VMEM) for at in range(len(args))],
            out_specs=jax.tree.map(lambda _: pl.BlockSpec(memory_space=pltpu.VMEM), outs),
            scratch_shapes=[pltpu.VMEM(entry, F32) if isinstance(entry, tuple) else entry for entry in scratch],
            compiler_params=pltpu.CompilerParams(vmem_limit_bytes=32 * 1024 * 1024),
            name=name,
        )(*args)

    return run


def in_hbm(array):
    return pltpu.with_memory_space_constraint(array, pltpu.HBM)


def exchange(array, axes):
    return lax.all_to_all(array, axes, 0, 0, tiled=True)


def on_device(pair_rep, chain_lengths, in_gain, in_bias, weight_in, out_gain, out_bias, weight_out):
    place = jnp.concatenate([
        jnp.full((8, LANES), lax.axis_index(axes), jnp.int32) for axes in (ROW_AXES, COL_AXES)
    ])
    tile = jax.ShapeDtypeStruct((LANES, CELLS), F32)
    sent = jax.ShapeDtypeStruct((1024, LANES), BF16)

    strided, spread = (1024 + SPARE, LANES), (17 * PITCH, LANES)
    small = (jax.ShapeDtypeStruct((LANES, 8), F32), jax.ShapeDtypeStruct((1, CELLS), F32))
    send, gate, columns, vectors, mask = call(
        first_kernel, (sent, tile, tile) + small, [
            (CELLS, LANES), strided, (8, LANES), pltpu.SMEM(chain_lengths.shape, jnp.int32),
            pltpu.VMEM(pair_rep.shape, BF16), in_gain.shape, in_bias.shape, out_gain.shape, out_bias.shape,
            pltpu.VMEM(weight_in.shape[1:], BF16), pltpu.SemaphoreType.DMA((7,)),
        ], "first", range(1, 8),
    )(place, *map(in_hbm, (chain_lengths, pair_rep, in_gain, in_bias, weight_in, out_gain, out_bias)))
    mine = exchange(send.reshape(128, 8, LANES), GROUP1).reshape(1024, LANES)
    both = lax.all_gather(mine, "core", axis=0, tiled=True)
    home = call(
        outgoing_kernel, sent, [strided, (2048 + SPARE, LANES), spread], "outgoing"
    )(mine, both)
    home = exchange(home.reshape(256, 4, LANES), BACK).reshape(1024, LANES)

    send, gate, columns = call(
        middle_kernel, (sent, tile, tile), [spread, (9 * WIDE_PITCH, LANES)], "middle"
    )(home, gate, columns, vectors, mask, weight_in, weight_out)
    mine = exchange(send.reshape(128, 8, LANES), GROUP2).reshape(1024, LANES)
    both = lax.all_gather(mine, "core", axis=0, tiled=True)
    home = call(
        incoming_kernel, sent, [(17 * WIDE_PITCH, LANES), spread], "incoming"
    )(place, both)
    home = exchange(home.reshape(256, 4, LANES), BACK).reshape(1024, LANES)

    out = jax.ShapeDtypeStruct(pair_rep.shape, BF16)
    return call(last_kernel, out, [spread, (CELLS, LANES)], "last")(home, gate, columns, vectors, weight_out)


def solution(mesh):
    fine = Mesh(mesh.devices.reshape(2, 4, 2, 2, 2, 2, 4), ROW_AXES + COL_AXES)
    placed = P(ROW_AXES, COL_AXES, None)
    return jax.shard_map(
        on_device, mesh=fine, in_specs=(placed,) + (P(),) * 7, out_specs=placed, check_vma=False
    )
```

```python
import jax
import jax.numpy as jnp
from jax import lax
from jax.experimental import pallas as pl
from jax.experimental.pallas import tpu as pltpu
from jax.sharding import Mesh, PartitionSpec as P

EPSILON = 1e-05
F32 = jnp.float32
BF16 = jnp.bfloat16

SPARE = 8
PITCH = 72

ROWS = 14
COLS = 28
WIDE = 32
CELLS = 512
GROUPS = 4
LANES = 128
SLOT = 112
CHAINS = 4

ROW_AXES = ("yh", "yl", "zl", "core")
COL_AXES = ("xh", "xl", "zh")
GROUP1 = ("yh", "yl", "zl", "xl", "zh")
GROUP2 = ("zh", "xh", "xl", "yl", "zl")
BACK = ("yh", "yl", "zl", "xh", "xl", "zh")


def nt_dot(left, right):
    return lax.dot_general(left, right, (((1,), (1,)), ((), ())), preferred_element_type=F32)


def tn_dot(left, right):
    return lax.dot_general(left, right, (((0,), (0,)), ((), ())), preferred_element_type=F32)


def nn_dot(left, right):
    return jnp.dot(left, right, preferred_element_type=F32)


def stack(pieces):
    return jnp.concatenate(list(pieces), axis=0)


def norm_rows(values, gain, bias):
    average = jnp.mean(values, axis=0, keepdims=True)
    centered = values - average
    variance = jnp.mean(centered * centered, axis=0, keepdims=True)
    return (centered * lax.rsqrt(variance + EPSILON) * gain + bias).astype(BF16)


def swap_groups(tiles):
    group = lax.broadcasted_iota(jnp.int32, tiles[0].shape, 1) >> 5
    for bit in (1, 2):
        keep = (group & bit) == 0
        out = list(tiles)
        for p in range(4):
            if p & bit == 0:
                low, high = tiles[p], tiles[p + bit]
                out[p] = jnp.where(keep, low, pltpu.roll(high, 32 * bit, 1))
                out[p + bit] = jnp.where(keep, pltpu.roll(low, LANES - 32 * bit, 1), high)
        tiles = out
    return tiles


def token_matrix():
    code = lax.broadcasted_iota(jnp.int32, (8, CELLS), 1)
    token = jnp.where(code & 31 < COLS, (code >> 5) * COLS + (code & 31), -4096)
    token = token - COLS * lax.broadcasted_iota(jnp.int32, (8, CELLS), 0)
    none = jnp.zeros((8, CELLS), F32)
    rows = []
    for core in range(2):
        for q in range(4):
            for m in range(GROUPS):
                for yh in range(2):
                    a = 4 * m + q
                    first = yh * 8 * COLS + core * ROWS + a
                    rows.append(jnp.where(token == first, 1.0, 0.0).astype(F32) if a < ROWS else none)
    return jnp.concatenate(rows, axis=0).astype(BF16)


def fields(code, *widths):
    out = []
    for width in reversed(widths):
        out.append(code & (width - 1))
        code = code >> (width.bit_length() - 1)
    return out[::-1]


def own_matrix(core):
    q, m, yh, s = fields(lax.broadcasted_iota(jnp.int32, (8, CELLS // 2), 1), 4, 4, 2, 8)
    a = 4 * m + q
    sub = lax.broadcasted_iota(jnp.int32, (8, CELLS // 2), 0)
    token = jnp.where(a < ROWS, ((yh * 8 + s) * 2 + core) * ROWS + a, -4096) - sub
    last = jnp.where(sub < COLS - 24, token, -4096)
    return jnp.concatenate([
        jnp.where((last if b == 24 else token) == c * COLS + b, 1.0, 0.0).astype(F32)
        for c in range(16) for b in range(0, WIDE, 8)
    ], axis=0).astype(BF16)


def valid_token(token, lengths_ref):
    valid = jnp.zeros(token.shape, jnp.bool_)
    for chain in range(CHAINS):
        start = chain * SLOT
        valid = valid | ((token >= start) & (token < start + lengths_ref[chain]))
    return valid


def cell_mask(place, lengths_ref):
    lane = lax.broadcasted_iota(jnp.int32, (1, CELLS), 1)
    a, b = lane >> 5, lane & 31
    row = valid_token(place[0:1, 0:1] * ROWS + a, lengths_ref)
    col = valid_token(place[8:9, 0:1] * COLS + b, lengths_ref)
    inside = (a < ROWS) & (b < COLS)
    return jnp.where(row & col & inside, 1.0, 0.0).astype(F32)


def store_across(send, values, row):
    for zh in range(4):
        for xl in range(2):
            start, at = (xl * 4 + zh) * 8 + row, (zh * 2 + xl) * 16
            send[pl.ds(start, 16, stride=PITCH), :] = values[at : at + 16]


def store_in_order(send, values, row):
    send[pl.ds(row, 128, stride=8), :] = values


def project(columns, mask, gain, bias, weight, store, send, gate_ref):
    for m in range(GROUPS):
        lanes = slice(m * LANES, (m + 1) * LANES)
        normed = norm_rows(columns[:, lanes], gain, bias)
        projected = tn_dot(weight, normed)
        weighting = mask[:, lanes]
        left = weighting * jax.nn.sigmoid(projected[128:256]) * projected[0:128]
        right = weighting * jax.nn.sigmoid(projected[384:512]) * projected[256:384]
        store(send, left, m)
        store(send, right, 4 + m)
        gate_ref[:, lanes] = jax.nn.sigmoid(projected[512:640])


def first_kernel(
    place, lengths_hbm, pair_hbm, in_gain_hbm, in_bias_hbm, weight_hbm, out_gain_hbm, out_bias_hbm,
    send_ref, gate_ref, columns_ref, vectors_ref, mask_ref, cells, send, norms, lengths, pair, in_gain, in_bias, out_gain, out_bias, weight, sems,
):
    copies = [
        pltpu.make_async_copy(source, target, sems.at[at])
        for at, (source, target) in enumerate((
            (pair_hbm, pair), (weight_hbm.at[0], weight), (in_gain_hbm, in_gain), (in_bias_hbm, in_bias),
            (out_gain_hbm, out_gain), (out_bias_hbm, out_bias), (lengths_hbm, lengths),
        ))
    ]
    for copy in copies:
        copy.start()
    cells[...] = jnp.zeros_like(cells)
    norms[...] = jnp.zeros_like(norms)
    for copy in copies:
        copy.wait()
    mask = cell_mask(place, lengths)
    mask_ref[...] = mask
    for at, pair_of in enumerate((in_gain, in_bias, out_gain, out_bias)):
        norms[pl.ds(2 * at, 2), :] = pair_of[...]
    vectors = norms[...].T
    vectors_ref[...] = vectors
    for a in range(ROWS):
        cells[pl.ds(a * WIDE, COLS), :] = pair[a].astype(F32)
    columns = cells[...].T
    columns_ref[...] = columns
    project(columns, mask, vectors[:, 0:1], vectors[:, 2:3], weight[...], store_across, send, gate_ref)
    for at in range(16):
        send_ref[pl.ds(at * 64, 64), :] = send[pl.ds(at * PITCH, 64), :].astype(BF16)


def finish(home, source_rows, gain, bias, gate, columns, weight_out, got):
    for at in range(16):
        got[pl.ds(at * PITCH, 64), :] = home[pl.ds(at * 64, 64), :].astype(F32)
    parts = []
    for m in range(GROUPS):
        lanes = slice(m * LANES, (m + 1) * LANES)
        triangle = source_rows(got, 0, m) + source_rows(got, 1, m)
        change = tn_dot(weight_out, norm_rows(triangle, gain, bias))
        parts.append(columns[:, lanes] + gate[:, lanes] * change)
    return jnp.concatenate(parts, axis=1).astype(BF16)


def rows_after_first(got, xh, m):
    return stack(
        got[pl.ds((xh * 2 + xl) * 16 + zh * 4 + m, 16, stride=PITCH), :] for zh in range(4) for xl in range(2)
    )


def rows_after_second(got, yh, m):
    return stack(
        got[pl.ds(yh * 8 * PITCH + x * 16 + zh * 4 + m, 8, stride=PITCH), :] for zh in range(4) for x in range(4)
    )


def middle_kernel(
    home, gate, columns, vectors, mask, weight, weight_out, send_ref, gate_ref, columns_ref, got, send
):
    middle = finish(
        home, rows_after_first, vectors[:, 4:5], vectors[:, 6:7], gate, columns, weight_out[0], got
    ).astype(F32)
    columns_ref[...] = middle
    project(middle, mask, vectors[:, 1:2], vectors[:, 3:4], weight[1], store_in_order, send, gate_ref)
    send_ref[...] = send[pl.ds(0, 1024), :].astype(BF16)


def last_kernel(home, gate, columns, vectors, weight_out, out_ref, got, cells):
    updated = finish(
        home, rows_after_second, vectors[:, 5:6], vectors[:, 7:8], gate, columns, weight_out[1], got
    ).astype(F32)
    cells[...] = updated.T
    for a in range(ROWS):
        out_ref[a] = cells[pl.ds(a * WIDE, COLS), :].astype(BF16)


def send_home(triangle, out_ref, out_f):
    tiles = swap_groups([
        stack(
            triangle[((q * 4 + m) * 2 + yh) * 8 : ((q * 4 + m) * 2 + yh) * 8 + 8, x * 128 : x * 128 + 128]
            for m in range(GROUPS) for yh in range(2) for x in range(4)
        )
        for q in range(4)
    ])
    for m in range(GROUPS):
        for yh in range(2):
            for x in range(4):
                at = ((m * 2 + yh) * 4 + x) * 8
                for zh in range(4):
                    out_f[pl.ds(yh * 8 * PITCH + x * 16 + zh * 4 + m, 8, stride=PITCH), :] = tiles[zh][at : at + 8]
    for at in range(16):
        out_ref[pl.ds(at * 64, 64), :] = out_f[pl.ds(at * PITCH, 64), :].astype(BF16)


def outgoing_kernel(mine, both, out_ref, mine_f, both_f, out_f):
    for at in range(16):
        mine_f[pl.ds(at * PITCH, 64), :] = mine[pl.ds(at * 64, 64), :].astype(F32)
    for at in range(32):
        both_f[pl.ds(at * PITCH, 64), :] = both[pl.ds(at * 64, 64), :].astype(F32)

    def matrix(source, base):
        tiles = swap_groups([
            stack(
                source[pl.ds(base + yh * 8 * PITCH + (xl * 4 + zh) * 8 + m, 8, stride=PITCH), :]
                for xl in range(2) for m in range(GROUPS) for yh in range(2)
            )
            for zh in range(4)
        ])
        half = tiles[0].shape[0] // 2
        return stack(jnp.concatenate([tile[:half], tile[half:]], axis=1) for tile in tiles).astype(BF16)

    left = matrix(mine_f, 0)
    right = stack(matrix(both_f, core * 16 * PITCH + 4) for core in range(2))
    triangle = nt_dot(left, right).astype(BF16)
    send_home(nn_dot(triangle, token_matrix()), out_ref, out_f)


def incoming_kernel(place, both, out_ref, both_f, out_f):
    both_f[pl.ds(0, 2048), :] = both[...].astype(F32)

    def matrix(base):
        tiles = swap_groups([
            stack(
                both_f[pl.ds(base + core * 1024 + (zh * 4 + x) * 64 + m, 8, stride=8), :]
                for x in range(4) for m in range(GROUPS) for core in range(2)
            )
            for zh in range(4)
        ])
        return stack(
            jnp.concatenate([tile[x * 64 : x * 64 + 64] for x in range(4)], axis=1) for tile in tiles
        ).astype(BF16)

    left = nn_dot(matrix(0), own_matrix(place[0:1, 0:1] & 1)).astype(BF16)
    send_home(tn_dot(left, matrix(4)), out_ref, out_f)


def call(kernel, outs, scratch, name, held=()):
    def run(*args):
        return pl.pallas_call(
            kernel,
            out_shape=outs,
            in_specs=[pl.BlockSpec(memory_space=pltpu.HBM if at in held else pltpu.VMEM) for at in range(len(args))],
            out_specs=jax.tree.map(lambda _: pl.BlockSpec(memory_space=pltpu.VMEM), outs),
            scratch_shapes=[pltpu.VMEM(entry, F32) if isinstance(entry, tuple) else entry for entry in scratch],
            compiler_params=pltpu.CompilerParams(vmem_limit_bytes=32 * 1024 * 1024),
            name=name,
        )(*args)

    return run


def in_hbm(array):
    return pltpu.with_memory_space_constraint(array, pltpu.HBM)


def exchange(array, axes):
    return lax.all_to_all(array, axes, 0, 0, tiled=True)


def on_device(pair_rep, chain_lengths, in_gain, in_bias, weight_in, out_gain, out_bias, weight_out):
    place = jnp.concatenate([
        jnp.full((8, LANES), lax.axis_index(axes), jnp.int32) for axes in (ROW_AXES, COL_AXES)
    ])
    tile = jax.ShapeDtypeStruct((LANES, CELLS), F32)
    sent = jax.ShapeDtypeStruct((1024, LANES), BF16)

    strided, spread = (1024 + SPARE, LANES), (17 * PITCH, LANES)
    small = (jax.ShapeDtypeStruct((LANES, 8), F32), jax.ShapeDtypeStruct((1, CELLS), F32))
    send, gate, columns, vectors, mask = call(
        first_kernel, (sent, tile, tile) + small, [
            (CELLS, LANES), spread, (8, LANES), pltpu.SMEM(chain_lengths.shape, jnp.int32),
            pltpu.VMEM(pair_rep.shape, BF16), in_gain.shape, in_bias.shape, out_gain.shape, out_bias.shape,
            pltpu.VMEM(weight_in.shape[1:], BF16), pltpu.SemaphoreType.DMA((7,)),
        ], "first", range(1, 8),
    )(place, *map(in_hbm, (chain_lengths, pair_rep, in_gain, in_bias, weight_in, out_gain, out_bias)))
    mine = exchange(send.reshape(128, 8, LANES), GROUP1).reshape(1024, LANES)
    both = lax.all_gather(mine, "core", axis=0, tiled=True)
    home = call(
        outgoing_kernel, sent, [spread, (33 * PITCH, LANES), spread], "outgoing"
    )(mine, both)
    home = exchange(home.reshape(256, 4, LANES), BACK).reshape(1024, LANES)

    send, gate, columns = call(
        middle_kernel, (sent, tile, tile), [spread, strided], "middle"
    )(home, gate, columns, vectors, mask, weight_in, weight_out)
    mine = exchange(send.reshape(128, 8, LANES), GROUP2).reshape(1024, LANES)
    both = lax.all_gather(mine, "core", axis=0, tiled=True)
    home = call(
        incoming_kernel, sent, [(2048 + SPARE, LANES), spread], "incoming"
    )(place, both)
    home = exchange(home.reshape(256, 4, LANES), BACK).reshape(1024, LANES)

    out = jax.ShapeDtypeStruct(pair_rep.shape, BF16)
    return call(last_kernel, out, [spread, (CELLS, LANES)], "last")(home, gate, columns, vectors, weight_out)


def solution(mesh):
    fine = Mesh(mesh.devices.reshape(2, 4, 2, 2, 2, 2, 4), ROW_AXES + COL_AXES)
    placed = P(ROW_AXES, COL_AXES, None)
    return jax.shard_map(
        on_device, mesh=fine, in_specs=(placed,) + (P(),) * 7, out_specs=placed, check_vma=False
    )
```

```python
import jax
import jax.numpy as jnp
from jax import lax
from jax.experimental import pallas as pl
from jax.experimental.pallas import tpu as pltpu
from jax.sharding import Mesh, PartitionSpec as P

EPSILON = 1e-05
F32 = jnp.float32
BF16 = jnp.bfloat16

SPARE = 8
PITCH = 72

ROWS = 14
COLS = 28
WIDE = 32
CELLS = 512
GROUPS = 4
LANES = 128
SLOT = 112
CHAINS = 4

ROW_AXES = ("yh", "yl", "zl", "core")
COL_AXES = ("xh", "xl", "zh")
GROUP1 = ("zh", "xl", "yh", "yl", "zl")
GROUP2 = ("zh", "xh", "xl", "yl", "zl")
BACK = ("yh", "yl", "zl", "xh", "xl", "zh")


def nt_dot(left, right):
    return lax.dot_general(left, right, (((1,), (1,)), ((), ())), preferred_element_type=F32)


def tn_dot(left, right):
    return lax.dot_general(left, right, (((0,), (0,)), ((), ())), preferred_element_type=F32)


def nn_dot(left, right):
    return jnp.dot(left, right, preferred_element_type=F32)


def stack(pieces):
    return jnp.concatenate(list(pieces), axis=0)


def norm_rows(values, gain, bias):
    average = jnp.mean(values, axis=0, keepdims=True)
    centered = values - average
    variance = jnp.mean(centered * centered, axis=0, keepdims=True)
    return (centered * lax.rsqrt(variance + EPSILON) * gain + bias).astype(BF16)


def swap_groups(tiles):
    group = lax.broadcasted_iota(jnp.int32, tiles[0].shape, 1) >> 5
    for bit in (1, 2):
        keep = (group & bit) == 0
        out = list(tiles)
        for p in range(4):
            if p & bit == 0:
                low, high = tiles[p], tiles[p + bit]
                out[p] = jnp.where(keep, low, pltpu.roll(high, 32 * bit, 1))
                out[p + bit] = jnp.where(keep, pltpu.roll(low, LANES - 32 * bit, 1), high)
        tiles = out
    return tiles


def token_matrix():
    code = lax.broadcasted_iota(jnp.int32, (8, CELLS), 1)
    token = jnp.where(code & 31 < COLS, (code >> 5) * COLS + (code & 31), -4096)
    token = token - COLS * lax.broadcasted_iota(jnp.int32, (8, CELLS), 0)
    none = jnp.zeros((8, CELLS), F32)
    rows = []
    for core in range(2):
        for q in range(4):
            for m in range(GROUPS):
                for yh in range(2):
                    a = 4 * m + q
                    first = yh * 8 * COLS + core * ROWS + a
                    rows.append(jnp.where(token == first, 1.0, 0.0).astype(F32) if a < ROWS else none)
    return jnp.concatenate(rows, axis=0).astype(BF16)


def fields(code, *widths):
    out = []
    for width in reversed(widths):
        out.append(code & (width - 1))
        code = code >> (width.bit_length() - 1)
    return out[::-1]


def own_matrix(core):
    q, m, yh, s = fields(lax.broadcasted_iota(jnp.int32, (8, CELLS // 2), 1), 4, 4, 2, 8)
    a = 4 * m + q
    sub = lax.broadcasted_iota(jnp.int32, (8, CELLS // 2), 0)
    token = jnp.where(a < ROWS, ((yh * 8 + s) * 2 + core) * ROWS + a, -4096) - sub
    last = jnp.where(sub < COLS - 24, token, -4096)
    return jnp.concatenate([
        jnp.where((last if b == 24 else token) == c * COLS + b, 1.0, 0.0).astype(F32)
        for c in range(16) for b in range(0, WIDE, 8)
    ], axis=0).astype(BF16)


def valid_token(token, lengths_ref):
    valid = jnp.zeros(token.shape, jnp.bool_)
    for chain in range(CHAINS):
        start = chain * SLOT
        valid = valid | ((token >= start) & (token < start + lengths_ref[chain]))
    return valid


def cell_mask(place, lengths_ref):
    lane = lax.broadcasted_iota(jnp.int32, (1, CELLS), 1)
    a, b = lane >> 5, lane & 31
    row = valid_token(place[0:1, 0:1] * ROWS + a, lengths_ref)
    col = valid_token(place[8:9, 0:1] * COLS + b, lengths_ref)
    inside = (a < ROWS) & (b < COLS)
    return jnp.where(row & col & inside, 1.0, 0.0).astype(F32)


def project(columns, mask, gain, bias, weight, send, send_ref, gate_ref):
    for m in range(GROUPS):
        lanes = slice(m * LANES, (m + 1) * LANES)
        normed = norm_rows(columns[:, lanes], gain, bias)
        projected = tn_dot(weight, normed)
        weighting = mask[:, lanes]
        left = weighting * jax.nn.sigmoid(projected[128:256]) * projected[0:128]
        right = weighting * jax.nn.sigmoid(projected[384:512]) * projected[256:384]
        send[pl.ds(m, 128, stride=8), :] = left
        send[pl.ds(4 + m, 128, stride=8), :] = right
        gate_ref[:, lanes] = jax.nn.sigmoid(projected[512:640])
    send_ref[...] = send[pl.ds(0, 1024), :].astype(BF16)


def first_kernel(
    place, lengths_hbm, pair_hbm, in_gain_hbm, in_bias_hbm, weight_hbm, out_gain_hbm, out_bias_hbm,
    send_ref, gate_ref, columns_ref, vectors_ref, mask_ref, cells, send, norms, lengths, pair, in_gain, in_bias, out_gain, out_bias, weight, sems,
):
    copies = [
        pltpu.make_async_copy(source, target, sems.at[at])
        for at, (source, target) in enumerate((
            (pair_hbm, pair), (weight_hbm.at[0], weight), (in_gain_hbm, in_gain), (in_bias_hbm, in_bias),
            (out_gain_hbm, out_gain), (out_bias_hbm, out_bias), (lengths_hbm, lengths),
        ))
    ]
    for copy in copies:
        copy.start()
    cells[...] = jnp.zeros_like(cells)
    norms[...] = jnp.zeros_like(norms)
    for copy in copies:
        copy.wait()
    mask = cell_mask(place, lengths)
    mask_ref[...] = mask
    for at, pair_of in enumerate((in_gain, in_bias, out_gain, out_bias)):
        norms[pl.ds(2 * at, 2), :] = pair_of[...]
    vectors = norms[...].T
    vectors_ref[...] = vectors
    for a in range(ROWS):
        cells[pl.ds(a * WIDE, COLS), :] = pair[a].astype(F32)
    columns = cells[...].T
    columns_ref[...] = columns
    project(columns, mask, vectors[:, 0:1], vectors[:, 2:3], weight[...], send, send_ref, gate_ref)


def finish(home, source_rows, gain, bias, gate, columns, weight_out, got):
    for at in range(16):
        got[pl.ds(at * PITCH, 64), :] = home[pl.ds(at * 64, 64), :].astype(F32)
    for m in range(GROUPS):
        lanes = slice(m * LANES, (m + 1) * LANES)
        triangle = source_rows(got, 0, m) + source_rows(got, 1, m)
        change = tn_dot(weight_out, norm_rows(triangle, gain, bias))
        yield (columns[:, lanes] + gate[:, lanes] * change).astype(BF16).astype(F32)


def rows_after_first(got, xh, m):
    return stack(
        got[pl.ds((xh * 2 + xl) * 16 + zh * 4 + m, 16, stride=PITCH), :] for zh in range(4) for xl in range(2)
    )


def rows_after_second(got, yh, m):
    return stack(
        got[pl.ds(yh * 8 * PITCH + x * 16 + zh * 4 + m, 8, stride=PITCH), :] for zh in range(4) for x in range(4)
    )


def middle_kernel(
    home, gate, columns, vectors, mask, weight, weight_out, send_ref, gate_ref, columns_ref, got, send
):
    middle = jnp.concatenate(list(finish(
        home, rows_after_first, vectors[:, 4:5], vectors[:, 6:7], gate, columns, weight_out[0], got
    )), axis=1)
    columns_ref[...] = middle
    project(middle, mask, vectors[:, 1:2], vectors[:, 3:4], weight[1], send, send_ref, gate_ref)


def last_kernel(home, gate, columns, vectors, weight_out, out_hbm, got, cells, done, sems):
    copies = [
        pltpu.make_async_copy(done.at[part], out_hbm.at[part], sems.at[at])
        for at, part in enumerate((pl.ds(0, 8), pl.ds(8, ROWS - 8)))
    ]
    updated = finish(home, rows_after_second, vectors[:, 5:6], vectors[:, 7:8], gate, columns, weight_out[1], got)
    for m, part in enumerate(updated):
        cells[pl.ds(m * LANES, LANES), :] = part.T
        for a in range(4 * m, min(4 * m + 4, ROWS)):
            done[a] = cells[pl.ds(a * WIDE, COLS), :].astype(BF16)
        if m % 2 == 1:
            copies[m // 2].start()
    for copy in copies:
        copy.wait()


def send_home(triangle, out_ref, out_f):
    tiles = swap_groups([
        stack(
            triangle[((q * 4 + m) * 2 + yh) * 8 : ((q * 4 + m) * 2 + yh) * 8 + 8, x * 128 : x * 128 + 128]
            for m in range(GROUPS) for yh in range(2) for x in range(4)
        )
        for q in range(4)
    ])
    for m in range(GROUPS):
        for yh in range(2):
            for x in range(4):
                at = ((m * 2 + yh) * 4 + x) * 8
                for zh in range(4):
                    out_f[pl.ds(yh * 8 * PITCH + x * 16 + zh * 4 + m, 8, stride=PITCH), :] = tiles[zh][at : at + 8]
    for at in range(16):
        out_ref[pl.ds(at * 64, 64), :] = out_f[pl.ds(at * PITCH, 64), :].astype(BF16)


def outgoing_kernel(mine, both, out_ref, mine_f, both_f, out_f):
    mine_f[pl.ds(0, 1024), :] = mine[...].astype(F32)
    both_f[pl.ds(0, 2048), :] = both[...].astype(F32)

    def matrix(source, base):
        tiles = swap_groups([
            stack(
                source[pl.ds(base + ((zh * 2 + xl) * 2 + yh) * 64 + m, 8, stride=8), :]
                for xl in range(2) for m in range(GROUPS) for yh in range(2)
            )
            for zh in range(4)
        ])
        half = tiles[0].shape[0] // 2
        return stack(jnp.concatenate([tile[:half], tile[half:]], axis=1) for tile in tiles).astype(BF16)

    left = matrix(mine_f, 0)
    right = stack(matrix(both_f, core * 1024 + 4) for core in range(2))
    triangle = nt_dot(left, right).astype(BF16)
    send_home(nn_dot(triangle, token_matrix()), out_ref, out_f)


def incoming_kernel(place, both, out_ref, both_f, out_f):
    both_f[pl.ds(0, 2048), :] = both[...].astype(F32)

    def matrix(base):
        tiles = swap_groups([
            stack(
                both_f[pl.ds(base + core * 1024 + (zh * 4 + x) * 64 + m, 8, stride=8), :]
                for x in range(4) for m in range(GROUPS) for core in range(2)
            )
            for zh in range(4)
        ])
        return stack(
            jnp.concatenate([tile[x * 64 : x * 64 + 64] for x in range(4)], axis=1) for tile in tiles
        ).astype(BF16)

    left = nn_dot(matrix(0), own_matrix(place[0:1, 0:1] & 1)).astype(BF16)
    send_home(tn_dot(left, matrix(4)), out_ref, out_f)


def call(kernel, outs, scratch, name, held=(), out_space=pltpu.VMEM):
    def run(*args):
        return pl.pallas_call(
            kernel,
            out_shape=outs,
            in_specs=[pl.BlockSpec(memory_space=pltpu.HBM if at in held else pltpu.VMEM) for at in range(len(args))],
            out_specs=jax.tree.map(lambda _: pl.BlockSpec(memory_space=out_space), outs),
            scratch_shapes=[pltpu.VMEM(entry, F32) if isinstance(entry, tuple) else entry for entry in scratch],
            compiler_params=pltpu.CompilerParams(vmem_limit_bytes=32 * 1024 * 1024),
            name=name,
        )(*args)

    return run


def in_hbm(array):
    return pltpu.with_memory_space_constraint(array, pltpu.HBM)


def exchange(array, axes):
    return lax.all_to_all(array, axes, 0, 0, tiled=True)


def on_device(pair_rep, chain_lengths, in_gain, in_bias, weight_in, out_gain, out_bias, weight_out):
    place = jnp.concatenate([
        jnp.full((8, LANES), lax.axis_index(axes), jnp.int32) for axes in (ROW_AXES, COL_AXES)
    ])
    tile = jax.ShapeDtypeStruct((LANES, CELLS), F32)
    sent = jax.ShapeDtypeStruct((1024, LANES), BF16)

    strided, spread = (1024 + SPARE, LANES), (17 * PITCH, LANES)
    small = (jax.ShapeDtypeStruct((LANES, 8), F32), jax.ShapeDtypeStruct((1, CELLS), F32))
    send, gate, columns, vectors, mask = call(
        first_kernel, (sent, tile, tile) + small, [
            (CELLS, LANES), strided, (8, LANES), pltpu.SMEM(chain_lengths.shape, jnp.int32),
            pltpu.VMEM(pair_rep.shape, BF16), in_gain.shape, in_bias.shape, out_gain.shape, out_bias.shape,
            pltpu.VMEM(weight_in.shape[1:], BF16), pltpu.SemaphoreType.DMA((7,)),
        ], "first", range(1, 8),
    )(place, *map(in_hbm, (chain_lengths, pair_rep, in_gain, in_bias, weight_in, out_gain, out_bias)))
    mine = exchange(send.reshape(128, 8, LANES), GROUP1).reshape(1024, LANES)
    both = lax.all_gather(mine, "core", axis=0, tiled=True)
    home = call(
        outgoing_kernel, sent, [strided, (2048 + SPARE, LANES), spread], "outgoing"
    )(mine, both)
    home = exchange(home.reshape(256, 4, LANES), BACK).reshape(1024, LANES)

    send, gate, columns = call(
        middle_kernel, (sent, tile, tile), [spread, strided], "middle"
    )(home, gate, columns, vectors, mask, weight_in, weight_out)
    mine = exchange(send.reshape(128, 8, LANES), GROUP2).reshape(1024, LANES)
    both = lax.all_gather(mine, "core", axis=0, tiled=True)
    home = call(
        incoming_kernel, sent, [(2048 + SPARE, LANES), spread], "incoming"
    )(place, both)
    home = exchange(home.reshape(256, 4, LANES), BACK).reshape(1024, LANES)

    out = jax.ShapeDtypeStruct(pair_rep.shape, BF16)
    return call(
        last_kernel, out, [spread, (CELLS, LANES), pltpu.VMEM(out.shape, BF16), pltpu.SemaphoreType.DMA((2,))], "last",
        out_space=pltpu.HBM,
    )(home, gate, columns, vectors, weight_out)


def solution(mesh):
    fine = Mesh(mesh.devices.reshape(2, 4, 2, 2, 2, 2, 4), ROW_AXES + COL_AXES)
    placed = P(ROW_AXES, COL_AXES, None)
    return jax.shard_map(
        on_device, mesh=fine, in_specs=(placed,) + (P(),) * 7, out_specs=placed, check_vma=False
    )
```

```python
import jax
import jax.numpy as jnp
from jax import lax
from jax.experimental import pallas as pl
from jax.experimental.pallas import tpu as pltpu
from jax.sharding import Mesh, PartitionSpec as P

EPSILON = 1e-05
F32 = jnp.float32
BF16 = jnp.bfloat16

SPARE = 8
PITCH = 72

ROWS = 14
COLS = 28
WIDE = 32
CELLS = 512
GROUPS = 4
LANES = 128
SLOT = 112
CHAINS = 4

ROW_AXES = ("yh", "yl", "zl", "core")
COL_AXES = ("xh", "xl", "zh")
GROUP1 = ("zh", "xl", "yh", "yl", "zl")
GROUP2 = ("zh", "xh", "xl", "yl", "zl")
BACK = ("yh", "yl", "zl", "xh", "xl", "zh")


def nt_dot(left, right):
    return lax.dot_general(left, right, (((1,), (1,)), ((), ())), preferred_element_type=F32)


def tn_dot(left, right):
    return lax.dot_general(left, right, (((0,), (0,)), ((), ())), preferred_element_type=F32)


def nn_dot(left, right):
    return jnp.dot(left, right, preferred_element_type=F32)


def stack(pieces):
    return jnp.concatenate(list(pieces), axis=0)


def norm_rows(values, gain, bias):
    average = jnp.mean(values, axis=0, keepdims=True)
    centered = values - average
    variance = jnp.mean(centered * centered, axis=0, keepdims=True)
    return (centered * lax.rsqrt(variance + EPSILON) * gain + bias).astype(BF16)


def swap_groups(tiles):
    group = lax.broadcasted_iota(jnp.int32, tiles[0].shape, 1) >> 5
    for bit in (1, 2):
        keep = (group & bit) == 0
        out = list(tiles)
        for p in range(4):
            if p & bit == 0:
                low, high = tiles[p], tiles[p + bit]
                out[p] = jnp.where(keep, low, pltpu.roll(high, 32 * bit, 1))
                out[p + bit] = jnp.where(keep, pltpu.roll(low, LANES - 32 * bit, 1), high)
        tiles = out
    return tiles


def token_matrix():
    code = lax.broadcasted_iota(jnp.int32, (8, CELLS), 1)
    token = jnp.where(code & 31 < COLS, (code >> 5) * COLS + (code & 31), -4096)
    token = token - COLS * lax.broadcasted_iota(jnp.int32, (8, CELLS), 0)
    none = jnp.zeros((8, CELLS), F32)
    rows = []
    for core in range(2):
        for q in range(4):
            for m in range(GROUPS):
                for yh in range(2):
                    a = 4 * m + q
                    first = yh * 8 * COLS + core * ROWS + a
                    rows.append(jnp.where(token == first, 1.0, 0.0).astype(F32) if a < ROWS else none)
    return jnp.concatenate(rows, axis=0).astype(BF16)


def fields(code, *widths):
    out = []
    for width in reversed(widths):
        out.append(code & (width - 1))
        code = code >> (width.bit_length() - 1)
    return out[::-1]


def own_matrix(core):
    q, m, yh, s = fields(lax.broadcasted_iota(jnp.int32, (8, CELLS // 2), 1), 4, 4, 2, 8)
    a = 4 * m + q
    sub = lax.broadcasted_iota(jnp.int32, (8, CELLS // 2), 0)
    token = jnp.where(a < ROWS, ((yh * 8 + s) * 2 + core) * ROWS + a, -4096) - sub
    last = jnp.where(sub < COLS - 24, token, -4096)
    return jnp.concatenate([
        jnp.where((last if b == 24 else token) == c * COLS + b, 1.0, 0.0).astype(F32)
        for c in range(16) for b in range(0, WIDE, 8)
    ], axis=0).astype(BF16)


def valid_token(token, lengths_ref):
    valid = jnp.zeros(token.shape, jnp.bool_)
    for chain in range(CHAINS):
        start = chain * SLOT
        valid = valid | ((token >= start) & (token < start + lengths_ref[chain]))
    return valid


def cell_mask(place, lengths_ref):
    lane = lax.broadcasted_iota(jnp.int32, (1, CELLS), 1)
    a, b = lane >> 5, lane & 31
    row = valid_token(place[0:1, 0:1] * ROWS + a, lengths_ref)
    col = valid_token(place[8:9, 0:1] * COLS + b, lengths_ref)
    inside = (a < ROWS) & (b < COLS)
    return jnp.where(row & col & inside, 1.0, 0.0).astype(F32)


def project(columns, mask, gain, bias, weight, send, send_ref, gate_ref):
    for m in range(GROUPS):
        lanes = slice(m * LANES, (m + 1) * LANES)
        normed = norm_rows(columns[:, lanes], gain, bias)
        projected = tn_dot(weight, normed)
        weighting = mask[:, lanes]
        left = weighting * jax.nn.sigmoid(projected[128:256]) * projected[0:128]
        right = weighting * jax.nn.sigmoid(projected[384:512]) * projected[256:384]
        send[pl.ds(m, 128, stride=8), :] = left
        send[pl.ds(4 + m, 128, stride=8), :] = right
        gate_ref[:, lanes] = jax.nn.sigmoid(projected[512:640])
    send_ref[...] = send[pl.ds(0, 1024), :].astype(BF16)


def first_kernel(
    place, lengths_hbm, pair_hbm, in_gain_hbm, in_bias_hbm, weight_hbm, out_gain_hbm, out_bias_hbm,
    send_ref, gate_ref, columns_ref, vectors_ref, mask_ref, cells, send, norms, lengths, pair, in_gain, in_bias, out_gain, out_bias, weight, sems,
):
    copies = [
        pltpu.make_async_copy(source, target, sems.at[at])
        for at, (source, target) in enumerate((
            (pair_hbm, pair), (weight_hbm.at[0], weight), (in_gain_hbm, in_gain), (in_bias_hbm, in_bias),
            (out_gain_hbm, out_gain), (out_bias_hbm, out_bias), (lengths_hbm, lengths),
        ))
    ]
    for copy in copies:
        copy.start()
    cells[...] = jnp.zeros_like(cells)
    norms[...] = jnp.zeros_like(norms)
    for copy in copies:
        copy.wait()
    mask = cell_mask(place, lengths)
    mask_ref[...] = mask
    for at, pair_of in enumerate((in_gain, in_bias, out_gain, out_bias)):
        norms[pl.ds(2 * at, 2), :] = pair_of[...]
    vectors = norms[...].T
    vectors_ref[...] = vectors
    for a in range(ROWS):
        cells[pl.ds(a * WIDE, COLS), :] = pair[a].astype(F32)
    columns = cells[...].T
    columns_ref[...] = columns
    project(columns, mask, vectors[:, 0:1], vectors[:, 2:3], weight[...], send, send_ref, gate_ref)


def finish(home, source_rows, gain, bias, gate, columns, weight_out, got):
    for at in range(16):
        got[pl.ds(at * PITCH, 64), :] = home[pl.ds(at * 64, 64), :].astype(F32)
    parts = []
    for m in range(GROUPS):
        lanes = slice(m * LANES, (m + 1) * LANES)
        triangle = source_rows(got, 0, m) + source_rows(got, 1, m)
        change = tn_dot(weight_out, norm_rows(triangle, gain, bias))
        parts.append(columns[:, lanes] + gate[:, lanes] * change)
    return jnp.concatenate(parts, axis=1).astype(BF16)


def rows_after_first(got, xh, m):
    return stack(
        got[pl.ds((xh * 2 + xl) * 16 + zh * 4 + m, 16, stride=PITCH), :] for zh in range(4) for xl in range(2)
    )


def rows_after_second(got, yh, m):
    return stack(
        got[pl.ds(yh * 8 * PITCH + x * 16 + zh * 4 + m, 8, stride=PITCH), :] for zh in range(4) for x in range(4)
    )


def middle_kernel(
    home, gate, columns, vectors, mask, weight, weight_out, send_ref, gate_ref, columns_ref, got, send
):
    middle = finish(
        home, rows_after_first, vectors[:, 4:5], vectors[:, 6:7], gate, columns, weight_out[0], got
    ).astype(F32)
    columns_ref[...] = middle
    project(middle, mask, vectors[:, 1:2], vectors[:, 3:4], weight[1], send, send_ref, gate_ref)


def last_kernel(home, gate, columns, vectors, weight_out, out_ref, got, cells):
    updated = finish(
        home, rows_after_second, vectors[:, 5:6], vectors[:, 7:8], gate, columns, weight_out[1], got
    ).astype(F32)
    cells[...] = updated.T
    for a in range(ROWS):
        out_ref[a] = cells[pl.ds(a * WIDE, COLS), :].astype(BF16)


def send_home(triangle, out_ref, out_f):
    tiles = swap_groups([
        stack(
            triangle[((q * 4 + m) * 2 + yh) * 8 : ((q * 4 + m) * 2 + yh) * 8 + 8, x * 128 : x * 128 + 128]
            for m in range(GROUPS) for yh in range(2) for x in range(4)
        )
        for q in range(4)
    ])
    for m in range(GROUPS):
        for yh in range(2):
            for x in range(4):
                at = ((m * 2 + yh) * 4 + x) * 8
                for zh in range(4):
                    out_f[pl.ds(yh * 8 * PITCH + x * 16 + zh * 4 + m, 8, stride=PITCH), :] = tiles[zh][at : at + 8]
    for at in range(16):
        out_ref[pl.ds(at * 64, 64), :] = out_f[pl.ds(at * PITCH, 64), :].astype(BF16)


def outgoing_kernel(mine, both, out_ref, mine_f, both_f, out_f):
    mine_f[pl.ds(0, 1024), :] = mine[...].astype(F32)
    both_f[pl.ds(0, 1024), :] = both[...].astype(F32)

    def matrix(source, base, stride):
        tiles = swap_groups([
            stack(
                source[pl.ds(base + ((zh * 2 + xl) * 2 + yh) * 8 * stride + m, 8, stride=stride), :]
                for xl in range(2) for m in range(GROUPS) for yh in range(2)
            )
            for zh in range(4)
        ])
        half = tiles[0].shape[0] // 2
        return stack(jnp.concatenate([tile[:half], tile[half:]], axis=1) for tile in tiles).astype(BF16)

    left = matrix(mine_f, 0, 8)
    right = stack(matrix(both_f, core * 512, 4) for core in range(2))
    triangle = nt_dot(left, right).astype(BF16)
    send_home(nn_dot(triangle, token_matrix()), out_ref, out_f)


def incoming_kernel(place, both, out_ref, both_f, out_f):
    both_f[pl.ds(0, 2048), :] = both[...].astype(F32)

    def matrix(base):
        tiles = swap_groups([
            stack(
                both_f[pl.ds(base + core * 1024 + (zh * 4 + x) * 64 + m, 8, stride=8), :]
                for x in range(4) for m in range(GROUPS) for core in range(2)
            )
            for zh in range(4)
        ])
        return stack(
            jnp.concatenate([tile[x * 64 : x * 64 + 64] for x in range(4)], axis=1) for tile in tiles
        ).astype(BF16)

    left = nn_dot(matrix(0), own_matrix(place[0:1, 0:1] & 1)).astype(BF16)
    send_home(tn_dot(left, matrix(4)), out_ref, out_f)


def call(kernel, outs, scratch, name, held=()):
    def run(*args):
        return pl.pallas_call(
            kernel,
            out_shape=outs,
            in_specs=[pl.BlockSpec(memory_space=pltpu.HBM if at in held else pltpu.VMEM) for at in range(len(args))],
            out_specs=jax.tree.map(lambda _: pl.BlockSpec(memory_space=pltpu.VMEM), outs),
            scratch_shapes=[pltpu.VMEM(entry, F32) if isinstance(entry, tuple) else entry for entry in scratch],
            compiler_params=pltpu.CompilerParams(vmem_limit_bytes=32 * 1024 * 1024),
            name=name,
        )(*args)

    return run


def in_hbm(array):
    return pltpu.with_memory_space_constraint(array, pltpu.HBM)


def exchange(array, axes):
    return lax.all_to_all(array, axes, 0, 0, tiled=True)


def on_device(pair_rep, chain_lengths, in_gain, in_bias, weight_in, out_gain, out_bias, weight_out):
    place = jnp.concatenate([
        jnp.full((8, LANES), lax.axis_index(axes), jnp.int32) for axes in (ROW_AXES, COL_AXES)
    ])
    tile = jax.ShapeDtypeStruct((LANES, CELLS), F32)
    sent = jax.ShapeDtypeStruct((1024, LANES), BF16)

    strided, spread = (1024 + SPARE, LANES), (17 * PITCH, LANES)
    small = (jax.ShapeDtypeStruct((LANES, 8), F32), jax.ShapeDtypeStruct((1, CELLS), F32))
    send, gate, columns, vectors, mask = call(
        first_kernel, (sent, tile, tile) + small, [
            (CELLS, LANES), strided, (8, LANES), pltpu.SMEM(chain_lengths.shape, jnp.int32),
            pltpu.VMEM(pair_rep.shape, BF16), in_gain.shape, in_bias.shape, out_gain.shape, out_bias.shape,
            pltpu.VMEM(weight_in.shape[1:], BF16), pltpu.SemaphoreType.DMA((7,)),
        ], "first", range(1, 8),
    )(place, *map(in_hbm, (chain_lengths, pair_rep, in_gain, in_bias, weight_in, out_gain, out_bias)))
    mine = exchange(send.reshape(128, 8, LANES), GROUP1)
    both = lax.all_gather(mine[:, 4:].reshape(512, LANES), "core", axis=0, tiled=True)
    home = call(
        outgoing_kernel, sent, [strided, strided, spread], "outgoing"
    )(mine.reshape(1024, LANES), both)
    home = exchange(home.reshape(256, 4, LANES), BACK).reshape(1024, LANES)

    send, gate, columns = call(
        middle_kernel, (sent, tile, tile), [spread, strided], "middle"
    )(home, gate, columns, vectors, mask, weight_in, weight_out)
    mine = exchange(send.reshape(128, 8, LANES), GROUP2).reshape(1024, LANES)
    both = lax.all_gather(mine, "core", axis=0, tiled=True)
    home = call(
        incoming_kernel, sent, [(2048 + SPARE, LANES), spread], "incoming"
    )(place, both)
    home = exchange(home.reshape(256, 4, LANES), BACK).reshape(1024, LANES)

    out = jax.ShapeDtypeStruct(pair_rep.shape, BF16)
    return call(last_kernel, out, [spread, (CELLS, LANES)], "last")(home, gate, columns, vectors, weight_out)


def solution(mesh):
    fine = Mesh(mesh.devices.reshape(2, 4, 2, 2, 2, 2, 4), ROW_AXES + COL_AXES)
    placed = P(ROW_AXES, COL_AXES, None)
    return jax.shard_map(
        on_device, mesh=fine, in_specs=(placed,) + (P(),) * 7, out_specs=placed, check_vma=False
    )
```

```python
import jax
import jax.numpy as jnp
from jax import lax
from jax.experimental import pallas as pl
from jax.experimental.pallas import tpu as pltpu
from jax.sharding import Mesh, PartitionSpec as P

EPSILON = 1e-05
F32 = jnp.float32
BF16 = jnp.bfloat16

SPARE = 8
PITCH = 72

ROWS = 14
COLS = 28
WIDE = 32
CELLS = 512
GROUPS = 4
LANES = 128
SLOT = 112
CHAINS = 4

ROW_AXES = ("yh", "yl", "zl", "core")
COL_AXES = ("xh", "xl", "zh")
GROUP1 = ("yh", "yl", "zl", "xl", "zh")
GROUP2 = ("zh", "xh", "xl", "yl", "zl")
BACK = ("yh", "yl", "zl", "xh", "xl", "zh")


def nt_dot(left, right):
    return lax.dot_general(left, right, (((1,), (1,)), ((), ())), preferred_element_type=F32)


def tn_dot(left, right):
    return lax.dot_general(left, right, (((0,), (0,)), ((), ())), preferred_element_type=F32)


def nn_dot(left, right):
    return jnp.dot(left, right, preferred_element_type=F32)


def stack(pieces):
    return jnp.concatenate(list(pieces), axis=0)


def norm_rows(values, gain, bias):
    average = jnp.mean(values, axis=0, keepdims=True)
    centered = values - average
    variance = jnp.mean(centered * centered, axis=0, keepdims=True)
    return (centered * lax.rsqrt(variance + EPSILON) * gain + bias).astype(BF16)


def swap_groups(tiles):
    group = lax.broadcasted_iota(jnp.int32, tiles[0].shape, 1) >> 5
    for bit in (1, 2):
        keep = (group & bit) == 0
        out = list(tiles)
        for p in range(4):
            if p & bit == 0:
                low, high = tiles[p], tiles[p + bit]
                out[p] = jnp.where(keep, low, pltpu.roll(high, 32 * bit, 1))
                out[p + bit] = jnp.where(keep, pltpu.roll(low, LANES - 32 * bit, 1), high)
        tiles = out
    return tiles


def token_matrix():
    code = lax.broadcasted_iota(jnp.int32, (8, CELLS), 1)
    token = jnp.where(code & 31 < COLS, (code >> 5) * COLS + (code & 31), -4096)
    token = token - COLS * lax.broadcasted_iota(jnp.int32, (8, CELLS), 0)
    none = jnp.zeros((8, CELLS), F32)
    rows = []
    for core in range(2):
        for q in range(4):
            for m in range(GROUPS):
                for yh in range(2):
                    a = 4 * m + q
                    first = yh * 8 * COLS + core * ROWS + a
                    rows.append(jnp.where(token == first, 1.0, 0.0).astype(F32) if a < ROWS else none)
    return jnp.concatenate(rows, axis=0).astype(BF16)


def fields(code, *widths):
    out = []
    for width in reversed(widths):
        out.append(code & (width - 1))
        code = code >> (width.bit_length() - 1)
    return out[::-1]


def own_matrix(core):
    q, m, yh, s = fields(lax.broadcasted_iota(jnp.int32, (8, CELLS // 2), 1), 4, 4, 2, 8)
    a = 4 * m + q
    sub = lax.broadcasted_iota(jnp.int32, (8, CELLS // 2), 0)
    token = jnp.where(a < ROWS, ((yh * 8 + s) * 2 + core) * ROWS + a, -4096) - sub
    last = jnp.where(sub < COLS - 24, token, -4096)
    return jnp.concatenate([
        jnp.where((last if b == 24 else token) == c * COLS + b, 1.0, 0.0).astype(F32)
        for c in range(16) for b in range(0, WIDE, 8)
    ], axis=0).astype(BF16)


def valid_token(token, lengths_ref):
    valid = jnp.zeros(token.shape, jnp.bool_)
    for chain in range(CHAINS):
        start = chain * SLOT
        valid = valid | ((token >= start) & (token < start + lengths_ref[chain]))
    return valid


def cell_mask(place, lengths_ref):
    lane = lax.broadcasted_iota(jnp.int32, (1, CELLS), 1)
    a, b = lane >> 5, lane & 31
    row = valid_token(place[0:1, 0:1] * ROWS + a, lengths_ref)
    col = valid_token(place[8:9, 0:1] * COLS + b, lengths_ref)
    inside = (a < ROWS) & (b < COLS)
    return jnp.where(row & col & inside, 1.0, 0.0).astype(F32)


def store_across(send, values, row):
    for zh in range(4):
        for xl in range(2):
            start, at = (xl * 4 + zh) * 8 + row, (zh * 2 + xl) * 16
            send[pl.ds(start, 16, stride=PITCH), :] = values[at : at + 16]


def store_in_order(send, values, row):
    send[pl.ds(row, 128, stride=8), :] = values


def project(columns, mask, gain, bias, weight, store, send, gate_ref):
    for m in range(GROUPS):
        lanes = slice(m * LANES, (m + 1) * LANES)
        normed = norm_rows(columns[:, lanes], gain, bias)
        projected = tn_dot(weight, normed)
        weighting = mask[:, lanes]
        left = weighting * jax.nn.sigmoid(projected[128:256]) * projected[0:128]
        right = weighting * jax.nn.sigmoid(projected[384:512]) * projected[256:384]
        store(send, left, m)
        store(send, right, 4 + m)
        gate_ref[:, lanes] = jax.nn.sigmoid(projected[512:640])


def first_kernel(
    place, lengths_hbm, pair_hbm, in_gain_hbm, in_bias_hbm, weight_hbm, out_gain_hbm, out_bias_hbm,
    send_ref, gate_ref, columns_ref, vectors_ref, mask_ref, cells, send, norms, lengths, pair, in_gain, in_bias, out_gain, out_bias, weight, sems,
):
    copies = [
        pltpu.make_async_copy(source, target, sems.at[at])
        for at, (source, target) in enumerate((
            (pair_hbm, pair), (weight_hbm.at[0], weight), (in_gain_hbm, in_gain), (in_bias_hbm, in_bias),
            (out_gain_hbm, out_gain), (out_bias_hbm, out_bias), (lengths_hbm, lengths),
        ))
    ]
    for copy in copies:
        copy.start()
    cells[...] = jnp.zeros_like(cells)
    norms[...] = jnp.zeros_like(norms)
    for copy in copies:
        copy.wait()
    mask = cell_mask(place, lengths)
    mask_ref[...] = mask
    for at, pair_of in enumerate((in_gain, in_bias, out_gain, out_bias)):
        norms[pl.ds(2 * at, 2), :] = pair_of[...]
    vectors = norms[...].T
    vectors_ref[...] = vectors
    for a in range(ROWS):
        cells[pl.ds(a * WIDE, COLS), :] = pair[a].astype(F32)
    columns = cells[...].T
    columns_ref[...] = columns
    project(columns, mask, vectors[:, 0:1], vectors[:, 2:3], weight[...], store_across, send, gate_ref)
    for at in range(16):
        send_ref[pl.ds(at * 64, 64), :] = send[pl.ds(at * PITCH, 64), :].astype(BF16)


def finish(home, source_rows, gain, bias, gate, columns, weight_out, got):
    for at in range(16):
        got[pl.ds(at * PITCH, 64), :] = home[pl.ds(at * 64, 64), :].astype(F32)
    for m in range(GROUPS):
        lanes = slice(m * LANES, (m + 1) * LANES)
        triangle = source_rows(got, 0, m) + source_rows(got, 1, m)
        change = tn_dot(weight_out, norm_rows(triangle, gain, bias))
        yield (columns[:, lanes] + gate[:, lanes] * change).astype(BF16).astype(F32)


def rows_after_first(got, xh, m):
    return stack(
        got[pl.ds((xh * 2 + xl) * 16 + zh * 4 + m, 16, stride=PITCH), :] for zh in range(4) for xl in range(2)
    )


def rows_after_second(got, yh, m):
    return stack(
        got[pl.ds(yh * 8 * PITCH + x * 16 + zh * 4 + m, 8, stride=PITCH), :] for zh in range(4) for x in range(4)
    )


def middle_kernel(
    home, gate, columns, vectors, mask, weight, weight_out, send_ref, gate_ref, columns_ref, got, send
):
    middle = jnp.concatenate(list(finish(
        home, rows_after_first, vectors[:, 4:5], vectors[:, 6:7], gate, columns, weight_out[0], got
    )), axis=1)
    columns_ref[...] = middle
    project(middle, mask, vectors[:, 1:2], vectors[:, 3:4], weight[1], store_in_order, send, gate_ref)
    send_ref[...] = send[pl.ds(0, 1024), :].astype(BF16)


def last_kernel(home, gate, columns, vectors, weight_out, out_hbm, got, cells, done, sems):
    copies = [
        pltpu.make_async_copy(done.at[part], out_hbm.at[part], sems.at[at])
        for at, part in enumerate((pl.ds(0, 8), pl.ds(8, ROWS - 8)))
    ]
    updated = finish(home, rows_after_second, vectors[:, 5:6], vectors[:, 7:8], gate, columns, weight_out[1], got)
    for m, part in enumerate(updated):
        cells[pl.ds(m * LANES, LANES), :] = part.T
        for a in range(4 * m, min(4 * m + 4, ROWS)):
            done[a] = cells[pl.ds(a * WIDE, COLS), :].astype(BF16)
        if m % 2 == 1:
            copies[m // 2].start()
    for copy in copies:
        copy.wait()


def send_home(triangle, out_ref, out_f):
    tiles = swap_groups([
        stack(
            triangle[((q * 4 + m) * 2 + yh) * 8 : ((q * 4 + m) * 2 + yh) * 8 + 8, x * 128 : x * 128 + 128]
            for m in range(GROUPS) for yh in range(2) for x in range(4)
        )
        for q in range(4)
    ])
    for m in range(GROUPS):
        for yh in range(2):
            for x in range(4):
                at = ((m * 2 + yh) * 4 + x) * 8
                for zh in range(4):
                    out_f[pl.ds(yh * 8 * PITCH + x * 16 + zh * 4 + m, 8, stride=PITCH), :] = tiles[zh][at : at + 8]
    for at in range(16):
        out_ref[pl.ds(at * 64, 64), :] = out_f[pl.ds(at * PITCH, 64), :].astype(BF16)


def outgoing_kernel(mine, both, out_ref, mine_f, both_f, out_f):
    for at in range(16):
        mine_f[pl.ds(at * PITCH, 64), :] = mine[pl.ds(at * 64, 64), :].astype(F32)
    for at in range(32):
        both_f[pl.ds(at * PITCH, 64), :] = both[pl.ds(at * 64, 64), :].astype(F32)

    def matrix(source, base):
        tiles = swap_groups([
            stack(
                source[pl.ds(base + yh * 8 * PITCH + (xl * 4 + zh) * 8 + m, 8, stride=PITCH), :]
                for xl in range(2) for m in range(GROUPS) for yh in range(2)
            )
            for zh in range(4)
        ])
        half = tiles[0].shape[0] // 2
        return stack(jnp.concatenate([tile[:half], tile[half:]], axis=1) for tile in tiles).astype(BF16)

    left = matrix(mine_f, 0)
    right = stack(matrix(both_f, core * 16 * PITCH + 4) for core in range(2))
    triangle = nt_dot(left, right).astype(BF16)
    send_home(nn_dot(triangle, token_matrix()), out_ref, out_f)


def incoming_kernel(place, both, out_ref, both_f, out_f):
    both_f[pl.ds(0, 2048), :] = both[...].astype(F32)

    def matrix(base):
        tiles = swap_groups([
            stack(
                both_f[pl.ds(base + core * 1024 + (zh * 4 + x) * 64 + m, 8, stride=8), :]
                for x in range(4) for m in range(GROUPS) for core in range(2)
            )
            for zh in range(4)
        ])
        return stack(
            jnp.concatenate([tile[x * 64 : x * 64 + 64] for x in range(4)], axis=1) for tile in tiles
        ).astype(BF16)

    left = nn_dot(matrix(0), own_matrix(place[0:1, 0:1] & 1)).astype(BF16)
    send_home(tn_dot(left, matrix(4)), out_ref, out_f)


def call(kernel, outs, scratch, name, held=(), out_space=pltpu.VMEM):
    def run(*args):
        return pl.pallas_call(
            kernel,
            out_shape=outs,
            in_specs=[pl.BlockSpec(memory_space=pltpu.HBM if at in held else pltpu.VMEM) for at in range(len(args))],
            out_specs=jax.tree.map(lambda _: pl.BlockSpec(memory_space=out_space), outs),
            scratch_shapes=[pltpu.VMEM(entry, F32) if isinstance(entry, tuple) else entry for entry in scratch],
            compiler_params=pltpu.CompilerParams(vmem_limit_bytes=32 * 1024 * 1024),
            name=name,
        )(*args)

    return run


def in_hbm(array):
    return pltpu.with_memory_space_constraint(array, pltpu.HBM)


def exchange(array, axes):
    return lax.all_to_all(array, axes, 0, 0, tiled=True)


def on_device(pair_rep, chain_lengths, in_gain, in_bias, weight_in, out_gain, out_bias, weight_out):
    place = jnp.concatenate([
        jnp.full((8, LANES), lax.axis_index(axes), jnp.int32) for axes in (ROW_AXES, COL_AXES)
    ])
    tile = jax.ShapeDtypeStruct((LANES, CELLS), F32)
    sent = jax.ShapeDtypeStruct((1024, LANES), BF16)

    strided, spread = (1024 + SPARE, LANES), (17 * PITCH, LANES)
    small = (jax.ShapeDtypeStruct((LANES, 8), F32), jax.ShapeDtypeStruct((1, CELLS), F32))
    send, gate, columns, vectors, mask = call(
        first_kernel, (sent, tile, tile) + small, [
            (CELLS, LANES), spread, (8, LANES), pltpu.SMEM(chain_lengths.shape, jnp.int32),
            pltpu.VMEM(pair_rep.shape, BF16), in_gain.shape, in_bias.shape, out_gain.shape, out_bias.shape,
            pltpu.VMEM(weight_in.shape[1:], BF16), pltpu.SemaphoreType.DMA((7,)),
        ], "first", range(1, 8),
    )(place, *map(in_hbm, (chain_lengths, pair_rep, in_gain, in_bias, weight_in, out_gain, out_bias)))
    mine = exchange(send.reshape(128, 8, LANES), GROUP1).reshape(1024, LANES)
    both = lax.all_gather(mine, "core", axis=0, tiled=True)
    home = call(
        outgoing_kernel, sent, [spread, (33 * PITCH, LANES), spread], "outgoing"
    )(mine, both)
    home = exchange(home.reshape(256, 4, LANES), BACK).reshape(1024, LANES)

    send, gate, columns = call(
        middle_kernel, (sent, tile, tile), [spread, strided], "middle"
    )(home, gate, columns, vectors, mask, weight_in, weight_out)
    mine = exchange(send.reshape(128, 8, LANES), GROUP2).reshape(1024, LANES)
    both = lax.all_gather(mine, "core", axis=0, tiled=True)
    home = call(
        incoming_kernel, sent, [(2048 + SPARE, LANES), spread], "incoming"
    )(place, both)
    home = exchange(home.reshape(256, 4, LANES), BACK).reshape(1024, LANES)

    out = jax.ShapeDtypeStruct(pair_rep.shape, BF16)
    return call(
        last_kernel, out, [spread, (CELLS, LANES), pltpu.VMEM(out.shape, BF16), pltpu.SemaphoreType.DMA((2,))], "last",
        out_space=pltpu.HBM,
    )(home, gate, columns, vectors, weight_out)


def solution(mesh):
    fine = Mesh(mesh.devices.reshape(2, 4, 2, 2, 2, 2, 4), ROW_AXES + COL_AXES)
    placed = P(ROW_AXES, COL_AXES, None)
    return jax.shard_map(
        on_device, mesh=fine, in_specs=(placed,) + (P(),) * 7, out_specs=placed, check_vma=False
    )
```
